256 devices in a mesh: gz: 32 (over y, z), gy: 8 (over x, core).
Axes of the slice: x: 4, y: 4, z: 8, core: 2. Of those that a mesh axis runs over, the one named last changes fastest.
Arguments:
- volume: bfloat16 [32, 64, 128, 128], P('gz', 'gy'), may hold values from -1300 to 1300
- conv_weight: bfloat16 [3, 3, 3, 128, 128], replicated, may hold values from -2 to 2
- target: bfloat16 [32, 64, 128, 128], P('gz', 'gy'), may hold values from -4 to 4
Outputs:
- whitened: bfloat16 [32, 64, 128, 128], P('gz', 'gy')
- input_grad: bfloat16 [32, 64, 128, 128], P('gz', 'gy')
- weight_grad: float32 [3, 3, 3, 128, 128], P(None, None, None, 'gy')
The draws below stay inside these ranges and needn't reach their ends.
All inputs are finite; a program needn't handle non-finite values.
Results may differ from the reference program's by a relative error of at most 0.0095.
Values may be sent and summed in bfloat16 or wider, within the bound.
No kernel may reach another device: no remote copies, remote signals or barrier semaphores. Data moves between devices by JAX's collectives and lax.ppermute only.
A program may use at most 64 MiB of HBM per device.

```python
import math
import jax
import jax.numpy as jnp
from jax import lax

C = 128
G = 64
NEWTON = 5
NX = 128
CZ = 1
CY = 8
NZ = 32
NY = 64
VOXELS = 262144
GROUPS = 2
N_GZ = 32
N_GY = 8


def draw_volume(key, part):
    key = jax.random.fold_in(key, 5)
    noise_key, offset_key, scale_key, owner_key = jax.random.split(key, 4)
    depth_pos = jnp.arange(NZ, dtype=jnp.float32) / max(NZ - 1, 1)
    row_pos = jnp.arange(NY, dtype=jnp.float32) / max(NY - 1, 1)
    rise_factor = jnp.sqrt((1.0 + 2.0 * depth_pos)[:, None] * (1.0 + 2.0 * row_pos)[None, :])[:, :, None, None]
    base_noise = jnp.clip(jax.random.normal(noise_key, (NZ, NY, NX, C), jnp.float32), -4.0, 4.0)
    offset = jnp.clip(jax.random.normal(offset_key, (C,), jnp.float32), -2.0, 2.0)
    spread = math.log(10.0)
    voxel_scale = jnp.exp(jax.random.uniform(scale_key, (NZ, NY, NX, 1), jnp.float32, 0.0, spread))
    owner_block = jax.random.randint(owner_key, (C,), 0, N_GZ * N_GY)
    depth_block = jnp.arange(NZ, dtype=jnp.int32) // CZ
    row_block = jnp.arange(NY, dtype=jnp.int32) // CY
    block_id = depth_block[:, None] * N_GY + row_block[None, :]
    boost = jnp.where(block_id[:, :, None] == owner_block[None, None, :], 6.0, 1.0).astype(jnp.float32)
    return ((base_noise + offset) * rise_factor * voxel_scale * boost[:, :, None, :]).astype(jnp.bfloat16)


def draw_conv_weight(key, part):
    key = jax.random.fold_in(key, 9)
    noise_key, scale_key = jax.random.split(key, 2)
    base_noise = jnp.clip(jax.random.normal(noise_key, (3, 3, 3, C, C), jnp.float32), -4.0, 4.0)
    spread = math.log(10.0)
    column_scale = jnp.exp(jax.random.uniform(scale_key, (C,), jnp.float32, 0.0, spread))
    return (base_noise * column_scale / math.sqrt(27.0 * C)).astype(jnp.bfloat16)


def levels(key, extent, cuts, least, high):
    level = 1.0
    for position, blocks in cuts:
        steps = jax.random.uniform(jax.random.fold_in(jax.random.fold_in(key, 6), position), (blocks,), jnp.float32, least / len(cuts), high / len(cuts))
        level = level * jnp.repeat(jnp.exp(steps), extent[position] // blocks).reshape((-1,) + (1,) * (len(extent) - 1 - position))
    return level


def bell_draw(key, dims, scale, bound, shards=(), kind=jnp.bfloat16):
    gain = levels(key, dims, shards, -0.22, 0.18) if shards else 1.0
    entries = jax.random.normal(key, dims, jnp.float32) * scale * gain
    return jnp.minimum(jnp.maximum(entries, -bound), bound).astype(kind)


def setup_inputs(seed: int = 0) -> dict:
    splits = jax.random.split(jax.random.key(seed), 4)
    return {
        "volume": draw_volume(jax.random.fold_in(splits[3], 71), 0),
        "conv_weight": draw_conv_weight(jax.random.fold_in(splits[3], 71), 0),
        "target": bell_draw(splits[2], (NZ, NY, NX, C), 1.0, 4.0, ((0, 32), (1, 8))),
    }


EPSILON = 1e-05
HIGHEST = lax.Precision.HIGHEST

def newton_whitener(covariance):
    group_width = covariance.shape[1]
    trace_value = jnp.trace(covariance, axis1=1, axis2=2)
    scaled = covariance / trace_value[:, None, None]
    iterate = jnp.broadcast_to(jnp.eye(group_width, dtype=jnp.float32), covariance.shape)
    for sweep in range(NEWTON):
        squared = jnp.matmul(iterate, iterate, precision=HIGHEST)
        cubic_term = jnp.matmul(jnp.matmul(squared, iterate, precision=HIGHEST), scaled, precision=HIGHEST)
        iterate = 0.5 * (3.0 * iterate - cubic_term)
    return iterate / jnp.sqrt(trace_value)[:, None, None]

def convolve(field, kernel):
    return lax.conv_general_dilated(field, kernel, (1, 1, 1), ((1, 1), (1, 1), (1, 1)), dimension_numbers=('NDHWC', 'DHWIO', 'NDHWC'), precision=HIGHEST)

def reference(volume, conv_weight, target):
    volume_wide = volume.astype(jnp.float32)[None]
    kernel_wide = conv_weight.astype(jnp.float32)
    conv_out, pullback = jax.vjp(convolve, volume_wide, kernel_wide)
    hidden = conv_out.astype(jnp.bfloat16)
    grouped = hidden.reshape(-1, GROUPS, G).astype(jnp.float32)
    channel_mean = lax.optimization_barrier(jnp.sum(grouped, axis=0)) / VOXELS
    centered = grouped - channel_mean
    eye_block = jnp.eye(G, dtype=jnp.float32)
    covariance = jnp.einsum('vga,vgb->gab', centered, centered, precision=HIGHEST) / VOXELS + EPSILON * eye_block
    whitener, whiten_pull = jax.vjp(newton_whitener, covariance)
    white = jnp.einsum('gab,vgb->vga', whitener, centered, precision=HIGHEST)
    whitened = white.reshape(volume.shape).astype(jnp.bfloat16)
    residue = white - target.reshape(-1, GROUPS, G).astype(jnp.float32)
    residue_sum = lax.optimization_barrier(jnp.sum(residue, axis=0))
    white_grad = jnp.einsum('vga,vgb->gab', residue, centered, precision=HIGHEST)
    sigma_grad = whiten_pull(white_grad)[0]
    symmetric = (sigma_grad + jnp.swapaxes(sigma_grad, 1, 2)) / VOXELS
    grad_hidden = jnp.einsum('gba,vgb->vga', whitener, residue - residue_sum / VOXELS, precision=HIGHEST)
    grad_hidden = grad_hidden + jnp.einsum('gab,vgb->vga', symmetric, centered, precision=HIGHEST)
    grad_hidden = grad_hidden.reshape(conv_out.shape).astype(jnp.bfloat16)
    input_wide, kernel_grad = pullback(grad_hidden.astype(jnp.float32))
    input_grad = input_wide[0].astype(jnp.bfloat16)
    weight_grad = kernel_grad * (1.0 / math.sqrt(VOXELS))
    return (whitened, input_grad, weight_grad)
```

```python
import math

import jax
import jax.numpy as jnp
from jax import lax
from jax.sharding import Mesh, PartitionSpec as P

G = 64
NEWTON = 5
EPSILON = 1e-05
HIGHEST = lax.Precision.HIGHEST
GZ = ("y", "z")
GY = ("x", "c")
SPREAD = ("y", "x", "c")


def shifted_from(block, axes, count, step):
    pairs = [(i, i + step) for i in range(count) if 0 <= i + step < count]
    return lax.ppermute(block, axes, pairs)


def extended_fast(block):
    nz = lax.axis_size(GZ)
    ny = lax.axis_size(GY)
    below = shifted_from(block, GZ, nz, 1)
    above = shifted_from(block, GZ, nz, -1)
    low = shifted_from(block[:, -1:], GY, ny, 1)
    high = shifted_from(block[:, :1], GY, ny, -1)
    edges = jnp.concatenate([low, high], axis=1)
    edges_below = shifted_from(edges, GZ, nz, 1)
    edges_above = shifted_from(edges, GZ, nz, -1)
    planes = []
    for plane, edge in ((below, edges_below), (block, edges), (above, edges_above)):
        planes.append(jnp.concatenate([edge[:, :1], plane, edge[:, 1:]], axis=1))
    return jnp.concatenate(planes, axis=0)


def newton_whitener(covariance):
    group_width = covariance.shape[1]
    trace_value = jnp.trace(covariance, axis1=1, axis2=2)
    scaled = covariance / trace_value[:, None, None]
    iterate = jnp.broadcast_to(jnp.eye(group_width, dtype=jnp.float32), covariance.shape)
    for sweep in range(NEWTON):
        squared = jnp.matmul(iterate, iterate, precision=HIGHEST)
        cubic_term = jnp.matmul(
            jnp.matmul(squared, iterate, precision=HIGHEST), scaled, precision=HIGHEST
        )
        iterate = 0.5 * (3.0 * iterate - cubic_term)
    return iterate / jnp.sqrt(trace_value)[:, None, None]


def pad_columns(block):
    return jnp.pad(block, ((0, 0), (0, 0), (1, 1), (0, 0)))


def tap_slabs(padded, depth_cells, row_cells, column_cells):
    slab_list = []
    for tap_z in range(3):
        for tap_y in range(3):
            shifted = [
                padded[
                    tap_z : tap_z + depth_cells,
                    tap_y : tap_y + row_cells,
                    tap_x : tap_x + column_cells,
                ]
                for tap_x in range(3)
            ]
            merged = jnp.concatenate(shifted, axis=-1)
            slab_list.append(
                merged.reshape(depth_cells * row_cells * column_cells, merged.shape[-1])
            )
    return slab_list


def apply_taps(slab_list, kernel):
    channels_in = kernel.shape[3]
    channels_out = kernel.shape[4]
    total = jnp.zeros((slab_list[0].shape[0], channels_out), jnp.float32)
    for index_tap in range(9):
        kernel_rows = kernel[index_tap // 3, index_tap % 3].reshape(3 * channels_in, channels_out)
        total = total + jnp.dot(
            slab_list[index_tap], kernel_rows, preferred_element_type=jnp.float32
        )
    return total


def weight_terms(slab_list, grad_hidden):
    channels = grad_hidden.shape[1]
    pieces = [
        lax.dot_general(
            slab_cols, grad_hidden, (((0,), (0,)), ((), ())), preferred_element_type=jnp.float32
        ).reshape(3, channels, channels)
        for slab_cols in slab_list
    ]
    return jnp.concatenate(pieces, axis=0)


def exchange(parts, axes):
    return lax.all_to_all(parts, axes, 0, 0, tiled=True)


def copies(part, count):
    return jnp.broadcast_to(part[None], (count,) + part.shape)


def summed_everywhere(rows):
    spread = lax.axis_size(SPREAD)
    parts = rows.reshape(spread, rows.shape[0] // spread, rows.shape[1])
    mine = exchange(parts, SPREAD).sum(0)
    mine = exchange(copies(mine, lax.axis_size("z")), ("z",)).sum(0)
    return exchange(copies(mine, spread), SPREAD).reshape(rows.shape)


def local(volume, conv_weight, target):
    depth_cells, row_cells, column_cells, channels = volume.shape
    count_local = depth_cells * row_cells * column_cells
    voxels = count_local * lax.axis_size(GZ) * lax.axis_size(GY)
    groups = channels // G
    padded = pad_columns(extended_fast(volume))
    slab_list = tap_slabs(padded, depth_cells, row_cells, column_cells)
    hidden = apply_taps(slab_list, conv_weight).astype(jnp.bfloat16)
    hidden_wide = hidden.astype(jnp.float32)
    eye_block = jnp.eye(G, dtype=jnp.float32)

    flat_target = target.reshape(count_local, channels)
    target_wide = flat_target.astype(jnp.float32)
    pair = hidden.reshape(count_local, groups, G)
    target_pair = flat_target.reshape(count_local, groups, G)
    second_local = jnp.einsum("vga,vgb->agb", pair, pair, preferred_element_type=jnp.float32)
    cross_local = jnp.einsum("vga,vgb->agb", target_pair, pair, preferred_element_type=jnp.float32)
    sums_local = jnp.stack([jnp.sum(hidden_wide, axis=0), jnp.sum(target_wide, axis=0)])
    moments = jnp.concatenate(
        [second_local.reshape(G, channels), cross_local.reshape(G, channels)], axis=0
    )
    spread = lax.axis_size(SPREAD)
    sheet = jnp.concatenate(
        [
            moments.reshape(spread, 2 * G // spread, channels),
            jnp.pad(sums_local, ((0, spread - 2), (0, 0)))[:, None],
        ],
        axis=1,
    )
    depth = sheet.shape[1]
    sheet = summed_everywhere(sheet.reshape(spread * depth, channels)).reshape(
        spread, depth, channels
    )
    moments = sheet[:, : depth - 1].reshape(2 * G, channels)
    channel_mean = sheet[0, depth - 1] / voxels
    target_sum = sheet[1, depth - 1]
    mean_pair = channel_mean.reshape(groups, G)
    target_sum_pair = target_sum.reshape(groups, G)
    second = jnp.swapaxes(moments[:G].reshape(G, groups, G), 0, 1)
    cross = jnp.swapaxes(moments[G:].reshape(G, groups, G), 0, 1)
    centered_second = second - voxels * mean_pair[:, :, None] * mean_pair[:, None, :]
    centered_cross = cross - target_sum_pair[:, :, None] * mean_pair[:, None, :]
    covariance = centered_second / voxels + EPSILON * eye_block
    whitener, whiten_pull = jax.vjp(newton_whitener, covariance)
    white_grad = jnp.matmul(whitener, centered_second, precision=HIGHEST) - centered_cross
    residue_sum = -target_sum_pair
    sigma_grad = whiten_pull(white_grad)[0]
    symmetric = (sigma_grad + jnp.swapaxes(sigma_grad, 1, 2)) / voxels

    centered = (hidden_wide - channel_mean).reshape(count_local, groups, G)
    white = jnp.einsum("gab,vgb->vga", whitener, centered, precision=HIGHEST)
    whitened = white.reshape(volume.shape).astype(jnp.bfloat16)
    residue = white - target.reshape(count_local, groups, G).astype(jnp.float32)
    grad_wide = jnp.einsum(
        "gba,vgb->vga", whitener, residue - residue_sum / voxels, precision=HIGHEST
    )
    grad_wide = grad_wide + jnp.einsum("gab,vgb->vga", symmetric, centered, precision=HIGHEST)
    grad_hidden = grad_wide.reshape(count_local, channels).astype(jnp.bfloat16)

    terms = weight_terms(slab_list, grad_hidden).astype(jnp.bfloat16)
    rows_y = lax.axis_size("y")
    share = channels // lax.axis_size(GY)
    taps = terms.shape[0]
    taps_each = -(-taps // rows_y)
    terms = jnp.pad(terms, ((0, taps_each * rows_y - taps), (0, 0), (0, 0)))
    terms = terms.reshape(rows_y, taps_each, lax.axis_size(GY), share, channels)
    terms = jnp.swapaxes(terms, 1, 2).reshape(spread, taps_each * share, channels)
    part = exchange(terms, SPREAD).astype(jnp.float32).sum(0)
    part = exchange(copies(part.astype(jnp.bfloat16), lax.axis_size("z")), ("z",))
    part = part.astype(jnp.float32).sum(0) * (1.0 / math.sqrt(voxels))
    whole = exchange(copies(part, rows_y), ("y",))
    weight_grad = whole.reshape(rows_y * taps_each, share, channels)[:taps]
    weight_grad = weight_grad.reshape(3, 3, 3, share, channels)

    grad_padded = pad_columns(extended_fast(grad_hidden.reshape(volume.shape)))
    flipped = jnp.swapaxes(jnp.flip(conv_weight, (0, 1, 2)), 3, 4)
    input_grad = apply_taps(tap_slabs(grad_padded, depth_cells, row_cells, column_cells), flipped)
    input_grad = input_grad.astype(jnp.bfloat16).reshape(volume.shape)
    return (whitened, input_grad, weight_grad)


def solution(mesh):
    cells = mesh.devices.reshape(4, 8, 4, 2)
    split = Mesh(cells, ("y", "z", "x", "c"))
    in_specs = (P(GZ, GY, None, None), P(), P(GZ, GY, None, None))
    out_specs = (
        P(GZ, GY, None, None),
        P(GZ, GY, None, None),
        P(None, None, None, GY, None),
    )
    return jax.shard_map(local, mesh=split, in_specs=in_specs, out_specs=out_specs, check_vma=False)
```

```python
import math

import jax
import jax.numpy as jnp
from jax import lax
from jax.experimental import pallas as pl
from jax.experimental.pallas import tpu as pltpu
from jax.sharding import Mesh, PartitionSpec as P

G = 64
NEWTON = 5
EPSILON = 1e-05
HIGHEST = lax.Precision.HIGHEST
F32 = jnp.float32
BF16 = jnp.bfloat16
GZ = ("y", "z")
GY = ("x", "c")
SPREAD = ("y", "x", "c")
VMEM_BYTES = 48 * 1024 * 1024


def shifted_from(block, axes, count, step):
    pairs = [(i, i + step) for i in range(count) if 0 <= i + step < count]
    return lax.ppermute(block, axes, pairs)


def halo(block):
    nz = lax.axis_size(GZ)
    ny = lax.axis_size(GY)
    low = shifted_from(block[-1:], GY, ny, 1)
    high = shifted_from(block[:1], GY, ny, -1)
    below = shifted_from(block, GZ, nz, 1)
    above = shifted_from(block, GZ, nz, -1)
    edges = jnp.concatenate([low, high], axis=0)
    edges_below = shifted_from(edges, GZ, nz, 1)
    edges_above = shifted_from(edges, GZ, nz, -1)
    return (below, edges_below), (block, edges), (above, edges_above)


def call(kernel, out_shape, scratch, flops, moved, *operands):
    vmem = pl.BlockSpec(memory_space=pltpu.VMEM)
    many = isinstance(out_shape, (list, tuple))
    return pl.pallas_call(
        kernel,
        out_shape=out_shape,
        in_specs=[vmem] * len(operands),
        out_specs=[vmem] * len(out_shape) if many else vmem,
        scratch_shapes=scratch,
        compiler_params=pltpu.CompilerParams(vmem_limit_bytes=VMEM_BYTES),
        cost_estimate=pl.CostEstimate(flops=flops, bytes_accessed=moved, transcendentals=0),
    )(*operands)


def place_rows(wide, slot, plane, edge, tap_y):
    rows, _, channels = plane.shape
    cols = slice(slot * channels, (slot + 1) * channels)
    if tap_y == 0:
        wide[0:1, :, cols] = edge[0:1]
        wide[1:rows, :, cols] = plane[0 : rows - 1]
    elif tap_y == 1:
        wide[:, :, cols] = plane[...]
    else:
        wide[0 : rows - 1, :, cols] = plane[1:rows]
        wide[rows - 1 : rows, :, cols] = edge[1:2]


def moved_columns(flat, step, columns):
    count = flat.shape[0]
    column = lax.broadcasted_iota(jnp.int32, flat.shape, 0) % columns
    if step == 1:
        return jnp.where(column == 0, 0.0, pltpu.roll(flat, 1, 0))
    return jnp.where(column == columns - 1, 0.0, pltpu.roll(flat, count - 1, 0))


def over_rows(left, right):
    return lax.dot_general(left, right, (((0,), (0,)), ((), ())), preferred_element_type=F32)


def conv_kernel(
    below, below_edge, own, own_edge, above, above_edge, weight, target,
    hidden_out, sheet_out, wide, kernel_wide,
):
    rows, columns, channels = own.shape
    planes = ((below, below_edge), (own, own_edge), (above, above_edge))
    for tap_z in range(3):
        for tap_y in range(3):
            slot = tap_z * 3 + tap_y
            place_rows(wide, slot, planes[tap_z][0], planes[tap_z][1], tap_y)
            for tap_x in range(3):
                kernel_wide[
                    slot * channels : (slot + 1) * channels,
                    tap_x * channels : (tap_x + 1) * channels,
                ] = weight[slot * 3 + tap_x]
    flat = wide[...].reshape(rows * columns, 9 * channels)
    product = jnp.dot(flat, kernel_wide[...], preferred_element_type=F32)
    total = product[:, channels : 2 * channels]
    total = total + moved_columns(product[:, :channels], 1, columns)
    total = total + moved_columns(product[:, 2 * channels :], -1, columns)
    hidden = total.astype(BF16)
    hidden_out[...] = hidden
    features = target[...]
    second = over_rows(hidden, hidden)
    cross = over_rows(features, hidden)
    first = lax.broadcasted_iota(jnp.int32, (G, channels), 1) < G
    second = jnp.where(first, second[:G], second[G:])
    cross = jnp.where(first, cross[:G], cross[G:])
    spread, depth, _ = sheet_out.shape
    each = depth - 1
    half = spread // 2
    for j in range(half):
        sheet_out[j, 0:each, :] = second[each * j : each * (j + 1)]
        sheet_out[half + j, 0:each, :] = cross[each * j : each * (j + 1)]
    for j in range(2, spread):
        sheet_out[j, each:depth, :] = jnp.zeros((1, channels), F32)
    sheet_out[0, each:depth, :] = jnp.sum(hidden.astype(F32), axis=0, keepdims=True)
    sheet_out[1, each:depth, :] = jnp.sum(features.astype(F32), axis=0, keepdims=True)


def exact(left, right):
    return jnp.dot(left, right, precision=HIGHEST, preferred_element_type=F32)


def thirds(value):
    high = value.astype(BF16)
    rest = value - high.astype(F32)
    middle = rest.astype(BF16)
    return high, middle, (rest - middle.astype(F32)).astype(BF16)


def through(values, matrix):
    high, middle, low = thirds(matrix)
    total = jnp.dot(values, low, preferred_element_type=F32)
    total = total + jnp.dot(values, middle, preferred_element_type=F32)
    return total + jnp.dot(values, high, preferred_element_type=F32)


def whiten_kernel(voxels, sheet, hidden, target, whitened_out, grad_out, mats):
    spread, depth, channels = sheet.shape
    each = depth - 1
    for j in range(spread):
        mats[each * j : each * (j + 1), :] = sheet[j, 0:each, :]
    row = lax.broadcasted_iota(jnp.int32, (channels, channels), 0)
    col = lax.broadcasted_iota(jnp.int32, (channels, channels), 1)
    same = (row < G) == (col < G)
    diagonal = row == col
    low_lane = lax.broadcasted_iota(jnp.int32, (1, channels), 1) < G

    def group_sums(value):
        line = jnp.sum(value, axis=0, keepdims=True)
        low = jnp.sum(jnp.where(low_lane, line, 0.0), axis=1, keepdims=True)
        high = jnp.sum(jnp.where(low_lane, 0.0, line), axis=1, keepdims=True)
        return jnp.where(low_lane, low, high)

    second = jnp.concatenate([mats[:G], mats[:G]], axis=0)
    cross = jnp.concatenate([mats[G:], mats[G:]], axis=0)
    mean = sheet[0, each:depth, :] / voxels
    target_sum = sheet[1, each:depth, :]
    mean_rows = jnp.broadcast_to(mean, (channels, channels))
    mean_cols = mean_rows.T
    target_cols = jnp.broadcast_to(target_sum, (channels, channels)).T
    second = jnp.where(same, second - voxels * (mean_cols * mean_rows), 0.0)
    cross = jnp.where(same, cross - target_cols * mean_rows, 0.0)
    covariance = second / voxels + jnp.where(diagonal, EPSILON, 0.0)
    trace = group_sums(jnp.where(diagonal, covariance, 0.0))
    scaled = covariance / trace
    root = jnp.sqrt(trace)

    iterate = jnp.where(diagonal, 1.5, 0.0) - 0.5 * scaled
    saved = []
    for sweep in range(1, NEWTON):
        pair = exact(iterate, jnp.concatenate([iterate, scaled], axis=1))
        squared, once = pair[:, :channels], pair[:, channels:]
        triple = exact(squared, jnp.concatenate([once, scaled, iterate], axis=1))
        saved.append(
            (iterate, squared, once, triple[:, channels : 2 * channels], triple[:, 2 * channels :])
        )
        iterate = 1.5 * iterate - 0.5 * triple[:, :channels]
    whitener = iterate / root
    white_grad = exact(whitener, second) - cross
    direction = white_grad / root
    change = -0.5 * direction
    for iterate_k, squared, once, cubic, cube in saved:
        left = exact(jnp.concatenate([iterate_k, squared], axis=0), change)
        both = jnp.concatenate([left[:channels], left[channels:]], axis=1)
        moved = exact(both, jnp.concatenate([once, scaled], axis=0))
        moved = moved + exact(
            jnp.concatenate([change, cube], axis=1), jnp.concatenate([cubic, direction], axis=0)
        )
        change = 1.5 * change - 0.5 * moved
    trace_grad = -0.5 * group_sums(white_grad * whitener) / trace
    trace_grad = trace_grad - group_sums(change * scaled) / trace
    sigma_grad = change / trace + jnp.where(diagonal, trace_grad, 0.0)
    symmetric = (sigma_grad + sigma_grad.T) / voxels
    whitener_t = whitener.T
    backward = (exact(whitener_t, whitener) + symmetric).T

    both = jnp.concatenate([whitener_t, backward], axis=1)
    offset = exact(jnp.broadcast_to(mean, (8, channels)), both)[0:1]
    target_offset = exact(jnp.broadcast_to(target_sum / voxels, (8, channels)), whitener)[0:1]
    mixed = through(hidden[...], both) - offset
    whitened_out[...] = mixed[:, :channels].astype(BF16)
    pulled = through(target[...], whitener) - target_offset
    grad_out[...] = (mixed[:, channels:] - pulled).astype(BF16)


def turn_kernel(below, below_edge, own, own_edge, above, above_edge, turned_out):
    rows, columns, channels = own.shape
    planes = ((below, below_edge), (own, own_edge), (above, above_edge))
    for tap_z in range(3):
        plane, edge = planes[tap_z]
        for source in range(-1, rows + 1):
            if source < 0:
                tile = edge[0]
            elif source == rows:
                tile = edge[1]
            else:
                tile = plane[source]
            tile = tile.T
            for tap_y in range(3):
                here = source + 1 - tap_y
                if 0 <= here < rows:
                    slot = tap_z * 3 + tap_y
                    turned_out[
                        slot * channels : (slot + 1) * channels,
                        here * columns : (here + 1) * columns,
                    ] = tile


def weight_kernel(columns, share, turned, grad, parts_out, wide):
    count, channels = grad.shape
    value = grad[...].astype(F32)
    wide[:, :channels] = moved_columns(value, -1, columns).astype(BF16)
    wide[:, channels : 2 * channels] = grad[...]
    wide[:, 2 * channels :] = moved_columns(value, 1, columns).astype(BF16)
    blocks = channels // share
    taps_each = parts_out.shape[1] // share
    terms = jnp.dot(turned[...], wide[...], preferred_element_type=F32).astype(BF16)
    for tap in range(27):
        slot, tap_x = tap // 3, tap % 3
        group, place = tap // taps_each, tap % taps_each
        for block in range(blocks):
            first = slot * channels + block * share
            parts_out[group * blocks + block, place * share : (place + 1) * share, :] = terms[
                first : first + share, tap_x * channels : (tap_x + 1) * channels
            ]
    spare = parts_out.shape[0] // blocks * taps_each
    for tap in range(27, spare):
        group, place = tap // taps_each, tap % taps_each
        for block in range(blocks):
            parts_out[group * blocks + block, place * share : (place + 1) * share, :] = jnp.zeros(
                (share, channels), BF16
            )


def input_kernel(
    below, below_edge, own, own_edge, above, above_edge, weight, grad_out, wide, kernel_wide
):
    rows, columns, channels = own.shape
    planes = ((below, below_edge), (own, own_edge), (above, above_edge))
    for tap_z in range(3):
        for tap_y in range(3):
            slot = tap_z * 3 + tap_y
            place_rows(wide, slot, planes[2 - tap_z][0], planes[2 - tap_z][1], 2 - tap_y)
            for tap_x in range(3):
                kernel_wide[
                    tap_x * channels : (tap_x + 1) * channels,
                    slot * channels : (slot + 1) * channels,
                ] = weight[slot * 3 + tap_x]
    flat = wide[...].reshape(rows * columns, 9 * channels)
    product = lax.dot_general(
        flat, kernel_wide[...], (((1,), (1,)), ((), ())), preferred_element_type=F32
    )
    total = product[:, channels : 2 * channels]
    total = total + moved_columns(product[:, :channels], -1, columns)
    total = total + moved_columns(product[:, 2 * channels :], 1, columns)
    grad_out[...] = total.astype(BF16)


def exchange(parts, axes):
    return lax.all_to_all(parts, axes, 0, 0, tiled=True)


def copies(part, count):
    return jnp.broadcast_to(part[None], (count,) + part.shape)


def local(volume, conv_weight, target):
    _, rows, columns, channels = volume.shape
    count = rows * columns
    voxels = count * lax.axis_size(GZ) * lax.axis_size(GY)
    spread = lax.axis_size(SPREAD)
    levels = lax.axis_size("z")
    rows_y = lax.axis_size("y")
    share = channels // lax.axis_size(GY)
    taps_each = -(-27 // rows_y)
    flops = 2 * count * 27 * channels * channels
    weight = conv_weight.reshape(27, channels, channels)
    target_flat = target.reshape(count, channels)

    planes = halo(volume.reshape(rows, columns, channels))
    planes = [piece for plane in planes for piece in plane]
    wide = pltpu.VMEM((rows, columns, 9 * channels), BF16)
    hidden, sheet = call(
        conv_kernel,
        [
            jax.ShapeDtypeStruct((count, channels), BF16),
            jax.ShapeDtypeStruct((spread, 2 * G // spread + 1, channels), F32),
        ],
        [wide, pltpu.VMEM((9 * channels, 3 * channels), BF16)],
        flops, 3 * 2**20, *planes, weight, target_flat,
    )
    turned = call(
        turn_kernel,
        jax.ShapeDtypeStruct((9 * channels, count), BF16),
        [], 0, 3 * 2**20, *planes,
    )

    mine = exchange(sheet, SPREAD).sum(0)
    mine = exchange(copies(mine, levels), ("z",)).sum(0)
    sheet = exchange(copies(mine, spread), SPREAD)
    whitened, grad_hidden = call(
        lambda *refs: whiten_kernel(voxels, *refs),
        [jax.ShapeDtypeStruct((count, channels), BF16)] * 2,
        [pltpu.VMEM((2 * G, channels), F32)],
        100 * 2 * channels**3, 2**20, sheet, hidden, target_flat,
    )

    parts = call(
        lambda *refs: weight_kernel(columns, share, *refs),
        jax.ShapeDtypeStruct((spread, taps_each * share, channels), BF16),
        [pltpu.VMEM((count, 3 * channels), BF16)],
        flops, 4 * 2**20, turned, grad_hidden,
    )
    part = exchange(parts, SPREAD).astype(F32).sum(0)
    part = exchange(copies(part.astype(BF16), levels), ("z",))
    part = part.astype(F32).sum(0) * (1.0 / math.sqrt(voxels))
    whole = exchange(copies(part, rows_y), ("y",))
    weight_grad = whole.reshape(rows_y * taps_each, share, channels)[:27]
    weight_grad = weight_grad.reshape(3, 3, 3, share, channels)

    planes = halo(grad_hidden.reshape(rows, columns, channels))
    planes = [piece for plane in planes for piece in plane]
    input_grad = call(
        input_kernel,
        jax.ShapeDtypeStruct((count, channels), BF16),
        [wide, pltpu.VMEM((3 * channels, 9 * channels), BF16)],
        flops, 3 * 2**20, *planes, weight,
    )
    return (whitened.reshape(volume.shape), input_grad.reshape(volume.shape), weight_grad)


def solution(mesh):
    cells = mesh.devices.reshape(4, 8, 4, 2)
    split = Mesh(cells, ("y", "z", "x", "c"))
    in_specs = (P(GZ, GY, None, None), P(), P(GZ, GY, None, None))
    out_specs = (
        P(GZ, GY, None, None),
        P(GZ, GY, None, None),
        P(None, None, None, GY, None),
    )
    return jax.shard_map(local, mesh=split, in_specs=in_specs, out_specs=out_specs, check_vma=False)
```

```python
import math

import jax
import jax.numpy as jnp
from jax import lax
from jax.experimental import pallas as pl
from jax.experimental.pallas import tpu as pltpu
from jax.sharding import Mesh, PartitionSpec as P

G = 64
NEWTON = 5
EPSILON = 1e-05
HIGHEST = lax.Precision.HIGHEST
F32 = jnp.float32
BF16 = jnp.bfloat16
GZ = ("y", "z")
GY = ("x", "c")
SPREAD = ("y", "x", "c")
VMEM_BYTES = 20 * 1024 * 1024


def swapped(block, axes, count, first):
    pairs = []
    for i in range(first, count - 1, 2):
        pairs += [(i, i + 1), (i + 1, i)]
    return lax.ppermute(block, axes, pairs)


def row_swaps(first_send, second_send):
    ny = lax.axis_size(GY)
    return jnp.concatenate(
        [swapped(first_send, GY, ny, 0), swapped(second_send, GY, ny, 1)], axis=0
    )


def plane_swaps(block):
    nz = lax.axis_size(GZ)
    return swapped(block, GZ, nz, 0), swapped(block, GZ, nz, 1)


def call(kernel, out_shape, scratch, flops, moved, *operands):
    vmem = pl.BlockSpec(memory_space=pltpu.VMEM)
    many = isinstance(out_shape, (list, tuple))
    return pl.pallas_call(
        kernel,
        out_shape=out_shape,
        in_specs=[vmem] * len(operands),
        out_specs=[vmem] * len(out_shape) if many else vmem,
        scratch_shapes=scratch,
        compiler_params=pltpu.CompilerParams(vmem_limit_bytes=VMEM_BYTES),
        cost_estimate=pl.CostEstimate(flops=flops, bytes_accessed=moved, transcendentals=0),
    )(*operands)


def place_rows(wide, slot, plane, edge, tap_y):
    rows, _, channels = plane.shape
    cols = slice(slot * channels, (slot + 1) * channels)
    odd_row = lax.axis_index("c")
    if tap_y == 0:
        wide[0:1, :, cols] = edge[pl.ds(1 - odd_row, 1)]
        wide[1:rows, :, cols] = plane[0 : rows - 1]
    elif tap_y == 1:
        wide[:, :, cols] = plane[...]
    else:
        wide[0 : rows - 1, :, cols] = plane[1:rows]
        wide[rows - 1 : rows, :, cols] = edge[pl.ds(odd_row, 1)]


def place_all(wide, own, even, odd, flip):
    odd_plane = lax.rem(lax.axis_index("z"), 2)

    order = range(3)
    for tap_z in order:
        for tap_y in order:
            slot = tap_z * 3 + tap_y
            step_z, step_y = (2 - tap_z, 2 - tap_y) if flip else (tap_z, tap_y)
            if step_z == 1:
                place_rows(wide, slot, own[0], own[1], step_y)
    for parity in range(2):

        @pl.when(odd_plane == parity)
        def _():
            below, above = (odd, even) if parity == 0 else (even, odd)
            for tap_z in order:
                for tap_y in order:
                    slot = tap_z * 3 + tap_y
                    step_z, step_y = (2 - tap_z, 2 - tap_y) if flip else (tap_z, tap_y)
                    if step_z != 1:
                        piece = below if step_z == 0 else above
                        place_rows(wide, slot, piece[0], piece[1], step_y)


def moved_columns(flat, step, columns):
    count = flat.shape[0]
    column = lax.broadcasted_iota(jnp.int32, flat.shape, 0) % columns
    if step == 1:
        return jnp.where(column == 0, 0.0, pltpu.roll(flat, 1, 0))
    return jnp.where(column == columns - 1, 0.0, pltpu.roll(flat, count - 1, 0))


def over_rows(left, right):
    return lax.dot_general(left, right, (((0,), (0,)), ((), ())), preferred_element_type=F32)


def conv_kernel(
    own, own_edge, even, even_edge, odd, odd_edge, weight, target,
    hidden_out, sheet_out, wide, kernel_wide,
):
    rows, columns, channels = own.shape
    place_all(wide, (own, own_edge), (even, even_edge), (odd, odd_edge), False)
    for slot in range(9):
        for tap_x in range(3):
            kernel_wide[
                slot * channels : (slot + 1) * channels,
                tap_x * channels : (tap_x + 1) * channels,
            ] = weight[slot * 3 + tap_x]
    flat = wide[...].reshape(rows * columns, 9 * channels)
    product = jnp.dot(flat, kernel_wide[...], preferred_element_type=F32)
    total = product[:, channels : 2 * channels]
    total = total + moved_columns(product[:, :channels], 1, columns)
    total = total + moved_columns(product[:, 2 * channels :], -1, columns)
    hidden = total.astype(BF16)
    hidden_out[...] = hidden
    features = target[...]
    second = over_rows(hidden, hidden)
    cross = over_rows(features, hidden)
    first = lax.broadcasted_iota(jnp.int32, (G, channels), 1) < G
    second = jnp.where(first, second[:G], second[G:])
    cross = jnp.where(first, cross[:G], cross[G:])
    spread, depth, _ = sheet_out.shape
    each = depth - 1
    half = spread // 2
    for j in range(half):
        sheet_out[j, 0:each, :] = second[each * j : each * (j + 1)]
        sheet_out[half + j, 0:each, :] = cross[each * j : each * (j + 1)]
    for j in range(2, spread):
        sheet_out[j, each:depth, :] = jnp.zeros((1, channels), F32)
    sheet_out[0, each:depth, :] = jnp.sum(hidden.astype(F32), axis=0, keepdims=True)
    sheet_out[1, each:depth, :] = jnp.sum(features.astype(F32), axis=0, keepdims=True)


def exact(left, right):
    return jnp.dot(left, right, precision=HIGHEST, preferred_element_type=F32)


def thirds(value):
    high = value.astype(BF16)
    rest = value - high.astype(F32)
    middle = rest.astype(BF16)
    return high, middle, (rest - middle.astype(F32)).astype(BF16)


def through(values, matrix):
    high, middle, low = thirds(matrix)
    total = jnp.dot(values, low, preferred_element_type=F32)
    total = total + jnp.dot(values, middle, preferred_element_type=F32)
    return total + jnp.dot(values, high, preferred_element_type=F32)


def whiten_kernel(
    voxels, columns, sheet, hidden, target, whitened_out, grad_out, first_out, second_out, mats
):
    spread, depth, channels = sheet.shape
    each = depth - 1
    for j in range(spread):
        mats[each * j : each * (j + 1), :] = sheet[j, 0:each, :]
    row = lax.broadcasted_iota(jnp.int32, (channels, channels), 0)
    col = lax.broadcasted_iota(jnp.int32, (channels, channels), 1)
    same = (row < G) == (col < G)
    diagonal = row == col
    low_lane = lax.broadcasted_iota(jnp.int32, (1, channels), 1) < G

    def group_sums(value):
        line = jnp.sum(value, axis=0, keepdims=True)
        low = jnp.sum(jnp.where(low_lane, line, 0.0), axis=1, keepdims=True)
        high = jnp.sum(jnp.where(low_lane, 0.0, line), axis=1, keepdims=True)
        return jnp.where(low_lane, low, high)

    second = jnp.concatenate([mats[:G], mats[:G]], axis=0)
    cross = jnp.concatenate([mats[G:], mats[G:]], axis=0)
    mean = sheet[0, each:depth, :] / voxels
    target_sum = sheet[1, each:depth, :]
    mean_rows = jnp.broadcast_to(mean, (channels, channels))
    mean_cols = mean_rows.T
    target_cols = jnp.broadcast_to(target_sum, (channels, channels)).T
    second = jnp.where(same, second - voxels * (mean_cols * mean_rows), 0.0)
    cross = jnp.where(same, cross - target_cols * mean_rows, 0.0)
    covariance = second / voxels + jnp.where(diagonal, EPSILON, 0.0)
    trace = group_sums(jnp.where(diagonal, covariance, 0.0))
    scaled = covariance / trace
    root = jnp.sqrt(trace)

    iterate = jnp.where(diagonal, 1.5, 0.0) - 0.5 * scaled
    saved = []
    for sweep in range(1, NEWTON):
        pair = exact(iterate, jnp.concatenate([iterate, scaled], axis=1))
        squared, once = pair[:, :channels], pair[:, channels:]
        triple = exact(squared, jnp.concatenate([once, scaled, iterate], axis=1))
        saved.append(
            (iterate, squared, once, triple[:, channels : 2 * channels], triple[:, 2 * channels :])
        )
        iterate = 1.5 * iterate - 0.5 * triple[:, :channels]
    whitener = iterate / root
    white_grad = exact(whitener, second) - cross
    direction = white_grad / root
    change = -0.5 * direction
    for iterate_k, squared, once, cubic, cube in saved:
        left = exact(jnp.concatenate([iterate_k, squared], axis=0), change)
        both = jnp.concatenate([left[:channels], left[channels:]], axis=1)
        moved = exact(both, jnp.concatenate([once, scaled], axis=0))
        moved = moved + exact(
            jnp.concatenate([change, cube], axis=1), jnp.concatenate([cubic, direction], axis=0)
        )
        change = 1.5 * change - 0.5 * moved
    trace_grad = -0.5 * group_sums(white_grad * whitener) / trace
    trace_grad = trace_grad - group_sums(change * scaled) / trace
    sigma_grad = change / trace + jnp.where(diagonal, trace_grad, 0.0)
    symmetric = (sigma_grad + sigma_grad.T) / voxels
    whitener_t = whitener.T
    backward = (exact(whitener_t, whitener) + symmetric).T

    both = jnp.concatenate([whitener_t, backward], axis=1)
    offset = exact(jnp.broadcast_to(mean, (8, channels)), both)[0:1]
    target_offset = exact(jnp.broadcast_to(target_sum / voxels, (8, channels)), whitener)[0:1]
    mixed = through(hidden[...], both) - offset
    whitened_out[...] = mixed[:, :channels].astype(BF16)
    pulled = through(target[...], whitener) - target_offset
    grad = (mixed[:, channels:] - pulled).astype(BF16)
    grad_out[...] = grad
    odd_row = lax.axis_index("c")

    @pl.when(odd_row == 0)
    def _():
        first_out[0] = grad[-columns:]
        second_out[0] = grad[:columns]

    @pl.when(odd_row == 1)
    def _():
        first_out[0] = grad[:columns]
        second_out[0] = grad[-columns:]


def turn_kernel(own, own_edge, even, even_edge, odd, odd_edge, turned_out):
    rows, columns, channels = own.shape
    odd_row = lax.axis_index("c")
    odd_plane = lax.rem(lax.axis_index("z"), 2)

    def turn(tap_z, plane, edge):
        for source in range(-1, rows + 1):
            if source < 0:
                tile = edge[1 - odd_row]
            elif source == rows:
                tile = edge[odd_row]
            else:
                tile = plane[source]
            tile = tile.T
            for tap_y in range(3):
                here = source + 1 - tap_y
                if 0 <= here < rows:
                    slot = tap_z * 3 + tap_y
                    turned_out[
                        slot * channels : (slot + 1) * channels,
                        here * columns : (here + 1) * columns,
                    ] = tile

    turn(1, own, own_edge)
    for parity in range(2):

        @pl.when(odd_plane == parity)
        def _():
            below, above = ((odd, odd_edge), (even, even_edge))[:: 1 - 2 * parity]
            turn(0, *below)
            turn(2, *above)


def weight_kernel(columns, share, turned, grad, parts_out, wide):
    count, channels = grad.shape
    value = grad[...].astype(F32)
    wide[:, :channels] = moved_columns(value, -1, columns).astype(BF16)
    wide[:, channels : 2 * channels] = grad[...]
    wide[:, 2 * channels :] = moved_columns(value, 1, columns).astype(BF16)
    blocks = channels // share
    taps_each = parts_out.shape[1] // share
    terms = jnp.dot(turned[...], wide[...], preferred_element_type=F32).astype(BF16)
    for tap in range(27):
        slot, tap_x = tap // 3, tap % 3
        group, place = tap // taps_each, tap % taps_each
        for block in range(blocks):
            first = slot * channels + block * share
            parts_out[group * blocks + block, place * share : (place + 1) * share, :] = terms[
                first : first + share, tap_x * channels : (tap_x + 1) * channels
            ]
    spare = parts_out.shape[0] // blocks * taps_each
    for tap in range(27, spare):
        group, place = tap // taps_each, tap % taps_each
        for block in range(blocks):
            parts_out[group * blocks + block, place * share : (place + 1) * share, :] = jnp.zeros(
                (share, channels), BF16
            )


def input_kernel(
    own, own_edge, even, even_edge, odd, odd_edge, weight, grad_out, wide, kernel_wide
):
    rows, columns, channels = own.shape
    place_all(wide, (own, own_edge), (even, even_edge), (odd, odd_edge), True)
    for slot in range(9):
        for tap_x in range(3):
            kernel_wide[
                tap_x * channels : (tap_x + 1) * channels,
                slot * channels : (slot + 1) * channels,
            ] = weight[slot * 3 + tap_x]
    flat = wide[...].reshape(rows * columns, 9 * channels)
    product = lax.dot_general(
        flat, kernel_wide[...], (((1,), (1,)), ((), ())), preferred_element_type=F32
    )
    total = product[:, channels : 2 * channels]
    total = total + moved_columns(product[:, :channels], -1, columns)
    total = total + moved_columns(product[:, 2 * channels :], 1, columns)
    grad_out[...] = total.astype(BF16)


def total_kernel(scale, parts, copies_out):
    total = parts[0].astype(F32)
    for i in range(1, parts.shape[0]):
        total = total + parts[i].astype(F32)
    total = (total * scale if scale != 1.0 else total).astype(copies_out.dtype)
    for i in range(copies_out.shape[0]):
        copies_out[i] = total


def exchange(parts, axes):
    return lax.all_to_all(parts, axes, 0, 0, tiled=True)


def total_copies(parts, count, dtype, scale=1.0):
    shape = jax.ShapeDtypeStruct((count,) + parts.shape[1:], dtype)
    return call(
        lambda *refs: total_kernel(scale, *refs), shape, [], parts.size, 2 * parts.size, parts
    )


def local(volume, conv_weight, target):
    _, rows, columns, channels = volume.shape
    count = rows * columns
    voxels = count * lax.axis_size(GZ) * lax.axis_size(GY)
    spread = lax.axis_size(SPREAD)
    levels = lax.axis_size("z")
    rows_y = lax.axis_size("y")
    share = channels // lax.axis_size(GY)
    taps_each = -(-27 // rows_y)
    flops = 2 * count * 27 * channels * channels
    weight = conv_weight.reshape(27, channels, channels)
    target_flat = target.reshape(count, channels)

    block = volume.reshape(rows, columns, channels)
    odd_row = lax.axis_index("c")
    first_send = lax.dynamic_slice_in_dim(block, (1 - odd_row) * (rows - 1), 1, 0)
    second_send = lax.dynamic_slice_in_dim(block, odd_row * (rows - 1), 1, 0)
    edges = row_swaps(first_send, second_send)
    even, odd = plane_swaps(block)
    even_edges, odd_edges = plane_swaps(edges)
    planes = [block, edges, even, even_edges, odd, odd_edges]
    wide = pltpu.VMEM((rows, columns, 9 * channels), BF16)
    hidden, sheet = call(
        conv_kernel,
        [
            jax.ShapeDtypeStruct((count, channels), BF16),
            jax.ShapeDtypeStruct((spread, 2 * G // spread + 1, channels), F32),
        ],
        [wide, pltpu.VMEM((9 * channels, 3 * channels), BF16)],
        flops, 3 * 2**20, *planes, weight, target_flat,
    )
    turned = call(
        turn_kernel,
        jax.ShapeDtypeStruct((9 * channels, count), BF16),
        [], 0, 3 * 2**20, *planes,
    )

    mine = total_copies(exchange(sheet, SPREAD), levels, F32)
    mine = total_copies(exchange(mine, ("z",)), spread, F32)
    sheet = exchange(mine, SPREAD)
    line = jax.ShapeDtypeStruct((1, columns, channels), BF16)
    whitened, grad_hidden, first_send, second_send = call(
        lambda *refs: whiten_kernel(voxels, columns, *refs),
        [jax.ShapeDtypeStruct((count, channels), BF16)] * 2 + [line] * 2,
        [pltpu.VMEM((2 * G, channels), F32)],
        100 * 2 * channels**3, 2**20, sheet, hidden, target_flat,
    )

    parts = call(
        lambda *refs: weight_kernel(columns, share, *refs),
        jax.ShapeDtypeStruct((spread, taps_each * share, channels), BF16),
        [pltpu.VMEM((count, 3 * channels), BF16)],
        flops, 4 * 2**20, turned, grad_hidden,
    )
    block, first_send, second_send, parts = lax.optimization_barrier(
        (grad_hidden.reshape(rows, columns, channels), first_send, second_send, parts)
    )
    edges = row_swaps(first_send, second_send)
    even, odd = plane_swaps(block)
    part = total_copies(exchange(parts, SPREAD), levels, BF16)
    part, edges, even, odd = lax.optimization_barrier((part, edges, even, odd))
    even_edges, odd_edges = plane_swaps(edges)
    part = total_copies(exchange(part, ("z",)), rows_y, F32, 1.0 / math.sqrt(voxels))
    part, even_edges, odd_edges = lax.optimization_barrier((part, even_edges, odd_edges))
    whole = exchange(part, ("y",))
    weight_grad = whole.reshape(rows_y * taps_each, share, channels)[:27]
    weight_grad = weight_grad.reshape(3, 3, 3, share, channels)

    planes = [block, edges, even, even_edges, odd, odd_edges]
    input_grad = call(
        input_kernel,
        jax.ShapeDtypeStruct((count, channels), BF16),
        [wide, pltpu.VMEM((3 * channels, 9 * channels), BF16)],
        flops, 3 * 2**20, *planes, weight,
    )
    return (whitened.reshape(volume.shape), input_grad.reshape(volume.shape), weight_grad)


def solution(mesh):
    cells = mesh.devices.reshape(4, 8, 4, 2)
    split = Mesh(cells, ("y", "z", "x", "c"))
    in_specs = (P(GZ, GY, None, None), P(), P(GZ, GY, None, None))
    out_specs = (
        P(GZ, GY, None, None),
        P(GZ, GY, None, None),
        P(None, None, None, GY, None),
    )
    return jax.shard_map(local, mesh=split, in_specs=in_specs, out_specs=out_specs, check_vma=False)
```

```python
import math

import jax
import jax.numpy as jnp
from jax import lax
from jax.experimental import pallas as pl
from jax.experimental.pallas import tpu as pltpu
from jax.sharding import Mesh, PartitionSpec as P

G = 64
NEWTON = 5
EPSILON = 1e-05
HIGHEST = lax.Precision.HIGHEST
F32 = jnp.float32
BF16 = jnp.bfloat16
GZ = ("y", "z")
GY = ("x", "c")
SPREAD = ("y", "x", "c")
VMEM_BYTES = 20 * 1024 * 1024


def swapped(block, axes, count, first):
    pairs = []
    for i in range(first, count - 1, 2):
        pairs += [(i, i + 1), (i + 1, i)]
    return lax.ppermute(block, axes, pairs)


def row_swaps(first_send, second_send):
    ny = lax.axis_size(GY)
    return jnp.concatenate(
        [swapped(first_send, GY, ny, 0), swapped(second_send, GY, ny, 1)], axis=0
    )


def plane_swaps(block):
    nz = lax.axis_size(GZ)
    return swapped(block, GZ, nz, 0), swapped(block, GZ, nz, 1)


def call(kernel, out_shape, scratch, flops, moved, *operands, far=()):
    vmem = pl.BlockSpec(memory_space=pltpu.VMEM)
    hbm = pl.BlockSpec(memory_space=pltpu.HBM)
    many = isinstance(out_shape, (list, tuple))
    return pl.pallas_call(
        kernel,
        out_shape=out_shape,
        in_specs=[hbm if i in far else vmem for i in range(len(operands))],
        out_specs=[vmem] * len(out_shape) if many else vmem,
        scratch_shapes=scratch,
        compiler_params=pltpu.CompilerParams(vmem_limit_bytes=VMEM_BYTES),
        cost_estimate=pl.CostEstimate(flops=flops, bytes_accessed=moved, transcendentals=0),
    )(*operands)


def place_rows(wide, slot, plane, edge, tap_y):
    rows, _, channels = plane.shape
    cols = slice(slot * channels, (slot + 1) * channels)
    odd_row = lax.axis_index("c")
    if tap_y == 0:
        wide[0:1, :, cols] = edge[pl.ds(1 - odd_row, 1)]
        wide[1:rows, :, cols] = plane[0 : rows - 1]
    elif tap_y == 1:
        wide[:, :, cols] = plane[...]
    else:
        wide[0 : rows - 1, :, cols] = plane[1:rows]
        wide[rows - 1 : rows, :, cols] = edge[pl.ds(odd_row, 1)]


def place_all(wide, own, even, odd, flip):
    odd_plane = lax.rem(lax.axis_index("z"), 2)

    order = range(3)
    for tap_z in order:
        for tap_y in order:
            slot = tap_z * 3 + tap_y
            step_z, step_y = (2 - tap_z, 2 - tap_y) if flip else (tap_z, tap_y)
            if step_z == 1:
                place_rows(wide, slot, own[0], own[1], step_y)
    for parity in range(2):

        @pl.when(odd_plane == parity)
        def _():
            below, above = (odd, even) if parity == 0 else (even, odd)
            for tap_z in order:
                for tap_y in order:
                    slot = tap_z * 3 + tap_y
                    step_z, step_y = (2 - tap_z, 2 - tap_y) if flip else (tap_z, tap_y)
                    if step_z != 1:
                        piece = below if step_z == 0 else above
                        place_rows(wide, slot, piece[0], piece[1], step_y)


def moved_columns(flat, step, columns):
    count = flat.shape[0]
    column = lax.broadcasted_iota(jnp.int32, flat.shape, 0) % columns
    if step == 1:
        return jnp.where(column == 0, 0.0, pltpu.roll(flat, 1, 0))
    return jnp.where(column == columns - 1, 0.0, pltpu.roll(flat, count - 1, 0))


def over_rows(left, right):
    return lax.dot_general(left, right, (((0,), (0,)), ((), ())), preferred_element_type=F32)


def ready_kernel(block, weight, target, block_out, wide_out, target_out, sems):
    _, channels, _ = weight.shape
    moves = [
        pltpu.make_async_copy(block, block_out, sems.at[27]),
        pltpu.make_async_copy(target, target_out, sems.at[28]),
    ]
    for tap in range(27):
        slot, tap_x = tap // 3, tap % 3
        place = wide_out.at[
            slot * channels : (slot + 1) * channels, tap_x * channels : (tap_x + 1) * channels
        ]
        moves.append(pltpu.make_async_copy(weight.at[tap], place, sems.at[tap]))
    for move in moves:
        move.start()
    for move in moves:
        move.wait()


def conv_kernel(
    own, own_edge, even, even_edge, odd, odd_edge, kernel_wide, target,
    hidden_out, sheet_out, wide,
):
    rows, columns, channels = own.shape
    place_all(wide, (own, own_edge), (even, even_edge), (odd, odd_edge), False)
    flat = wide[...].reshape(rows * columns, 9 * channels)
    product = jnp.dot(flat, kernel_wide[...], preferred_element_type=F32)
    total = product[:, channels : 2 * channels]
    total = total + moved_columns(product[:, :channels], 1, columns)
    total = total + moved_columns(product[:, 2 * channels :], -1, columns)
    hidden = total.astype(BF16)
    hidden_out[...] = hidden
    features = target[...]
    second = over_rows(hidden, hidden)
    cross = over_rows(features, hidden)
    first = lax.broadcasted_iota(jnp.int32, (G, channels), 1) < G
    second = jnp.where(first, second[:G], second[G:])
    cross = jnp.where(first, cross[:G], cross[G:])
    spread, depth, _ = sheet_out.shape
    each = depth - 1
    half = spread // 2
    for j in range(half):
        sheet_out[j, 0:each, :] = second[each * j : each * (j + 1)]
        sheet_out[half + j, 0:each, :] = cross[each * j : each * (j + 1)]
    for j in range(2, spread):
        sheet_out[j, each:depth, :] = jnp.zeros((1, channels), F32)
    sheet_out[0, each:depth, :] = jnp.sum(hidden.astype(F32), axis=0, keepdims=True)
    sheet_out[1, each:depth, :] = jnp.sum(features.astype(F32), axis=0, keepdims=True)


def thirds(value):
    high = value.astype(BF16)
    rest = value - high.astype(F32)
    middle = rest.astype(BF16)
    return high, middle, (rest - middle.astype(F32)).astype(BF16)


def left_terms(value):
    high, middle, low = thirds(value)
    return jnp.concatenate([low, high, middle, middle, high, high], axis=1)


def right_terms(value):
    high, middle, low = thirds(value)
    return jnp.concatenate([high, low, middle, high, middle, high], axis=0)


def exact(left, *rights):
    if len(rights) == 1:
        right = right_terms(rights[0])
    else:
        right = jnp.concatenate([right_terms(value) for value in rights], axis=1)
    return jnp.dot(left_terms(left), right, preferred_element_type=F32)


def through(values, matrix):
    high, middle, low = thirds(matrix)
    total = jnp.dot(values, low, preferred_element_type=F32)
    total = total + jnp.dot(values, middle, preferred_element_type=F32)
    return total + jnp.dot(values, high, preferred_element_type=F32)


def whiten_kernel(
    voxels, columns, sheet, hidden, target, whitened_out, grad_out, first_out, second_out,
    mats, hidden_here, target_here, sems,
):
    hidden_move = pltpu.make_async_copy(hidden, hidden_here, sems.at[0])
    target_move = pltpu.make_async_copy(target, target_here, sems.at[1])
    hidden_move.start()
    target_move.start()
    spread, depth, channels = sheet.shape
    each = depth - 1
    for j in range(spread):
        mats[each * j : each * (j + 1), :] = sheet[j, 0:each, :]
    row = lax.broadcasted_iota(jnp.int32, (channels, channels), 0)
    col = lax.broadcasted_iota(jnp.int32, (channels, channels), 1)
    same = (row < G) == (col < G)
    diagonal = row == col
    low_lane = lax.broadcasted_iota(jnp.int32, (1, channels), 1) < G

    def group_sums(value):
        line = jnp.sum(value, axis=0, keepdims=True)
        low = jnp.sum(jnp.where(low_lane, line, 0.0), axis=1, keepdims=True)
        high = jnp.sum(jnp.where(low_lane, 0.0, line), axis=1, keepdims=True)
        return jnp.where(low_lane, low, high)

    second = jnp.concatenate([mats[:G], mats[:G]], axis=0)
    cross = jnp.concatenate([mats[G:], mats[G:]], axis=0)
    mean = sheet[0, each:depth, :] / voxels
    target_sum = sheet[1, each:depth, :]
    mean_rows = jnp.broadcast_to(mean, (channels, channels))
    mean_cols = mean_rows.T
    target_cols = jnp.broadcast_to(target_sum, (channels, channels)).T
    second = jnp.where(same, second - voxels * (mean_cols * mean_rows), 0.0)
    cross = jnp.where(same, cross - target_cols * mean_rows, 0.0)
    covariance = second / voxels + jnp.where(diagonal, EPSILON, 0.0)
    trace = group_sums(jnp.where(diagonal, covariance, 0.0))
    scaled = covariance / trace
    root = jnp.sqrt(trace)

    direction = cross / root
    iterate = jnp.where(diagonal, 1.5, 0.0) - 0.5 * scaled
    change = -0.5 * direction
    slope = jnp.where(diagonal, -0.5, 0.0)

    def column(value, i):
        return value[:, i * channels : (i + 1) * channels]

    for sweep in range(1, NEWTON):
        first = exact(iterate, iterate, scaled, change, direction)
        squared, once = column(first, 0), column(first, 1)
        turned = exact(change, iterate, scaled)
        steep = exact(slope, scaled)
        second_level = exact(squared, once, column(first, 3) + column(turned, 1), steep, iterate)
        moved = column(second_level, 1) + exact(column(first, 2) + column(turned, 0), once)
        change = 1.5 * change - 0.5 * moved
        slope = 1.5 * slope - 0.5 * (3.0 * column(second_level, 2) + column(second_level, 3))
        iterate = 1.5 * iterate - 0.5 * column(second_level, 0)
    whitener = iterate / root
    whitener_t = whitener.T
    aligned = exact(whitener, second)
    white_grad = aligned - cross
    change = exact(slope, aligned) / root - change
    trace_grad = -0.5 * group_sums(white_grad * whitener) / trace
    trace_grad = trace_grad - group_sums(change * scaled) / trace
    sigma_grad = change / trace + jnp.where(diagonal, trace_grad, 0.0)
    symmetric = (sigma_grad + sigma_grad.T) / voxels
    backward = (exact(whitener_t, whitener) + symmetric).T

    both = jnp.concatenate([whitener_t, backward], axis=1)
    offset = exact(jnp.broadcast_to(mean, (8, channels)), whitener_t, backward)[0:1]
    target_offset = exact(jnp.broadcast_to(target_sum / voxels, (8, channels)), whitener)[0:1]
    hidden_move.wait()
    target_move.wait()
    mixed = through(hidden_here[...], both) - offset
    whitened_out[...] = mixed[:, :channels].astype(BF16)
    pulled = through(target_here[...], whitener) - target_offset
    grad = (mixed[:, channels:] - pulled).astype(BF16)
    grad_out[...] = grad
    odd_row = lax.axis_index("c")

    @pl.when(odd_row == 0)
    def _():
        first_out[0] = grad[-columns:]
        second_out[0] = grad[:columns]

    @pl.when(odd_row == 1)
    def _():
        first_out[0] = grad[:columns]
        second_out[0] = grad[-columns:]


def turn_kernel(own, own_edge, even, even_edge, odd, odd_edge, turned_out):
    rows, columns, channels = own.shape
    odd_row = lax.axis_index("c")
    odd_plane = lax.rem(lax.axis_index("z"), 2)

    def turn(tap_z, plane, edge):
        for source in range(-1, rows + 1):
            if source < 0:
                tile = edge[1 - odd_row]
            elif source == rows:
                tile = edge[odd_row]
            else:
                tile = plane[source]
            tile = tile.T
            for tap_y in range(3):
                here = source + 1 - tap_y
                if 0 <= here < rows:
                    slot = tap_z * 3 + tap_y
                    turned_out[
                        slot * channels : (slot + 1) * channels,
                        here * columns : (here + 1) * columns,
                    ] = tile

    turn(1, own, own_edge)
    for parity in range(2):

        @pl.when(odd_plane == parity)
        def _():
            below, above = ((odd, odd_edge), (even, even_edge))[:: 1 - 2 * parity]
            turn(0, *below)
            turn(2, *above)


def weight_kernel(columns, share, turned, grad, keep_out, send_out, wide, terms):
    count, channels = grad.shape
    value = grad[...].astype(F32)
    wide[:, :channels] = moved_columns(value, -1, columns).astype(BF16)
    wide[:, channels : 2 * channels] = grad[...]
    wide[:, 2 * channels :] = moved_columns(value, 1, columns).astype(BF16)
    pairs = channels // share // 2
    taps_each = keep_out.shape[1] // share
    terms[...] = jnp.dot(turned[...], wide[...], preferred_element_type=F32)
    mine = pl.multiple_of(lax.axis_index("c") * share, share)
    others = pl.multiple_of((1 - lax.axis_index("c")) * share, share)
    for tap in range(keep_out.shape[0] // pairs * taps_each):
        slot, tap_x = tap // 3, tap % 3
        cols = slice(tap_x * channels, (tap_x + 1) * channels)
        place = slice(tap % taps_each * share, (tap % taps_each + 1) * share)
        for pair in range(pairs):
            group = tap // taps_each * pairs + pair
            base = slot * channels + pair * 2 * share
            if tap < 27:
                keep_out[group, place, :] = terms[pl.ds(base + mine, share), cols]
                send_out[group, place, :] = terms[pl.ds(base + others, share), cols].astype(BF16)
            else:
                keep_out[group, place, :] = jnp.zeros((share, channels), F32)
                send_out[group, place, :] = jnp.zeros((share, channels), BF16)


def pair_kernel(kept, received, sum_out):
    sum_out[...] = (kept[...] + received[...].astype(F32)).astype(BF16)


def input_kernel(
    own, own_edge, even, even_edge, odd, odd_edge, weight, grad_out, wide, kernel_wide
):
    rows, columns, channels = own.shape
    place_all(wide, (own, own_edge), (even, even_edge), (odd, odd_edge), True)
    for slot in range(9):
        for tap_x in range(3):
            kernel_wide[
                tap_x * channels : (tap_x + 1) * channels,
                slot * channels : (slot + 1) * channels,
            ] = weight[slot * 3 + tap_x]
    flat = wide[...].reshape(rows * columns, 9 * channels)
    product = lax.dot_general(
        flat, kernel_wide[...], (((1,), (1,)), ((), ())), preferred_element_type=F32
    )
    total = product[:, channels : 2 * channels]
    total = total + moved_columns(product[:, :channels], -1, columns)
    total = total + moved_columns(product[:, 2 * channels :], 1, columns)
    grad_out[...] = total.astype(BF16)


def total_kernel(scale, parts, copies_out):
    total = parts[0].astype(F32)
    for i in range(1, parts.shape[0]):
        total = total + parts[i].astype(F32)
    total = (total * scale if scale != 1.0 else total).astype(copies_out.dtype)
    for i in range(copies_out.shape[0]):
        copies_out[i] = total


def exchange(parts, axes):
    return lax.all_to_all(parts, axes, 0, 0, tiled=True)


def total_copies(parts, count, dtype, scale=1.0):
    shape = jax.ShapeDtypeStruct((count,) + parts.shape[1:], dtype)
    return call(
        lambda *refs: total_kernel(scale, *refs), shape, [], parts.size, 2 * parts.size, parts
    )


def local(volume, conv_weight, target):
    _, rows, columns, channels = volume.shape
    count = rows * columns
    voxels = count * lax.axis_size(GZ) * lax.axis_size(GY)
    spread = lax.axis_size(SPREAD)
    levels = lax.axis_size("z")
    rows_y = lax.axis_size("y")
    share = channels // lax.axis_size(GY)
    taps_each = -(-27 // rows_y)
    flops = 2 * count * 27 * channels * channels
    weight = conv_weight.reshape(27, channels, channels)
    target_flat = target.reshape(count, channels)

    block = volume.reshape(rows, columns, channels)
    odd_row = lax.axis_index("c")
    first_send = lax.dynamic_slice_in_dim(block, (1 - odd_row) * (rows - 1), 1, 0)
    second_send = lax.dynamic_slice_in_dim(block, odd_row * (rows - 1), 1, 0)
    edges = row_swaps(first_send, second_send)
    even, odd = plane_swaps(block)
    even_edges, odd_edges = plane_swaps(edges)
    near, kernel_wide, target_near = call(
        ready_kernel,
        [
            jax.ShapeDtypeStruct(block.shape, BF16),
            jax.ShapeDtypeStruct((9 * channels, 3 * channels), BF16),
            jax.ShapeDtypeStruct((count, channels), BF16),
        ],
        [pltpu.SemaphoreType.DMA((29,))],
        0, 2**20, block, weight, target_flat, far=(0, 1, 2),
    )
    planes = [near, edges, even, even_edges, odd, odd_edges]
    wide = pltpu.VMEM((rows, columns, 9 * channels), BF16)
    hidden, sheet = call(
        conv_kernel,
        [
            jax.ShapeDtypeStruct((count, channels), BF16),
            jax.ShapeDtypeStruct((spread, 2 * G // spread + 1, channels), F32),
        ],
        [wide],
        flops, 3 * 2**20, *planes, kernel_wide, target_near,
    )
    turned = call(
        turn_kernel,
        jax.ShapeDtypeStruct((9 * channels, count), BF16),
        [], 0, 3 * 2**20, *planes,
    )

    mine = total_copies(exchange(sheet, SPREAD), levels, F32)
    mine = total_copies(exchange(mine, ("z",)), spread, F32)
    sheet = exchange(mine, SPREAD)
    line = jax.ShapeDtypeStruct((1, columns, channels), BF16)
    whitened, grad_hidden, first_send, second_send = call(
        lambda *refs: whiten_kernel(voxels, columns, *refs),
        [jax.ShapeDtypeStruct((count, channels), BF16)] * 2 + [line] * 2,
        [
            pltpu.VMEM((2 * G, channels), F32),
            pltpu.VMEM((count, channels), BF16),
            pltpu.VMEM((count, channels), BF16),
            pltpu.SemaphoreType.DMA((2,)),
        ],
        100 * 2 * channels**3, 2**20, sheet, hidden, target_flat, far=(1, 2),
    )

    groups = spread // 2
    shape = (groups, taps_each * share, channels)
    keep, send = call(
        lambda *refs: weight_kernel(columns, share, *refs),
        [jax.ShapeDtypeStruct(shape, F32), jax.ShapeDtypeStruct(shape, BF16)],
        [
            pltpu.VMEM((count, 3 * channels), BF16),
            pltpu.VMEM((9 * channels, 3 * channels), F32),
        ],
        flops, 4 * 2**20, turned, grad_hidden,
    )
    received = lax.ppermute(send, ("c",), [(0, 1), (1, 0)])
    parts = call(
        pair_kernel, jax.ShapeDtypeStruct(shape, BF16), [], keep.size, 2**21, keep, received
    )
    block, first_send, second_send, parts = lax.optimization_barrier(
        (grad_hidden.reshape(rows, columns, channels), first_send, second_send, parts)
    )
    edges = row_swaps(first_send, second_send)
    even, odd = plane_swaps(block)
    part = total_copies(exchange(parts, ("y", "x")), levels, BF16)
    part, edges, even, odd = lax.optimization_barrier((part, edges, even, odd))
    even_edges, odd_edges = plane_swaps(edges)
    part = total_copies(exchange(part, ("z",)), rows_y, F32, 1.0 / math.sqrt(voxels))
    part, even_edges, odd_edges = lax.optimization_barrier((part, even_edges, odd_edges))
    whole = exchange(part, ("y",))
    weight_grad = whole.reshape(rows_y * taps_each, share, channels)[:27]
    weight_grad = weight_grad.reshape(3, 3, 3, share, channels)

    planes = [block, edges, even, even_edges, odd, odd_edges]
    input_grad = call(
        input_kernel,
        jax.ShapeDtypeStruct((count, channels), BF16),
        [wide, pltpu.VMEM((3 * channels, 9 * channels), BF16)],
        flops, 3 * 2**20, *planes, weight,
    )
    return (whitened.reshape(volume.shape), input_grad.reshape(volume.shape), weight_grad)


def solution(mesh):
    cells = mesh.devices.reshape(4, 8, 4, 2)
    split = Mesh(cells, ("y", "z", "x", "c"))
    in_specs = (P(GZ, GY, None, None), P(), P(GZ, GY, None, None))
    out_specs = (
        P(GZ, GY, None, None),
        P(GZ, GY, None, None),
        P(None, None, None, GY, None),
    )
    return jax.shard_map(local, mesh=split, in_specs=in_specs, out_specs=out_specs, check_vma=False)
```

```python
import math

import jax
import jax.numpy as jnp
from jax import lax
from jax.experimental import pallas as pl
from jax.experimental.pallas import tpu as pltpu
from jax.sharding import Mesh, PartitionSpec as P

G = 64
NEWTON = 5
EPSILON = 1e-05
HIGHEST = lax.Precision.HIGHEST
F32 = jnp.float32
BF16 = jnp.bfloat16
GZ = ("y", "z")
GY = ("x", "c")
SPREAD = ("y", "x", "c")
VMEM_BYTES = 20 * 1024 * 1024
JOIN_FLOPS = 2 * 2**30


def swapped(block, axes, count, first):
    pairs = []
    for i in range(first, count - 1, 2):
        pairs += [(i, i + 1), (i + 1, i)]
    return lax.ppermute(block, axes, pairs)


def join_kernel(even, odd, rows_out):
    rows_out[0:1] = even[...]
    rows_out[1:2] = odd[...]


def row_swaps(first_send, second_send):
    ny = lax.axis_size(GY)
    even, odd = swapped(first_send, GY, ny, 0), swapped(second_send, GY, ny, 1)
    joined = jax.ShapeDtypeStruct((2,) + even.shape[1:], BF16)
    return call(join_kernel, joined, [], JOIN_FLOPS, 2**18, even, odd)


def plane_swaps(block):
    nz = lax.axis_size(GZ)
    return swapped(block, GZ, nz, 0), swapped(block, GZ, nz, 1)


def call(kernel, out_shape, scratch, flops, moved, *operands, far=()):
    vmem = pl.BlockSpec(memory_space=pltpu.VMEM)
    hbm = pl.BlockSpec(memory_space=pltpu.HBM)
    many = isinstance(out_shape, (list, tuple))
    return pl.pallas_call(
        kernel,
        out_shape=out_shape,
        in_specs=[hbm if i in far else vmem for i in range(len(operands))],
        out_specs=[vmem] * len(out_shape) if many else vmem,
        scratch_shapes=scratch,
        compiler_params=pltpu.CompilerParams(vmem_limit_bytes=VMEM_BYTES),
        cost_estimate=pl.CostEstimate(flops=flops, bytes_accessed=moved, transcendentals=0),
    )(*operands)


def place_rows(wide, slot, plane, edge, tap_y):
    rows, _, channels = plane.shape
    cols = slice(slot * channels, (slot + 1) * channels)
    odd_row = lax.axis_index("c")
    if tap_y == 0:
        wide[0:1, :, cols] = edge[pl.ds(1 - odd_row, 1)]
        wide[1:rows, :, cols] = plane[0 : rows - 1]
    elif tap_y == 1:
        wide[:, :, cols] = plane[...]
    else:
        wide[0 : rows - 1, :, cols] = plane[1:rows]
        wide[rows - 1 : rows, :, cols] = edge[pl.ds(odd_row, 1)]


def place_all(wide, own, even, odd, flip):
    odd_plane = lax.rem(lax.axis_index("z"), 2)

    order = range(3)
    for tap_z in order:
        for tap_y in order:
            slot = tap_z * 3 + tap_y
            step_z, step_y = (2 - tap_z, 2 - tap_y) if flip else (tap_z, tap_y)
            if step_z == 1:
                place_rows(wide, slot, own[0], own[1], step_y)
    for parity in range(2):

        @pl.when(odd_plane == parity)
        def _():
            below, above = (odd, even) if parity == 0 else (even, odd)
            for tap_z in order:
                for tap_y in order:
                    slot = tap_z * 3 + tap_y
                    step_z, step_y = (2 - tap_z, 2 - tap_y) if flip else (tap_z, tap_y)
                    if step_z != 1:
                        piece = below if step_z == 0 else above
                        place_rows(wide, slot, piece[0], piece[1], step_y)


def moved_columns(flat, step, columns):
    count = flat.shape[0]
    column = lax.broadcasted_iota(jnp.int32, flat.shape, 0) % columns
    if step == 1:
        return jnp.where(column == 0, 0.0, pltpu.roll(flat, 1, 0))
    return jnp.where(column == columns - 1, 0.0, pltpu.roll(flat, count - 1, 0))


def over_rows(left, right):
    return lax.dot_general(left, right, (((0,), (0,)), ((), ())), preferred_element_type=F32)


def ready_kernel(block, weight, target, block_out, wide_out, target_out, sems):
    _, channels, _ = weight.shape
    moves = [
        pltpu.make_async_copy(block, block_out, sems.at[27]),
        pltpu.make_async_copy(target, target_out, sems.at[28]),
    ]
    for tap in range(27):
        slot, tap_x = tap // 3, tap % 3
        place = wide_out.at[
            slot * channels : (slot + 1) * channels, tap_x * channels : (tap_x + 1) * channels
        ]
        moves.append(pltpu.make_async_copy(weight.at[tap], place, sems.at[tap]))
    for move in moves:
        move.start()
    for move in moves:
        move.wait()


def conv_kernel(
    own, own_edge, even, even_edge, odd, odd_edge, kernel_wide, target,
    hidden_out, sheet_out, wide,
):
    rows, columns, channels = own.shape
    place_all(wide, (own, own_edge), (even, even_edge), (odd, odd_edge), False)
    flat = wide[...].reshape(rows * columns, 9 * channels)
    product = jnp.dot(flat, kernel_wide[...], preferred_element_type=F32)
    total = product[:, channels : 2 * channels]
    total = total + moved_columns(product[:, :channels], 1, columns)
    total = total + moved_columns(product[:, 2 * channels :], -1, columns)
    hidden = total.astype(BF16)
    hidden_out[...] = hidden
    features = target[...]
    second = over_rows(hidden, hidden)
    cross = over_rows(features, hidden)
    first = lax.broadcasted_iota(jnp.int32, (G, channels), 1) < G
    second = jnp.where(first, second[:G], second[G:])
    cross = jnp.where(first, cross[:G], cross[G:])
    spread, depth, _ = sheet_out.shape
    each = depth - 1
    half = spread // 2
    for j in range(half):
        sheet_out[j, 0:each, :] = second[each * j : each * (j + 1)]
        sheet_out[half + j, 0:each, :] = cross[each * j : each * (j + 1)]
    for j in range(2, spread):
        sheet_out[j, each:depth, :] = jnp.zeros((1, channels), F32)
    sheet_out[0, each:depth, :] = jnp.sum(hidden.astype(F32), axis=0, keepdims=True)
    sheet_out[1, each:depth, :] = jnp.sum(features.astype(F32), axis=0, keepdims=True)


def thirds(value):
    high = value.astype(BF16)
    rest = value - high.astype(F32)
    middle = rest.astype(BF16)
    return high, middle, (rest - middle.astype(F32)).astype(BF16)


def left_terms(value):
    high, middle, low = thirds(value)
    return jnp.concatenate([low, high, middle, middle, high, high], axis=1)


def right_terms(value):
    high, middle, low = thirds(value)
    return jnp.concatenate([high, low, middle, high, middle, high], axis=0)


def exact(left, *rights):
    if len(rights) == 1:
        right = right_terms(rights[0])
    else:
        right = jnp.concatenate([right_terms(value) for value in rights], axis=1)
    return jnp.dot(left_terms(left), right, preferred_element_type=F32)


def through(values, matrix):
    high, middle, low = thirds(matrix)
    total = jnp.dot(values, low, preferred_element_type=F32)
    total = total + jnp.dot(values, middle, preferred_element_type=F32)
    return total + jnp.dot(values, high, preferred_element_type=F32)


def grad_kernel(
    voxels, columns, share, sheet, hidden, target, turned,
    grad_out, first_out, second_out, keep_out, send_out, whitener_out, offset_out,
    mats, wide, terms,
):
    spread, depth, channels = sheet.shape
    each = depth - 1
    for j in range(spread):
        mats[each * j : each * (j + 1), :] = sheet[j, 0:each, :]
    row = lax.broadcasted_iota(jnp.int32, (channels, channels), 0)
    col = lax.broadcasted_iota(jnp.int32, (channels, channels), 1)
    same = (row < G) == (col < G)
    diagonal = row == col
    low_lane = lax.broadcasted_iota(jnp.int32, (1, channels), 1) < G

    def group_sums(value):
        line = jnp.sum(value, axis=0, keepdims=True)
        low = jnp.sum(jnp.where(low_lane, line, 0.0), axis=1, keepdims=True)
        high = jnp.sum(jnp.where(low_lane, 0.0, line), axis=1, keepdims=True)
        return jnp.where(low_lane, low, high)

    second = jnp.concatenate([mats[:G], mats[:G]], axis=0)
    cross = jnp.concatenate([mats[G:], mats[G:]], axis=0)
    mean = sheet[0, each:depth, :] / voxels
    target_sum = sheet[1, each:depth, :]
    mean_rows = jnp.broadcast_to(mean, (channels, channels))
    mean_cols = mean_rows.T
    target_cols = jnp.broadcast_to(target_sum, (channels, channels)).T
    second = jnp.where(same, second - voxels * (mean_cols * mean_rows), 0.0)
    cross = jnp.where(same, cross - target_cols * mean_rows, 0.0)
    covariance = second / voxels + jnp.where(diagonal, EPSILON, 0.0)
    trace = group_sums(jnp.where(diagonal, covariance, 0.0))
    scaled = covariance / trace
    root = jnp.sqrt(trace)

    direction = cross / root
    iterate = jnp.where(diagonal, 1.5, 0.0) - 0.5 * scaled
    change = -0.5 * direction
    slope = jnp.where(diagonal, -0.5, 0.0)

    def column(value, i):
        return value[:, i * channels : (i + 1) * channels]

    for sweep in range(1, NEWTON):
        first = exact(iterate, iterate, scaled, change, direction)
        squared, once = column(first, 0), column(first, 1)
        crossed = exact(change, iterate, scaled)
        steep = exact(slope, scaled)
        second_level = exact(squared, once, column(first, 3) + column(crossed, 1), steep, iterate)
        moved = column(second_level, 1) + exact(column(first, 2) + column(crossed, 0), once)
        change = 1.5 * change - 0.5 * moved
        slope = 1.5 * slope - 0.5 * (3.0 * column(second_level, 2) + column(second_level, 3))
        iterate = 1.5 * iterate - 0.5 * column(second_level, 0)
    whitener = iterate / root
    whitener_t = whitener.T
    aligned = exact(whitener, second)
    white_grad = aligned - cross
    change = exact(slope, aligned) / root - change
    trace_grad = -0.5 * group_sums(white_grad * whitener) / trace
    trace_grad = trace_grad - group_sums(change * scaled) / trace
    sigma_grad = change / trace + jnp.where(diagonal, trace_grad, 0.0)
    symmetric = (sigma_grad + sigma_grad.T) / voxels
    backward = (exact(whitener_t, whitener) + symmetric).T

    offset = exact(jnp.broadcast_to(mean, (8, channels)), whitener_t, backward)
    target_offset = exact(jnp.broadcast_to(target_sum / voxels, (8, channels)), whitener)
    whitener_out[...] = whitener_t
    offset_out[...] = offset[:, :channels]
    grad = through(hidden[...], backward) - through(target[...], whitener)
    wide_grad = grad - (offset[:1, channels:] - target_offset[:1])
    grad = wide_grad.astype(BF16)
    grad_out[...] = grad
    odd_row = lax.axis_index("c")

    @pl.when(odd_row == 0)
    def _():
        first_out[0] = grad[-columns:]
        second_out[0] = grad[:columns]

    @pl.when(odd_row == 1)
    def _():
        first_out[0] = grad[:columns]
        second_out[0] = grad[-columns:]

    weight_terms(columns, share, turned, grad, keep_out, send_out, wide, terms)


def white_kernel(hidden, whitener, offset, whitened_out):
    whitened_out[...] = (through(hidden[...], whitener[...]) - offset[0:1]).astype(BF16)


def turn_kernel(
    own, own_edge, even, even_edge, odd, odd_edge, hidden, target,
    turned_out, hidden_out, target_out,
):
    hidden_out[...] = hidden[...]
    target_out[...] = target[...]
    rows, columns, channels = own.shape
    odd_row = lax.axis_index("c")
    odd_plane = lax.rem(lax.axis_index("z"), 2)

    def turn(tap_z, plane, edge):
        for source in range(-1, rows + 1):
            if source < 0:
                tile = edge[1 - odd_row]
            elif source == rows:
                tile = edge[odd_row]
            else:
                tile = plane[source]
            tile = tile.T
            for tap_y in range(3):
                here = source + 1 - tap_y
                if 0 <= here < rows:
                    slot = tap_z * 3 + tap_y
                    turned_out[
                        slot * channels : (slot + 1) * channels,
                        here * columns : (here + 1) * columns,
                    ] = tile

    turn(1, own, own_edge)
    for parity in range(2):

        @pl.when(odd_plane == parity)
        def _():
            below, above = ((odd, odd_edge), (even, even_edge))[:: 1 - 2 * parity]
            turn(0, *below)
            turn(2, *above)


def weight_terms(columns, share, turned, grad, keep_out, send_out, wide, terms):
    _, channels = grad.shape
    value = grad.astype(F32)
    wide[:, :channels] = moved_columns(value, -1, columns).astype(BF16)
    wide[:, channels : 2 * channels] = grad
    wide[:, 2 * channels :] = moved_columns(value, 1, columns).astype(BF16)
    pairs = channels // share // 2
    taps_each = keep_out.shape[1] // share
    terms[...] = jnp.dot(turned[...], wide[...], preferred_element_type=F32)
    mine = pl.multiple_of(lax.axis_index("c") * share, share)
    others = pl.multiple_of((1 - lax.axis_index("c")) * share, share)
    for tap in range(keep_out.shape[0] // pairs * taps_each):
        slot, tap_x = tap // 3, tap % 3
        cols = slice(tap_x * channels, (tap_x + 1) * channels)
        place = slice(tap % taps_each * share, (tap % taps_each + 1) * share)
        for pair in range(pairs):
            group = tap // taps_each * pairs + pair
            base = slot * channels + pair * 2 * share
            if tap < 27:
                keep_out[group, place, :] = terms[pl.ds(base + mine, share), cols]
                send_out[group, place, :] = terms[pl.ds(base + others, share), cols].astype(BF16)
            else:
                keep_out[group, place, :] = jnp.zeros((share, channels), F32)
                send_out[group, place, :] = jnp.zeros((share, channels), BF16)


def pair_kernel(kept, received, sum_out):
    sum_out[...] = (kept[...] + received[...].astype(F32)).astype(BF16)


def input_kernel(
    own, own_edge, even, even_edge, odd, odd_edge, weight, grad_out, wide, kernel_wide
):
    rows, columns, channels = own.shape
    place_all(wide, (own, own_edge), (even, even_edge), (odd, odd_edge), True)
    for slot in range(9):
        for tap_x in range(3):
            kernel_wide[
                tap_x * channels : (tap_x + 1) * channels,
                slot * channels : (slot + 1) * channels,
            ] = weight[slot * 3 + tap_x]
    flat = wide[...].reshape(rows * columns, 9 * channels)
    product = lax.dot_general(
        flat, kernel_wide[...], (((1,), (1,)), ((), ())), preferred_element_type=F32
    )
    total = product[:, channels : 2 * channels]
    total = total + moved_columns(product[:, :channels], -1, columns)
    total = total + moved_columns(product[:, 2 * channels :], 1, columns)
    grad_out[...] = total.astype(BF16)


def total_kernel(scale, parts, copies_out):
    total = parts[0].astype(F32)
    for i in range(1, parts.shape[0]):
        total = total + parts[i].astype(F32)
    total = (total * scale if scale != 1.0 else total).astype(copies_out.dtype)
    for i in range(copies_out.shape[0]):
        copies_out[i] = total


def exchange(parts, axes):
    return lax.all_to_all(parts, axes, 0, 0, tiled=True)


def total_copies(parts, count, dtype, scale=1.0):
    shape = jax.ShapeDtypeStruct((count,) + parts.shape[1:], dtype)
    return call(
        lambda *refs: total_kernel(scale, *refs), shape, [], parts.size, 2 * parts.size, parts
    )


def local(volume, conv_weight, target):
    _, rows, columns, channels = volume.shape
    count = rows * columns
    voxels = count * lax.axis_size(GZ) * lax.axis_size(GY)
    spread = lax.axis_size(SPREAD)
    levels = lax.axis_size("z")
    rows_y = lax.axis_size("y")
    share = channels // lax.axis_size(GY)
    taps_each = -(-27 // rows_y)
    flops = 2 * count * 27 * channels * channels
    weight = conv_weight.reshape(27, channels, channels)
    target_flat = target.reshape(count, channels)

    block = volume.reshape(rows, columns, channels)
    odd_row = lax.axis_index("c")
    first_send = lax.dynamic_slice_in_dim(block, (1 - odd_row) * (rows - 1), 1, 0)
    second_send = lax.dynamic_slice_in_dim(block, odd_row * (rows - 1), 1, 0)
    edges = row_swaps(first_send, second_send)
    even, odd = plane_swaps(block)
    even_edges, odd_edges = plane_swaps(edges)
    near, kernel_wide, target_near = call(
        ready_kernel,
        [
            jax.ShapeDtypeStruct(block.shape, BF16),
            jax.ShapeDtypeStruct((9 * channels, 3 * channels), BF16),
            jax.ShapeDtypeStruct((count, channels), BF16),
        ],
        [pltpu.SemaphoreType.DMA((29,))],
        0, 2**20, block, weight, target_flat, far=(0, 1, 2),
    )
    planes = [near, edges, even, even_edges, odd, odd_edges]
    wide = pltpu.VMEM((rows, columns, 9 * channels), BF16)
    hidden, sheet = call(
        conv_kernel,
        [
            jax.ShapeDtypeStruct((count, channels), BF16),
            jax.ShapeDtypeStruct((spread, 2 * G // spread + 1, channels), F32),
        ],
        [wide],
        flops, 3 * 2**20, *planes, kernel_wide, target_near,
    )
    flat = jax.ShapeDtypeStruct((count, channels), BF16)
    turned, hidden, target_near = call(
        turn_kernel,
        [jax.ShapeDtypeStruct((9 * channels, count), BF16), flat, flat],
        [], 0, 3 * 2**20, *planes, hidden, target_flat,
    )

    mine = total_copies(exchange(sheet, SPREAD), levels, F32)
    mine = total_copies(exchange(mine, ("z",)), spread, F32)
    sheet = exchange(mine, SPREAD)
    line = jax.ShapeDtypeStruct((1, columns, channels), BF16)
    groups = spread // 2
    shape = (groups, taps_each * share, channels)
    grad_hidden, first_send, second_send, keep, send, whitener, offset = call(
        lambda *refs: grad_kernel(voxels, columns, share, *refs),
        [
            flat, line, line,
            jax.ShapeDtypeStruct(shape, F32),
            jax.ShapeDtypeStruct(shape, BF16),
            jax.ShapeDtypeStruct((channels, channels), F32),
            jax.ShapeDtypeStruct((8, channels), F32),
        ],
        [
            pltpu.VMEM((2 * G, channels), F32),
            pltpu.VMEM((count, 3 * channels), BF16),
            pltpu.VMEM((9 * channels, 3 * channels), F32),
        ],
        flops, 2**20, sheet, hidden, target_near, turned,
    )
    received = lax.ppermute(send, ("c",), [(0, 1), (1, 0)])
    parts = call(
        pair_kernel, jax.ShapeDtypeStruct(shape, BF16), [], keep.size, 2**21, keep, received
    )
    block, first_send, second_send, whitener, parts = lax.optimization_barrier(
        (grad_hidden.reshape(rows, columns, channels), first_send, second_send, whitener, parts)
    )
    whitened = call(white_kernel, flat, [], flops, 2**20, hidden, whitener, offset)
    edges = row_swaps(first_send, second_send)
    even, odd = plane_swaps(block)
    part = total_copies(exchange(parts, ("y", "x")), levels, BF16)
    part, edges, even, odd, whitened = lax.optimization_barrier(
        (part, edges, even, odd, whitened)
    )
    even_edges, odd_edges = plane_swaps(edges)
    part = total_copies(exchange(part, ("z",)), rows_y, BF16, 1.0 / math.sqrt(voxels))
    part, even_edges, odd_edges = lax.optimization_barrier((part, even_edges, odd_edges))
    whole = exchange(part, ("y",))
    weight_grad = whole.reshape(rows_y * taps_each, share, channels)[:27].astype(F32)
    weight_grad = weight_grad.reshape(3, 3, 3, share, channels)

    planes = [block, edges, even, even_edges, odd, odd_edges]
    input_grad = call(
        input_kernel,
        jax.ShapeDtypeStruct((count, channels), BF16),
        [wide, pltpu.VMEM((3 * channels, 9 * channels), BF16)],
        flops, 3 * 2**20, *planes, weight,
    )
    return (whitened.reshape(volume.shape), input_grad.reshape(volume.shape), weight_grad)


def solution(mesh):
    cells = mesh.devices.reshape(4, 8, 4, 2)
    split = Mesh(cells, ("y", "z", "x", "c"))
    in_specs = (P(GZ, GY, None, None), P(), P(GZ, GY, None, None))
    out_specs = (
        P(GZ, GY, None, None),
        P(GZ, GY, None, None),
        P(None, None, None, GY, None),
    )
    return jax.shard_map(local, mesh=split, in_specs=in_specs, out_specs=out_specs, check_vma=False)
```

```python
import math

import jax
import jax.numpy as jnp
from jax import lax
from jax.experimental import pallas as pl
from jax.experimental.pallas import tpu as pltpu
from jax.sharding import Mesh, PartitionSpec as P

G = 64
NEWTON = 5
EPSILON = 1e-05
HIGHEST = lax.Precision.HIGHEST
F32 = jnp.float32
BF16 = jnp.bfloat16
GZ = ("y", "z")
GY = ("x", "c")
SPREAD = ("y", "x", "c")
VMEM_BYTES = 12 * 1024 * 1024


def swapped(block, axes, count, first):
    pairs = []
    for i in range(first, count - 1, 2):
        pairs += [(i, i + 1), (i + 1, i)]
    return lax.ppermute(block, axes, pairs)


def ends_kernel(own, even, odd, first_out, second_out):
    last = own.shape[0] - 1
    odd_row = lax.axis_index("c")
    for place, plane in enumerate((own, even, odd)):
        first_out[place : place + 1] = plane[pl.ds((1 - odd_row) * last, 1)]
        second_out[place : place + 1] = plane[pl.ds(odd_row * last, 1)]


def row_swaps(own, even, odd):
    ny = lax.axis_size(GY)
    ends = jax.ShapeDtypeStruct((3,) + own.shape[1:], BF16)
    first, second = call(ends_kernel, [ends, ends], [], 0, 2**18, own, even, odd)
    return swapped(first, GY, ny, 0), swapped(second, GY, ny, 1)


def plane_swaps(block):
    nz = lax.axis_size(GZ)
    return swapped(block, GZ, nz, 0), swapped(block, GZ, nz, 1)


def call(kernel, out_shape, scratch, flops, moved, *operands, far=()):
    vmem = pl.BlockSpec(memory_space=pltpu.VMEM)
    hbm = pl.BlockSpec(memory_space=pltpu.HBM)
    many = isinstance(out_shape, (list, tuple))
    return pl.pallas_call(
        kernel,
        out_shape=out_shape,
        in_specs=[hbm if i in far else vmem for i in range(len(operands))],
        out_specs=[vmem] * len(out_shape) if many else vmem,
        scratch_shapes=scratch,
        compiler_params=pltpu.CompilerParams(vmem_limit_bytes=VMEM_BYTES),
        cost_estimate=pl.CostEstimate(flops=flops, bytes_accessed=moved, transcendentals=0),
    )(*operands)


def place_rows(wide, slot, plane, edge, tap_y):
    rows, _, channels = plane.shape
    cols = slice(slot * channels, (slot + 1) * channels)
    odd_row = lax.axis_index("c")
    if tap_y == 0:
        wide[0:1, :, cols] = edge[0][pl.ds(1 - odd_row, 1), edge[1]]
        wide[1:rows, :, cols] = plane[0 : rows - 1]
    elif tap_y == 1:
        wide[:, :, cols] = plane[...]
    else:
        wide[0 : rows - 1, :, cols] = plane[1:rows]
        wide[rows - 1 : rows, :, cols] = edge[0][pl.ds(odd_row, 1), edge[1]]


def gather_rows(even_rows, odd_rows, ends):
    ends[0] = even_rows[...]
    ends[1] = odd_rows[...]


def place_all(wide, own, even, odd, flip):
    odd_plane = lax.rem(lax.axis_index("z"), 2)

    order = range(3)
    for tap_z in order:
        for tap_y in order:
            slot = tap_z * 3 + tap_y
            step_z, step_y = (2 - tap_z, 2 - tap_y) if flip else (tap_z, tap_y)
            if step_z == 1:
                place_rows(wide, slot, own[0], own[1], step_y)
    for parity in range(2):

        @pl.when(odd_plane == parity)
        def _():
            below, above = (odd, even) if parity == 0 else (even, odd)
            for tap_z in order:
                for tap_y in order:
                    slot = tap_z * 3 + tap_y
                    step_z, step_y = (2 - tap_z, 2 - tap_y) if flip else (tap_z, tap_y)
                    if step_z != 1:
                        piece = below if step_z == 0 else above
                        place_rows(wide, slot, piece[0], piece[1], step_y)


def moved_columns(flat, step, columns):
    count = flat.shape[0]
    column = lax.broadcasted_iota(jnp.int32, flat.shape, 0) % columns
    if step == 1:
        return jnp.where(column == 0, 0.0, pltpu.roll(flat, 1, 0))
    return jnp.where(column == columns - 1, 0.0, pltpu.roll(flat, count - 1, 0))


def over_rows(left, right):
    return lax.dot_general(left, right, (((0,), (0,)), ((), ())), preferred_element_type=F32)


def ready_kernel(block, weight, target, block_out, wide_out, target_out, sems):
    _, channels, _ = weight.shape
    moves = [
        pltpu.make_async_copy(block, block_out, sems.at[27]),
        pltpu.make_async_copy(target, target_out, sems.at[28]),
    ]
    for tap in range(27):
        slot, tap_x = tap // 3, tap % 3
        place = wide_out.at[
            slot * channels : (slot + 1) * channels, tap_x * channels : (tap_x + 1) * channels
        ]
        moves.append(pltpu.make_async_copy(weight.at[tap], place, sems.at[tap]))
    for move in moves:
        move.start()
    for move in moves:
        move.wait()


def conv_kernel(
    own, even, odd, even_rows, odd_rows, kernel_wide, target,
    hidden_out, sheet_out, wide, ends,
):
    rows, columns, channels = own.shape
    gather_rows(even_rows, odd_rows, ends)
    place_all(wide, (own, (ends, 0)), (even, (ends, 1)), (odd, (ends, 2)), False)
    flat = wide[...].reshape(rows * columns, 9 * channels)
    product = jnp.dot(flat, kernel_wide[...], preferred_element_type=F32)
    total = product[:, channels : 2 * channels]
    total = total + moved_columns(product[:, :channels], 1, columns)
    total = total + moved_columns(product[:, 2 * channels :], -1, columns)
    hidden = total.astype(BF16)
    hidden_out[...] = hidden
    features = target[...]
    second = over_rows(hidden, hidden)
    cross = over_rows(features, hidden)
    first = lax.broadcasted_iota(jnp.int32, (G, channels), 1) < G
    second = jnp.where(first, second[:G], second[G:])
    cross = jnp.where(first, cross[:G], cross[G:])
    spread, depth, _ = sheet_out.shape
    each = depth - 1
    half = spread // 2
    for j in range(half):
        sheet_out[j, 0:each, :] = second[each * j : each * (j + 1)]
        sheet_out[half + j, 0:each, :] = cross[each * j : each * (j + 1)]
    for j in range(2, spread):
        sheet_out[j, each:depth, :] = jnp.zeros((1, channels), F32)
    sheet_out[0, each:depth, :] = jnp.sum(hidden.astype(F32), axis=0, keepdims=True)
    sheet_out[1, each:depth, :] = jnp.sum(features.astype(F32), axis=0, keepdims=True)


def thirds(value):
    high = value.astype(BF16)
    rest = value - high.astype(F32)
    middle = rest.astype(BF16)
    return high, middle, (rest - middle.astype(F32)).astype(BF16)


def left_terms(value):
    high, middle, low = thirds(value)
    return jnp.concatenate([low, high, middle, middle, high, high], axis=1)


def right_terms(value):
    high, middle, low = thirds(value)
    return jnp.concatenate([high, low, middle, high, middle, high], axis=0)


def exact(left, *rights):
    if len(rights) == 1:
        right = right_terms(rights[0])
    else:
        right = jnp.concatenate([right_terms(value) for value in rights], axis=1)
    return jnp.dot(left_terms(left), right, preferred_element_type=F32)


def through(values, matrix):
    high, middle, low = thirds(matrix)
    total = jnp.dot(values, low, preferred_element_type=F32)
    total = total + jnp.dot(values, middle, preferred_element_type=F32)
    return total + jnp.dot(values, high, preferred_element_type=F32)


def grad_kernel(
    voxels, columns, share, sheet, pack,
    grad_out, keep_out, send_out, whitener_out, offset_out,
    mats, wide, terms, taps,
):
    place_turned(columns, pack, taps)
    count = taps.shape[1]
    base = pack.shape[0] - 2 * count
    spread, depth, channels = sheet.shape
    each = depth - 1
    for j in range(spread):
        mats[each * j : each * (j + 1), :] = sheet[j, 0:each, :]
    row = lax.broadcasted_iota(jnp.int32, (channels, channels), 0)
    col = lax.broadcasted_iota(jnp.int32, (channels, channels), 1)
    same = (row < G) == (col < G)
    diagonal = row == col
    low_lane = lax.broadcasted_iota(jnp.int32, (1, channels), 1) < G

    def group_sums(value):
        line = jnp.sum(value, axis=0, keepdims=True)
        low = jnp.sum(jnp.where(low_lane, line, 0.0), axis=1, keepdims=True)
        high = jnp.sum(jnp.where(low_lane, 0.0, line), axis=1, keepdims=True)
        return jnp.where(low_lane, low, high)

    second = jnp.concatenate([mats[:G], mats[:G]], axis=0)
    cross = jnp.concatenate([mats[G:], mats[G:]], axis=0)
    mean = sheet[0, each:depth, :] / voxels
    target_sum = sheet[1, each:depth, :]
    mean_rows = jnp.broadcast_to(mean, (channels, channels))
    mean_cols = mean_rows.T
    target_cols = jnp.broadcast_to(target_sum, (channels, channels)).T
    second = jnp.where(same, second - voxels * (mean_cols * mean_rows), 0.0)
    cross = jnp.where(same, cross - target_cols * mean_rows, 0.0)
    covariance = second / voxels + jnp.where(diagonal, EPSILON, 0.0)
    trace = group_sums(jnp.where(diagonal, covariance, 0.0))
    scaled = covariance / trace
    root = jnp.sqrt(trace)

    direction = cross / root
    iterate = jnp.where(diagonal, 1.5, 0.0) - 0.5 * scaled
    change = -0.5 * direction
    slope = jnp.where(diagonal, -0.5, 0.0)

    def column(value, i):
        return value[:, i * channels : (i + 1) * channels]

    for sweep in range(1, NEWTON):
        first = exact(iterate, iterate, scaled, change, direction)
        squared, once = column(first, 0), column(first, 1)
        crossed = exact(change, iterate, scaled)
        steep = exact(slope, scaled)
        second_level = exact(squared, once, column(first, 3) + column(crossed, 1), steep, iterate)
        moved = column(second_level, 1) + exact(column(first, 2) + column(crossed, 0), once)
        change = 1.5 * change - 0.5 * moved
        slope = 1.5 * slope - 0.5 * (3.0 * column(second_level, 2) + column(second_level, 3))
        iterate = 1.5 * iterate - 0.5 * column(second_level, 0)
    whitener = iterate / root
    whitener_t = whitener.T
    aligned = exact(whitener, second)
    white_grad = aligned - cross
    change = exact(slope, aligned) / root - change
    trace_grad = -0.5 * group_sums(white_grad * whitener) / trace
    trace_grad = trace_grad - group_sums(change * scaled) / trace
    sigma_grad = change / trace + jnp.where(diagonal, trace_grad, 0.0)
    symmetric = (sigma_grad + sigma_grad.T) / voxels
    backward = (exact(whitener_t, whitener) + symmetric).T

    offset = exact(jnp.broadcast_to(mean, (8, channels)), whitener_t, backward)
    target_offset = exact(jnp.broadcast_to(target_sum / voxels, (8, channels)), whitener)
    whitener_out[...] = whitener_t
    offset_out[...] = offset[:, :channels]
    grad = through(pack[base : base + count], backward)
    grad = grad - through(pack[base + count :], whitener)
    wide_grad = grad - (offset[:1, channels:] - target_offset[:1])
    grad = wide_grad.astype(BF16)
    grad_out[...] = grad
    weight_terms(columns, share, taps, grad, keep_out, send_out, wide, terms)


def white_kernel(pack, whitener, offset, whitened_out):
    count = whitened_out.shape[0]
    hidden = pack[pack.shape[0] - 2 * count : pack.shape[0] - count]
    whitened_out[...] = (through(hidden, whitener[...]) - offset[0:1]).astype(BF16)


def turn_kernel(own, even, odd, even_rows, odd_rows, hidden, target, pack_out, ends):
    rows, columns, channels = own.shape
    count = rows * columns
    base = 3 * (rows + 2) * channels
    gather_rows(even_rows, odd_rows, ends)
    pack_out[base : base + count] = hidden[...]
    pack_out[base + count : base + 2 * count] = target[...]
    odd_row = lax.axis_index("c")
    odd_plane = lax.rem(lax.axis_index("z"), 2)

    def turn(tap_z, plane, edge):
        for source in range(-1, rows + 1):
            if source < 0:
                tile = ends[1 - odd_row, edge]
            elif source == rows:
                tile = ends[odd_row, edge]
            else:
                tile = plane[source]
            first = (tap_z * (rows + 2) + source + 1) * channels
            pack_out[first : first + channels] = tile.T

    turn(1, own, 0)
    for parity in range(2):

        @pl.when(odd_plane == parity)
        def _():
            below, above = ((odd, 2), (even, 1))[:: 1 - 2 * parity]
            turn(0, *below)
            turn(2, *above)


def place_turned(columns, pack, taps):
    rows_all, count = taps.shape
    channels, rows = rows_all // 9, count // columns
    for tap_z in range(3):
        for tap_y in range(3):
            slot = tap_z * 3 + tap_y
            for row in range(rows):
                first = (tap_z * (rows + 2) + row + tap_y) * channels
                taps[
                    slot * channels : (slot + 1) * channels, row * columns : (row + 1) * columns
                ] = pack[first : first + channels]


def weight_terms(columns, share, taps, grad, keep_out, send_out, wide, terms):
    _, channels = grad.shape
    value = grad.astype(F32)
    wide[:, :channels] = moved_columns(value, -1, columns).astype(BF16)
    wide[:, channels : 2 * channels] = grad
    wide[:, 2 * channels :] = moved_columns(value, 1, columns).astype(BF16)
    pairs = channels // share // 2
    taps_each = keep_out.shape[1] // share
    terms[...] = jnp.dot(taps[...], wide[...], preferred_element_type=F32)
    mine = pl.multiple_of(lax.axis_index("c") * share, share)
    others = pl.multiple_of((1 - lax.axis_index("c")) * share, share)
    for tap in range(keep_out.shape[0] // pairs * taps_each):
        slot, tap_x = tap // 3, tap % 3
        cols = slice(tap_x * channels, (tap_x + 1) * channels)
        place = slice(tap % taps_each * share, (tap % taps_each + 1) * share)
        for pair in range(pairs):
            group = tap // taps_each * pairs + pair
            base = slot * channels + pair * 2 * share
            if tap < 27:
                keep_out[group, place, :] = terms[pl.ds(base + mine, share), cols]
                send_out[group, place, :] = terms[pl.ds(base + others, share), cols].astype(BF16)
            else:
                keep_out[group, place, :] = jnp.zeros((share, channels), F32)
                send_out[group, place, :] = jnp.zeros((share, channels), BF16)


def pair_kernel(kept, received, sum_out):
    sum_out[...] = (kept[...] + received[...].astype(F32)).astype(BF16)


def input_kernel(
    own, even, odd, even_rows, odd_rows, weight, grad_out, wide, ends, kernel_wide
):
    rows, columns, channels = own.shape
    gather_rows(even_rows, odd_rows, ends)
    place_all(wide, (own, (ends, 0)), (even, (ends, 1)), (odd, (ends, 2)), True)
    for slot in range(9):
        for tap_x in range(3):
            kernel_wide[
                tap_x * channels : (tap_x + 1) * channels,
                slot * channels : (slot + 1) * channels,
            ] = weight[slot * 3 + tap_x]
    flat = wide[...].reshape(rows * columns, 9 * channels)
    product = lax.dot_general(
        flat, kernel_wide[...], (((1,), (1,)), ((), ())), preferred_element_type=F32
    )
    total = product[:, channels : 2 * channels]
    total = total + moved_columns(product[:, :channels], -1, columns)
    total = total + moved_columns(product[:, 2 * channels :], 1, columns)
    grad_out[...] = total.astype(BF16)


def total_kernel(scale, parts, copies_out):
    total = parts[0].astype(F32)
    for i in range(1, parts.shape[0]):
        total = total + parts[i].astype(F32)
    total = (total * scale if scale != 1.0 else total).astype(copies_out.dtype)
    for i in range(copies_out.shape[0]):
        copies_out[i] = total


def exchange(parts, axes):
    return lax.all_to_all(parts, axes, 0, 0, tiled=True)


def total_copies(parts, count, dtype, scale=1.0):
    shape = jax.ShapeDtypeStruct((count,) + parts.shape[1:], dtype)
    return call(
        lambda *refs: total_kernel(scale, *refs), shape, [], parts.size, 2 * parts.size, parts
    )


def local(volume, conv_weight, target):
    _, rows, columns, channels = volume.shape
    count = rows * columns
    voxels = count * lax.axis_size(GZ) * lax.axis_size(GY)
    spread = lax.axis_size(SPREAD)
    levels = lax.axis_size("z")
    rows_y = lax.axis_size("y")
    share = channels // lax.axis_size(GY)
    taps_each = -(-27 // rows_y)
    flops = 2 * count * 27 * channels * channels
    weight = conv_weight.reshape(27, channels, channels)
    target_flat = target.reshape(count, channels)

    block = volume.reshape(rows, columns, channels)
    even, odd = plane_swaps(block)
    near, kernel_wide, target_near = call(
        ready_kernel,
        [
            jax.ShapeDtypeStruct(block.shape, BF16),
            jax.ShapeDtypeStruct((9 * channels, 3 * channels), BF16),
            jax.ShapeDtypeStruct((count, channels), BF16),
        ],
        [pltpu.SemaphoreType.DMA((29,))],
        0, 2**20, block, weight, target_flat, far=(0, 1, 2),
    )
    planes = [near, even, odd, *row_swaps(near, even, odd)]
    ends = pltpu.VMEM((2, 3, columns, channels), BF16)
    wide = pltpu.VMEM((rows, columns, 9 * channels), BF16)
    hidden, sheet = call(
        conv_kernel,
        [
            jax.ShapeDtypeStruct((count, channels), BF16),
            jax.ShapeDtypeStruct((spread, 2 * G // spread + 1, channels), F32),
        ],
        [wide, ends],
        flops, 3 * 2**20, *planes, kernel_wide, target_near,
    )
    flat = jax.ShapeDtypeStruct((count, channels), BF16)
    pack = call(
        turn_kernel,
        jax.ShapeDtypeStruct((3 * (rows + 2) * channels + 2 * count, channels), BF16),
        [ends], 0, 3 * 2**20, *planes, hidden, target_near,
    )

    mine = total_copies(exchange(sheet, SPREAD), levels, F32)
    mine = total_copies(exchange(mine, ("z",)), spread, F32)
    sheet = exchange(mine, SPREAD)
    groups = spread // 2
    shape = (groups, taps_each * share, channels)
    grad_hidden, keep, send, whitener, offset = call(
        lambda *refs: grad_kernel(voxels, columns, share, *refs),
        [
            flat,
            jax.ShapeDtypeStruct(shape, F32),
            jax.ShapeDtypeStruct(shape, BF16),
            jax.ShapeDtypeStruct((channels, channels), F32),
            jax.ShapeDtypeStruct((8, channels), F32),
        ],
        [
            pltpu.VMEM((2 * G, channels), F32),
            pltpu.VMEM((count, 3 * channels), BF16),
            pltpu.VMEM((9 * channels, 3 * channels), F32),
            pltpu.VMEM((9 * channels, count), BF16),
        ],
        flops, 2**20, sheet, pack,
    )
    received = lax.ppermute(send, ("c",), [(0, 1), (1, 0)])
    parts = call(
        pair_kernel, jax.ShapeDtypeStruct(shape, BF16), [], keep.size, 2**21, keep, received
    )
    block, whitener, parts = lax.optimization_barrier(
        (grad_hidden.reshape(rows, columns, channels), whitener, parts)
    )
    whitened = call(white_kernel, flat, [], flops, 2**20, pack, whitener, offset)
    even, odd = plane_swaps(block)
    part = total_copies(exchange(parts, ("y", "x")), levels, BF16)
    part, even, odd, whitened = lax.optimization_barrier((part, even, odd, whitened))
    row_ends = row_swaps(block, even, odd)
    part = total_copies(exchange(part, ("z",)), rows_y, BF16, 1.0 / math.sqrt(voxels))
    part, *row_ends = lax.optimization_barrier((part, *row_ends))
    whole = exchange(part, ("y",))
    weight_grad = whole.reshape(rows_y * taps_each, share, channels)[:27].astype(F32)
    weight_grad = weight_grad.reshape(3, 3, 3, share, channels)

    planes = [block, even, odd, *row_ends]
    input_grad = call(
        input_kernel,
        jax.ShapeDtypeStruct((count, channels), BF16),
        [wide, ends, pltpu.VMEM((3 * channels, 9 * channels), BF16)],
        flops, 3 * 2**20, *planes, weight,
    )
    return (whitened.reshape(volume.shape), input_grad.reshape(volume.shape), weight_grad)


def solution(mesh):
    cells = mesh.devices.reshape(4, 8, 4, 2)
    split = Mesh(cells, ("y", "z", "x", "c"))
    in_specs = (P(GZ, GY, None, None), P(), P(GZ, GY, None, None))
    out_specs = (
        P(GZ, GY, None, None),
        P(GZ, GY, None, None),
        P(None, None, None, GY, None),
    )
    return jax.shard_map(local, mesh=split, in_specs=in_specs, out_specs=out_specs, check_vma=False)
```

```python
import math

import jax
import jax.numpy as jnp
from jax import lax
from jax.experimental import pallas as pl
from jax.experimental.pallas import tpu as pltpu
from jax.sharding import Mesh, PartitionSpec as P

G = 64
NEWTON = 5
EPSILON = 1e-05
HIGHEST = lax.Precision.HIGHEST
F32 = jnp.float32
BF16 = jnp.bfloat16
GZ = ("y", "z")
GY = ("x", "c")
SPREAD = ("y", "x", "c")
VMEM_BYTES = 12 * 1024 * 1024


def swapped(block, axes, count, first):
    pairs = []
    for i in range(first, count - 1, 2):
        pairs += [(i, i + 1), (i + 1, i)]
    return lax.ppermute(block, axes, pairs)


def ends_kernel(own, even, odd, first_out, second_out):
    last = own.shape[0] - 1
    odd_row = lax.axis_index("c")
    for place, plane in enumerate((own, even, odd)):
        first_out[place : place + 1] = plane[pl.ds((1 - odd_row) * last, 1)]
        second_out[place : place + 1] = plane[pl.ds(odd_row * last, 1)]


def row_swaps(own, even, odd):
    ny = lax.axis_size(GY)
    ends = jax.ShapeDtypeStruct((3,) + own.shape[1:], BF16)
    first, second = call(ends_kernel, [ends, ends], [], 0, 2**18, own, even, odd)
    return swapped(first, GY, ny, 0), swapped(second, GY, ny, 1)


def plane_swaps(block):
    nz = lax.axis_size(GZ)
    return swapped(block, GZ, nz, 0), swapped(block, GZ, nz, 1)


def call(kernel, out_shape, scratch, flops, moved, *operands, far=()):
    vmem = pl.BlockSpec(memory_space=pltpu.VMEM)
    hbm = pl.BlockSpec(memory_space=pltpu.HBM)
    many = isinstance(out_shape, (list, tuple))
    return pl.pallas_call(
        kernel,
        out_shape=out_shape,
        in_specs=[hbm if i in far else vmem for i in range(len(operands))],
        out_specs=[vmem] * len(out_shape) if many else vmem,
        scratch_shapes=scratch,
        compiler_params=pltpu.CompilerParams(vmem_limit_bytes=VMEM_BYTES),
        cost_estimate=pl.CostEstimate(flops=flops, bytes_accessed=moved, transcendentals=0),
    )(*operands)


def place_rows(wide, slot, plane, edge, tap_y):
    rows, _, channels = plane.shape
    cols = slice(slot * channels, (slot + 1) * channels)
    odd_row = lax.axis_index("c")
    if tap_y == 0:
        wide[0:1, :, cols] = edge[0][pl.ds(1 - odd_row, 1), edge[1]]
        wide[1:rows, :, cols] = plane[0 : rows - 1]
    elif tap_y == 1:
        wide[:, :, cols] = plane[...]
    else:
        wide[0 : rows - 1, :, cols] = plane[1:rows]
        wide[rows - 1 : rows, :, cols] = edge[0][pl.ds(odd_row, 1), edge[1]]


def gather_rows(even_rows, odd_rows, ends):
    ends[0] = even_rows[...]
    ends[1] = odd_rows[...]


def place_all(wide, own, even, odd, flip):
    odd_plane = lax.rem(lax.axis_index("z"), 2)

    order = range(3)
    for tap_z in order:
        for tap_y in order:
            slot = tap_z * 3 + tap_y
            step_z, step_y = (2 - tap_z, 2 - tap_y) if flip else (tap_z, tap_y)
            if step_z == 1:
                place_rows(wide, slot, own[0], own[1], step_y)
    for parity in range(2):

        @pl.when(odd_plane == parity)
        def _():
            below, above = (odd, even) if parity == 0 else (even, odd)
            for tap_z in order:
                for tap_y in order:
                    slot = tap_z * 3 + tap_y
                    step_z, step_y = (2 - tap_z, 2 - tap_y) if flip else (tap_z, tap_y)
                    if step_z != 1:
                        piece = below if step_z == 0 else above
                        place_rows(wide, slot, piece[0], piece[1], step_y)


def moved_columns(flat, step, columns):
    count = flat.shape[0]
    column = lax.broadcasted_iota(jnp.int32, flat.shape, 0) % columns
    if step == 1:
        return jnp.where(column == 0, 0.0, pltpu.roll(flat, 1, 0))
    return jnp.where(column == columns - 1, 0.0, pltpu.roll(flat, count - 1, 0))


def over_rows(left, right):
    return lax.dot_general(left, right, (((0,), (0,)), ((), ())), preferred_element_type=F32)


def ready_kernel(block, weight, target, block_out, wide_out, target_out, sems):
    _, channels, _ = weight.shape
    moves = [
        pltpu.make_async_copy(block, block_out, sems.at[27]),
        pltpu.make_async_copy(target, target_out, sems.at[28]),
    ]
    for tap in range(27):
        slot, tap_x = tap // 3, tap % 3
        place = wide_out.at[
            slot * channels : (slot + 1) * channels, tap_x * channels : (tap_x + 1) * channels
        ]
        moves.append(pltpu.make_async_copy(weight.at[tap], place, sems.at[tap]))
    for move in moves:
        move.start()
    for move in moves:
        move.wait()


def with_shifts(product, columns):
    channels = product.shape[1] // 3
    total = product[:, channels : 2 * channels]
    total = total + moved_columns(product[:, :channels], 1, columns)
    return total + moved_columns(product[:, 2 * channels :], -1, columns)


def moments(hidden, features):
    second = over_rows(hidden, hidden)
    cross = over_rows(features, hidden)
    first = lax.broadcasted_iota(jnp.int32, (G, hidden.shape[1]), 1) < G
    second = jnp.where(first, second[:G], second[G:])
    return second, jnp.where(first, cross[:G], cross[G:])


def conv_kernel(
    own, even, odd, kernel_wide, target,
    hidden_out, ends_out, moments_out, sums_out, wide, none,
):
    rows, columns, channels = own.shape
    none[...] = jnp.zeros(none.shape, BF16)
    place_all(wide, (own, (none, 0)), (even, (none, 0)), (odd, (none, 0)), False)
    flat = wide[...].reshape(rows * columns, 9 * channels)
    product = jnp.dot(flat, kernel_wide[...], preferred_element_type=F32)
    total = with_shifts(product, columns)
    ends_out[:columns] = total[:columns]
    ends_out[columns:] = total[-columns:]
    hidden = total.astype(BF16)
    hidden_out[...] = hidden
    inner = hidden[columns:-columns]
    moments_out[:G], moments_out[G:] = moments(inner, target[columns:-columns])
    sums_out[0:1] = jnp.sum(inner.astype(F32), axis=0, keepdims=True)
    sums_out[1:2] = jnp.sum(target[...].astype(F32), axis=0, keepdims=True)
    sums_out[2:] = jnp.zeros((sums_out.shape[0] - 2, channels), F32)


def finish_kernel(
    totals, even_rows, odd_rows, kernel_wide, target, moments_in, sums,
    hidden_out, sheet_out, ends,
):
    _, columns, channels = even_rows.shape
    gather_rows(even_rows, odd_rows, ends)
    odd_row = lax.axis_index("c")
    odd_plane = lax.rem(lax.axis_index("z"), 2)
    order = (2 - odd_plane, 0, 1 + odd_plane)

    def part(side, tap_y):
        tiles = [ends[side, place] for place in order]
        taps = [(tap_z * 3 + tap_y) * channels for tap_z in range(3)]
        kernel = [kernel_wide[tap : tap + channels, :] for tap in taps]
        product = jnp.dot(
            jnp.concatenate(tiles, axis=1),
            jnp.concatenate(kernel, axis=0),
            preferred_element_type=F32,
        )
        return with_shifts(product, columns)

    total = totals[...] + jnp.concatenate([part(1 - odd_row, 0), part(odd_row, 2)], axis=0)
    hidden = total.astype(BF16)
    hidden_out[...] = hidden
    features = jnp.concatenate([target[:columns], target[target.shape[0] - columns :]], axis=0)
    second, cross = moments(hidden, features)
    second, cross = second + moments_in[:G], cross + moments_in[G:]
    spread, depth, _ = sheet_out.shape
    each = depth - 1
    half = spread // 2
    for j in range(half):
        sheet_out[j, 0:each, :] = second[each * j : each * (j + 1)]
        sheet_out[half + j, 0:each, :] = cross[each * j : each * (j + 1)]
    for j in range(2, spread):
        sheet_out[j, each:depth, :] = jnp.zeros((1, channels), F32)
    hidden_sum = jnp.sum(hidden.astype(F32), axis=0, keepdims=True)
    sheet_out[0, each:depth, :] = sums[0:1] + hidden_sum
    sheet_out[1, each:depth, :] = sums[1:2]


def thirds(value):
    high = value.astype(BF16)
    rest = value - high.astype(F32)
    middle = rest.astype(BF16)
    return high, middle, (rest - middle.astype(F32)).astype(BF16)


def left_terms(value):
    high, middle, low = thirds(value)
    return jnp.concatenate([low, high, middle, middle, high, high], axis=1)


def right_terms(value):
    high, middle, low = thirds(value)
    return jnp.concatenate([high, low, middle, high, middle, high], axis=0)


def exact(left, *rights):
    if len(rights) == 1:
        right = right_terms(rights[0])
    else:
        right = jnp.concatenate([right_terms(value) for value in rights], axis=1)
    return jnp.dot(left_terms(left), right, preferred_element_type=F32)


def through(values, matrix):
    high, middle, low = thirds(matrix)
    total = jnp.dot(values, low, preferred_element_type=F32)
    total = total + jnp.dot(values, middle, preferred_element_type=F32)
    return total + jnp.dot(values, high, preferred_element_type=F32)


def grad_kernel(
    voxels, columns, share, sheet, pack,
    grad_out, keep_out, send_out, whitener_out, offset_out,
    mats, wide, terms, taps,
):
    place_turned(columns, pack, taps)
    count = taps.shape[1]
    base = pack.shape[0] - 2 * count
    spread, depth, channels = sheet.shape
    each = depth - 1
    for j in range(spread):
        mats[each * j : each * (j + 1), :] = sheet[j, 0:each, :]
    row = lax.broadcasted_iota(jnp.int32, (channels, channels), 0)
    col = lax.broadcasted_iota(jnp.int32, (channels, channels), 1)
    same = (row < G) == (col < G)
    diagonal = row == col
    low_lane = lax.broadcasted_iota(jnp.int32, (1, channels), 1) < G

    def group_sums(value):
        line = jnp.sum(value, axis=0, keepdims=True)
        low = jnp.sum(jnp.where(low_lane, line, 0.0), axis=1, keepdims=True)
        high = jnp.sum(jnp.where(low_lane, 0.0, line), axis=1, keepdims=True)
        return jnp.where(low_lane, low, high)

    second = jnp.concatenate([mats[:G], mats[:G]], axis=0)
    cross = jnp.concatenate([mats[G:], mats[G:]], axis=0)
    mean = sheet[0, each:depth, :] / voxels
    target_sum = sheet[1, each:depth, :]
    mean_rows = jnp.broadcast_to(mean, (channels, channels))
    mean_cols = mean_rows.T
    target_cols = jnp.broadcast_to(target_sum, (channels, channels)).T
    second = jnp.where(same, second - voxels * (mean_cols * mean_rows), 0.0)
    cross = jnp.where(same, cross - target_cols * mean_rows, 0.0)
    covariance = second / voxels + jnp.where(diagonal, EPSILON, 0.0)
    trace = group_sums(jnp.where(diagonal, covariance, 0.0))
    scaled = covariance / trace
    root = jnp.sqrt(trace)

    direction = cross / root
    iterate = jnp.where(diagonal, 1.5, 0.0) - 0.5 * scaled
    change = -0.5 * direction
    slope = jnp.where(diagonal, -0.5, 0.0)

    def column(value, i):
        return value[:, i * channels : (i + 1) * channels]

    for sweep in range(1, NEWTON):
        first = exact(iterate, iterate, scaled, change, direction)
        squared, once = column(first, 0), column(first, 1)
        crossed = exact(change, iterate, scaled)
        steep = exact(slope, scaled)
        second_level = exact(squared, once, column(first, 3) + column(crossed, 1), steep, iterate)
        moved = column(second_level, 1) + exact(column(first, 2) + column(crossed, 0), once)
        change = 1.5 * change - 0.5 * moved
        slope = 1.5 * slope - 0.5 * (3.0 * column(second_level, 2) + column(second_level, 3))
        iterate = 1.5 * iterate - 0.5 * column(second_level, 0)
    whitener = iterate / root
    whitener_t = whitener.T
    aligned = exact(whitener, second)
    white_grad = aligned - cross
    change = exact(slope, aligned) / root - change
    trace_grad = -0.5 * group_sums(white_grad * whitener) / trace
    trace_grad = trace_grad - group_sums(change * scaled) / trace
    sigma_grad = change / trace + jnp.where(diagonal, trace_grad, 0.0)
    symmetric = (sigma_grad + sigma_grad.T) / voxels
    backward = (exact(whitener_t, whitener) + symmetric).T

    offset = exact(jnp.broadcast_to(mean, (8, channels)), whitener_t, backward)
    target_offset = exact(jnp.broadcast_to(target_sum / voxels, (8, channels)), whitener)
    whitener_out[...] = whitener_t
    offset_out[...] = offset[:, :channels]
    grad = through(pack[base : base + count], backward)
    grad = grad - through(pack[base + count :], whitener)
    wide_grad = grad - (offset[:1, channels:] - target_offset[:1])
    grad = wide_grad.astype(BF16)
    grad_out[...] = grad
    weight_terms(columns, share, taps, grad, keep_out, send_out, wide, terms)


def white_kernel(pack, whitener, offset, whitened_out):
    count = whitened_out.shape[0]
    hidden = pack[pack.shape[0] - 2 * count : pack.shape[0] - count]
    whitened_out[...] = (through(hidden, whitener[...]) - offset[0:1]).astype(BF16)


def turn_kernel(
    own, even, odd, even_rows, odd_rows, hidden, hidden_ends, target, pack_out, ends
):
    rows, columns, channels = own.shape
    count = rows * columns
    base = 3 * (rows + 2) * channels
    gather_rows(even_rows, odd_rows, ends)
    pack_out[base : base + columns] = hidden_ends[:columns]
    pack_out[base + columns : base + count - columns] = hidden[columns : count - columns]
    pack_out[base + count - columns : base + count] = hidden_ends[columns:]
    pack_out[base + count : base + 2 * count] = target[...]
    odd_row = lax.axis_index("c")
    odd_plane = lax.rem(lax.axis_index("z"), 2)

    def turn(tap_z, plane, edge):
        for source in range(-1, rows + 1):
            if source < 0:
                tile = ends[1 - odd_row, edge]
            elif source == rows:
                tile = ends[odd_row, edge]
            else:
                tile = plane[source]
            first = (tap_z * (rows + 2) + source + 1) * channels
            pack_out[first : first + channels] = tile.T

    turn(1, own, 0)
    for parity in range(2):

        @pl.when(odd_plane == parity)
        def _():
            below, above = ((odd, 2), (even, 1))[:: 1 - 2 * parity]
            turn(0, *below)
            turn(2, *above)


def place_turned(columns, pack, taps):
    rows_all, count = taps.shape
    channels, rows = rows_all // 9, count // columns
    for tap_z in range(3):
        for tap_y in range(3):
            slot = tap_z * 3 + tap_y
            for row in range(rows):
                first = (tap_z * (rows + 2) + row + tap_y) * channels
                taps[
                    slot * channels : (slot + 1) * channels, row * columns : (row + 1) * columns
                ] = pack[first : first + channels]


def weight_terms(columns, share, taps, grad, keep_out, send_out, wide, terms):
    _, channels = grad.shape
    value = grad.astype(F32)
    wide[:, :channels] = moved_columns(value, -1, columns).astype(BF16)
    wide[:, channels : 2 * channels] = grad
    wide[:, 2 * channels :] = moved_columns(value, 1, columns).astype(BF16)
    pairs = channels // share // 2
    taps_each = keep_out.shape[1] // share
    terms[...] = jnp.dot(taps[...], wide[...], preferred_element_type=F32)
    mine = pl.multiple_of(lax.axis_index("c") * share, share)
    others = pl.multiple_of((1 - lax.axis_index("c")) * share, share)
    for tap in range(keep_out.shape[0] // pairs * taps_each):
        slot, tap_x = tap // 3, tap % 3
        cols = slice(tap_x * channels, (tap_x + 1) * channels)
        place = slice(tap % taps_each * share, (tap % taps_each + 1) * share)
        for pair in range(pairs):
            group = tap // taps_each * pairs + pair
            base = slot * channels + pair * 2 * share
            if tap < 27:
                keep_out[group, place, :] = terms[pl.ds(base + mine, share), cols]
                send_out[group, place, :] = terms[pl.ds(base + others, share), cols].astype(BF16)
            else:
                keep_out[group, place, :] = jnp.zeros((share, channels), F32)
                send_out[group, place, :] = jnp.zeros((share, channels), BF16)


def pair_kernel(kept, received, sum_out):
    sum_out[...] = (kept[...] + received[...].astype(F32)).astype(BF16)


def input_kernel(
    own, even, odd, even_rows, odd_rows, weight, grad_out, wide, ends, kernel_wide
):
    rows, columns, channels = own.shape
    gather_rows(even_rows, odd_rows, ends)
    place_all(wide, (own, (ends, 0)), (even, (ends, 1)), (odd, (ends, 2)), True)
    for slot in range(9):
        for tap_x in range(3):
            kernel_wide[
                tap_x * channels : (tap_x + 1) * channels,
                slot * channels : (slot + 1) * channels,
            ] = weight[slot * 3 + tap_x]
    flat = wide[...].reshape(rows * columns, 9 * channels)
    product = lax.dot_general(
        flat, kernel_wide[...], (((1,), (1,)), ((), ())), preferred_element_type=F32
    )
    total = product[:, channels : 2 * channels]
    total = total + moved_columns(product[:, :channels], -1, columns)
    total = total + moved_columns(product[:, 2 * channels :], 1, columns)
    grad_out[...] = total.astype(BF16)


def total_kernel(scale, parts, copies_out):
    total = parts[0].astype(F32)
    for i in range(1, parts.shape[0]):
        total = total + parts[i].astype(F32)
    total = (total * scale if scale != 1.0 else total).astype(copies_out.dtype)
    for i in range(copies_out.shape[0]):
        copies_out[i] = total


def exchange(parts, axes):
    return lax.all_to_all(parts, axes, 0, 0, tiled=True)


def total_copies(parts, count, dtype, scale=1.0):
    shape = jax.ShapeDtypeStruct((count,) + parts.shape[1:], dtype)
    return call(
        lambda *refs: total_kernel(scale, *refs), shape, [], parts.size, 2 * parts.size, parts
    )


def local(volume, conv_weight, target):
    _, rows, columns, channels = volume.shape
    count = rows * columns
    voxels = count * lax.axis_size(GZ) * lax.axis_size(GY)
    spread = lax.axis_size(SPREAD)
    levels = lax.axis_size("z")
    rows_y = lax.axis_size("y")
    share = channels // lax.axis_size(GY)
    taps_each = -(-27 // rows_y)
    flops = 2 * count * 27 * channels * channels
    weight = conv_weight.reshape(27, channels, channels)
    target_flat = target.reshape(count, channels)

    block = volume.reshape(rows, columns, channels)
    even, odd = plane_swaps(block)
    near, kernel_wide, target_near = call(
        ready_kernel,
        [
            jax.ShapeDtypeStruct(block.shape, BF16),
            jax.ShapeDtypeStruct((9 * channels, 3 * channels), BF16),
            jax.ShapeDtypeStruct((count, channels), BF16),
        ],
        [pltpu.SemaphoreType.DMA((29,))],
        0, 2**20, block, weight, target_flat, far=(0, 1, 2),
    )
    even_rows, odd_rows = row_swaps(near, even, odd)
    ends = pltpu.VMEM((2, 3, columns, channels), BF16)
    wide = pltpu.VMEM((rows, columns, 9 * channels), BF16)
    hidden, totals, moments_here, sums_here = call(
        conv_kernel,
        [
            jax.ShapeDtypeStruct((count, channels), BF16),
            jax.ShapeDtypeStruct((2 * columns, channels), F32),
            jax.ShapeDtypeStruct((2 * G, channels), F32),
            jax.ShapeDtypeStruct((8, channels), F32),
        ],
        [wide, pltpu.VMEM((2, 1, columns, channels), BF16)],
        flops, 3 * 2**20, near, even, odd, kernel_wide, target_near,
    )
    hidden_ends, sheet = call(
        finish_kernel,
        [
            jax.ShapeDtypeStruct((2 * columns, channels), BF16),
            jax.ShapeDtypeStruct((spread, 2 * G // spread + 1, channels), F32),
        ],
        [ends],
        flops // 12, 2**20,
        totals, even_rows, odd_rows, kernel_wide, target_near, moments_here, sums_here,
    )
    flat = jax.ShapeDtypeStruct((count, channels), BF16)
    pack = call(
        turn_kernel,
        jax.ShapeDtypeStruct((3 * (rows + 2) * channels + 2 * count, channels), BF16),
        [ends], 0, 3 * 2**20, near, even, odd, even_rows, odd_rows, hidden, hidden_ends, target_near,
    )

    mine = total_copies(exchange(sheet, SPREAD), levels, F32)
    mine = total_copies(exchange(mine, ("z",)), spread, F32)
    sheet = exchange(mine, SPREAD)
    groups = spread // 2
    shape = (groups, taps_each * share, channels)
    grad_hidden, keep, send, whitener, offset = call(
        lambda *refs: grad_kernel(voxels, columns, share, *refs),
        [
            flat,
            jax.ShapeDtypeStruct(shape, F32),
            jax.ShapeDtypeStruct(shape, BF16),
            jax.ShapeDtypeStruct((channels, channels), F32),
            jax.ShapeDtypeStruct((8, channels), F32),
        ],
        [
            pltpu.VMEM((2 * G, channels), F32),
            pltpu.VMEM((count, 3 * channels), BF16),
            pltpu.VMEM((9 * channels, 3 * channels), F32),
            pltpu.VMEM((9 * channels, count), BF16),
        ],
        flops, 2**20, sheet, pack,
    )
    received = lax.ppermute(send, ("c",), [(0, 1), (1, 0)])
    parts = call(
        pair_kernel, jax.ShapeDtypeStruct(shape, BF16), [], keep.size, 2**21, keep, received
    )
    block, whitener, parts = lax.optimization_barrier(
        (grad_hidden.reshape(rows, columns, channels), whitener, parts)
    )
    whitened = call(white_kernel, flat, [], flops, 2**20, pack, whitener, offset)
    even, odd = plane_swaps(block)
    part = total_copies(exchange(parts, ("y", "x")), levels, BF16)
    part, even, odd, whitened = lax.optimization_barrier((part, even, odd, whitened))
    row_ends = row_swaps(block, even, odd)
    part = total_copies(exchange(part, ("z",)), rows_y, BF16, 1.0 / math.sqrt(voxels))
    part, *row_ends = lax.optimization_barrier((part, *row_ends))
    whole = exchange(part, ("y",))
    weight_grad = whole.reshape(rows_y * taps_each, share, channels)[:27].astype(F32)
    weight_grad = weight_grad.reshape(3, 3, 3, share, channels)

    planes = [block, even, odd, *row_ends]
    input_grad = call(
        input_kernel,
        jax.ShapeDtypeStruct((count, channels), BF16),
        [wide, ends, pltpu.VMEM((3 * channels, 9 * channels), BF16)],
        flops, 3 * 2**20, *planes, weight,
    )
    return (whitened.reshape(volume.shape), input_grad.reshape(volume.shape), weight_grad)


def solution(mesh):
    cells = mesh.devices.reshape(4, 8, 4, 2)
    split = Mesh(cells, ("y", "z", "x", "c"))
    in_specs = (P(GZ, GY, None, None), P(), P(GZ, GY, None, None))
    out_specs = (
        P(GZ, GY, None, None),
        P(GZ, GY, None, None),
        P(None, None, None, GY, None),
    )
    return jax.shard_map(local, mesh=split, in_specs=in_specs, out_specs=out_specs, check_vma=False)
```

```python
import math

import jax
import jax.numpy as jnp
from jax import lax
from jax.experimental import pallas as pl
from jax.experimental.pallas import tpu as pltpu
from jax.sharding import Mesh, PartitionSpec as P

G = 64
NEWTON = 5
EPSILON = 1e-05
HIGHEST = lax.Precision.HIGHEST
F32 = jnp.float32
BF16 = jnp.bfloat16
GZ = ("y", "z")
GY = ("x", "c")
SPREAD = ("y", "x", "c")
VMEM_BYTES = 12 * 1024 * 1024


def swapped(block, axes, count, first):
    pairs = []
    for i in range(first, count - 1, 2):
        pairs += [(i, i + 1), (i + 1, i)]
    return lax.ppermute(block, axes, pairs)


def ends_kernel(own, even, odd, first_out, second_out):
    last = own.shape[0] - 1
    odd_row = lax.axis_index("c")
    for place, plane in enumerate((own, even, odd)):
        first_out[place : place + 1] = plane[pl.ds((1 - odd_row) * last, 1)]
        second_out[place : place + 1] = plane[pl.ds(odd_row * last, 1)]


def row_swaps(own, even, odd):
    ny = lax.axis_size(GY)
    ends = jax.ShapeDtypeStruct((3,) + own.shape[1:], BF16)
    first, second = call(ends_kernel, [ends, ends], [], 24 * 2**30, 2**18, own, even, odd)
    return swapped(first, GY, ny, 0), swapped(second, GY, ny, 1)


def plane_swaps(block):
    nz = lax.axis_size(GZ)
    return swapped(block, GZ, nz, 0), swapped(block, GZ, nz, 1)


def call(kernel, out_shape, scratch, flops, moved, *operands, far=()):
    vmem = pl.BlockSpec(memory_space=pltpu.VMEM)
    hbm = pl.BlockSpec(memory_space=pltpu.HBM)
    many = isinstance(out_shape, (list, tuple))
    return pl.pallas_call(
        kernel,
        out_shape=out_shape,
        in_specs=[hbm if i in far else vmem for i in range(len(operands))],
        out_specs=[vmem] * len(out_shape) if many else vmem,
        scratch_shapes=scratch,
        compiler_params=pltpu.CompilerParams(vmem_limit_bytes=VMEM_BYTES),
        cost_estimate=pl.CostEstimate(flops=flops, bytes_accessed=moved, transcendentals=0),
    )(*operands)


def place_rows(wide, slot, plane, edge, tap_y):
    rows, _, channels = plane.shape
    cols = slice(slot * channels, (slot + 1) * channels)
    odd_row = lax.axis_index("c")
    if tap_y == 0:
        wide[0:1, :, cols] = edge[0][pl.ds(1 - odd_row, 1), edge[1]]
        wide[1:rows, :, cols] = plane[0 : rows - 1]
    elif tap_y == 1:
        wide[:, :, cols] = plane[...]
    else:
        wide[0 : rows - 1, :, cols] = plane[1:rows]
        wide[rows - 1 : rows, :, cols] = edge[0][pl.ds(odd_row, 1), edge[1]]


def gather_rows(even_rows, odd_rows, ends):
    ends[0] = even_rows[...]
    ends[1] = odd_rows[...]


def place_all(wide, own, even, odd, flip):
    odd_plane = lax.rem(lax.axis_index("z"), 2)

    order = range(3)
    for tap_z in order:
        for tap_y in order:
            slot = tap_z * 3 + tap_y
            step_z, step_y = (2 - tap_z, 2 - tap_y) if flip else (tap_z, tap_y)
            if step_z == 1:
                place_rows(wide, slot, own[0], own[1], step_y)
    for parity in range(2):

        @pl.when(odd_plane == parity)
        def _():
            below, above = (odd, even) if parity == 0 else (even, odd)
            for tap_z in order:
                for tap_y in order:
                    slot = tap_z * 3 + tap_y
                    step_z, step_y = (2 - tap_z, 2 - tap_y) if flip else (tap_z, tap_y)
                    if step_z != 1:
                        piece = below if step_z == 0 else above
                        place_rows(wide, slot, piece[0], piece[1], step_y)


def moved_columns(flat, step, columns):
    count = flat.shape[0]
    column = lax.broadcasted_iota(jnp.int32, flat.shape, 0) % columns
    if step == 1:
        return jnp.where(column == 0, 0.0, pltpu.roll(flat, 1, 0))
    return jnp.where(column == columns - 1, 0.0, pltpu.roll(flat, count - 1, 0))


def over_rows(left, right):
    return lax.dot_general(left, right, (((0,), (0,)), ((), ())), preferred_element_type=F32)


def ready_kernel(block, weight, target, block_out, wide_out, target_out, sems):
    _, channels, _ = weight.shape
    moves = [
        pltpu.make_async_copy(block, block_out, sems.at[27]),
        pltpu.make_async_copy(target, target_out, sems.at[28]),
    ]
    for tap in range(27):
        slot, tap_x = tap // 3, tap % 3
        place = wide_out.at[
            slot * channels : (slot + 1) * channels, tap_x * channels : (tap_x + 1) * channels
        ]
        moves.append(pltpu.make_async_copy(weight.at[tap], place, sems.at[tap]))
    for move in moves:
        move.start()
    for move in moves:
        move.wait()


def with_shifts(product, columns):
    channels = product.shape[1] // 3
    total = product[:, channels : 2 * channels]
    total = total + moved_columns(product[:, :channels], 1, columns)
    return total + moved_columns(product[:, 2 * channels :], -1, columns)


def moments(hidden, features):
    second = over_rows(hidden, hidden)
    cross = over_rows(features, hidden)
    first = lax.broadcasted_iota(jnp.int32, (G, hidden.shape[1]), 1) < G
    second = jnp.where(first, second[:G], second[G:])
    return second, jnp.where(first, cross[:G], cross[G:])


def conv_kernel(
    own, even, odd, kernel_wide, target,
    hidden_out, ends_out, moments_out, sums_out, wide, none,
):
    rows, columns, channels = own.shape
    none[...] = jnp.zeros(none.shape, BF16)
    place_all(wide, (own, (none, 0)), (even, (none, 0)), (odd, (none, 0)), False)
    flat = wide[...].reshape(rows * columns, 9 * channels)
    product = jnp.dot(flat, kernel_wide[...], preferred_element_type=F32)
    total = with_shifts(product, columns)
    ends_out[:columns] = total[:columns]
    ends_out[columns:] = total[-columns:]
    hidden = total.astype(BF16)
    hidden_out[...] = hidden
    inner = hidden[columns:-columns]
    moments_out[:G], moments_out[G:] = moments(inner, target[columns:-columns])
    sums_out[0:1] = jnp.sum(inner.astype(F32), axis=0, keepdims=True)
    sums_out[1:2] = jnp.sum(target[...].astype(F32), axis=0, keepdims=True)
    sums_out[2:] = jnp.zeros((sums_out.shape[0] - 2, channels), F32)


def finish_kernel(
    totals, even_rows, odd_rows, kernel_wide, target, moments_in, sums,
    hidden_out, sheet_out, ends,
):
    _, columns, channels = even_rows.shape
    gather_rows(even_rows, odd_rows, ends)
    odd_row = lax.axis_index("c")
    odd_plane = lax.rem(lax.axis_index("z"), 2)
    order = (2 - odd_plane, 0, 1 + odd_plane)

    def part(side, tap_y):
        tiles = [ends[side, place] for place in order]
        taps = [(tap_z * 3 + tap_y) * channels for tap_z in range(3)]
        kernel = [kernel_wide[tap : tap + channels, :] for tap in taps]
        product = jnp.dot(
            jnp.concatenate(tiles, axis=1),
            jnp.concatenate(kernel, axis=0),
            preferred_element_type=F32,
        )
        return with_shifts(product, columns)

    total = totals[...] + jnp.concatenate([part(1 - odd_row, 0), part(odd_row, 2)], axis=0)
    hidden = total.astype(BF16)
    hidden_out[...] = hidden
    features = jnp.concatenate([target[:columns], target[target.shape[0] - columns :]], axis=0)
    second, cross = moments(hidden, features)
    second, cross = second + moments_in[:G], cross + moments_in[G:]
    spread, depth, _ = sheet_out.shape
    each = depth - 1
    half = spread // 2
    for j in range(half):
        sheet_out[j, 0:each, :] = second[each * j : each * (j + 1)]
        sheet_out[half + j, 0:each, :] = cross[each * j : each * (j + 1)]
    for j in range(2, spread):
        sheet_out[j, each:depth, :] = jnp.zeros((1, channels), F32)
    hidden_sum = jnp.sum(hidden.astype(F32), axis=0, keepdims=True)
    sheet_out[0, each:depth, :] = sums[0:1] + hidden_sum
    sheet_out[1, each:depth, :] = sums[1:2]


def thirds(value):
    high = value.astype(BF16)
    rest = value - high.astype(F32)
    middle = rest.astype(BF16)
    return high, middle, (rest - middle.astype(F32)).astype(BF16)


def left_terms(value):
    high, middle, low = thirds(value)
    return jnp.concatenate([low, high, middle, middle, high, high], axis=1)


def right_terms(value):
    high, middle, low = thirds(value)
    return jnp.concatenate([high, low, middle, high, middle, high], axis=0)


def exact(left, *rights):
    if len(rights) == 1:
        right = right_terms(rights[0])
    else:
        right = jnp.concatenate([right_terms(value) for value in rights], axis=1)
    return jnp.dot(left_terms(left), right, preferred_element_type=F32)


def through(values, matrix):
    high, middle, low = thirds(matrix)
    total = jnp.dot(values, low, preferred_element_type=F32)
    total = total + jnp.dot(values, middle, preferred_element_type=F32)
    return total + jnp.dot(values, high, preferred_element_type=F32)


def grad_kernel(
    voxels, columns, share, sheet, pack,
    grad_out, keep_out, send_out, whitener_out, offset_out,
    mats, wide, terms, taps,
):
    place_turned(columns, pack, taps)
    count = taps.shape[1]
    base = pack.shape[0] - 2 * count
    spread, depth, channels = sheet.shape
    each = depth - 1
    for j in range(spread):
        mats[each * j : each * (j + 1), :] = sheet[j, 0:each, :]
    row = lax.broadcasted_iota(jnp.int32, (channels, channels), 0)
    col = lax.broadcasted_iota(jnp.int32, (channels, channels), 1)
    same = (row < G) == (col < G)
    diagonal = row == col
    low_lane = lax.broadcasted_iota(jnp.int32, (1, channels), 1) < G

    def group_sums(value):
        line = jnp.sum(value, axis=0, keepdims=True)
        low = jnp.sum(jnp.where(low_lane, line, 0.0), axis=1, keepdims=True)
        high = jnp.sum(jnp.where(low_lane, 0.0, line), axis=1, keepdims=True)
        return jnp.where(low_lane, low, high)

    second = jnp.concatenate([mats[:G], mats[:G]], axis=0)
    cross = jnp.concatenate([mats[G:], mats[G:]], axis=0)
    mean = sheet[0, each:depth, :] / voxels
    target_sum = sheet[1, each:depth, :]
    mean_rows = jnp.broadcast_to(mean, (channels, channels))
    mean_cols = mean_rows.T
    target_cols = jnp.broadcast_to(target_sum, (channels, channels)).T
    second = jnp.where(same, second - voxels * (mean_cols * mean_rows), 0.0)
    cross = jnp.where(same, cross - target_cols * mean_rows, 0.0)
    covariance = second / voxels + jnp.where(diagonal, EPSILON, 0.0)
    trace = group_sums(jnp.where(diagonal, covariance, 0.0))
    scaled = covariance / trace
    root = jnp.sqrt(trace)

    direction = cross / root
    iterate = jnp.where(diagonal, 1.5, 0.0) - 0.5 * scaled
    change = -0.5 * direction
    slope = jnp.where(diagonal, -0.5, 0.0)

    def column(value, i):
        return value[:, i * channels : (i + 1) * channels]

    for sweep in range(1, NEWTON):
        first = exact(iterate, iterate, scaled, change, direction)
        squared, once = column(first, 0), column(first, 1)
        crossed = exact(change, iterate, scaled)
        steep = exact(slope, scaled)
        second_level = exact(squared, once, column(first, 3) + column(crossed, 1), steep, iterate)
        moved = column(second_level, 1) + exact(column(first, 2) + column(crossed, 0), once)
        change = 1.5 * change - 0.5 * moved
        slope = 1.5 * slope - 0.5 * (3.0 * column(second_level, 2) + column(second_level, 3))
        iterate = 1.5 * iterate - 0.5 * column(second_level, 0)
    whitener = iterate / root
    whitener_t = whitener.T
    aligned = exact(whitener, second)
    white_grad = aligned - cross
    change = exact(slope, aligned) / root - change
    trace_grad = -0.5 * group_sums(white_grad * whitener) / trace
    trace_grad = trace_grad - group_sums(change * scaled) / trace
    sigma_grad = change / trace + jnp.where(diagonal, trace_grad, 0.0)
    symmetric = (sigma_grad + sigma_grad.T) / voxels
    backward = (exact(whitener_t, whitener) + symmetric).T

    offset = exact(jnp.broadcast_to(mean, (8, channels)), whitener_t, backward)
    target_offset = exact(jnp.broadcast_to(target_sum / voxels, (8, channels)), whitener)
    whitener_out[...] = whitener_t
    offset_out[...] = offset[:, :channels]
    grad = through(pack[base : base + count], backward)
    grad = grad - through(pack[base + count :], whitener)
    wide_grad = grad - (offset[:1, channels:] - target_offset[:1])
    grad = wide_grad.astype(BF16)
    grad_out[...] = grad
    weight_terms(columns, share, taps, grad, keep_out, send_out, wide, terms)


def white_kernel(pack, whitener, offset, whitened_out):
    count = whitened_out.shape[0]
    hidden = pack[pack.shape[0] - 2 * count : pack.shape[0] - count]
    whitened_out[...] = (through(hidden, whitener[...]) - offset[0:1]).astype(BF16)


def turn_kernel(
    own, even, odd, even_rows, odd_rows, hidden, hidden_ends, target, pack_out, ends
):
    rows, columns, channels = own.shape
    count = rows * columns
    base = 3 * (rows + 2) * channels
    gather_rows(even_rows, odd_rows, ends)
    pack_out[base : base + columns] = hidden_ends[:columns]
    pack_out[base + columns : base + count - columns] = hidden[columns : count - columns]
    pack_out[base + count - columns : base + count] = hidden_ends[columns:]
    pack_out[base + count : base + 2 * count] = target[...]
    odd_row = lax.axis_index("c")
    odd_plane = lax.rem(lax.axis_index("z"), 2)

    def turn(tap_z, plane, edge):
        for source in range(-1, rows + 1):
            if source < 0:
                tile = ends[1 - odd_row, edge]
            elif source == rows:
                tile = ends[odd_row, edge]
            else:
                tile = plane[source]
            first = (tap_z * (rows + 2) + source + 1) * channels
            pack_out[first : first + channels] = tile.T

    turn(1, own, 0)
    for parity in range(2):

        @pl.when(odd_plane == parity)
        def _():
            below, above = ((odd, 2), (even, 1))[:: 1 - 2 * parity]
            turn(0, *below)
            turn(2, *above)


def place_turned(columns, pack, taps):
    rows_all, count = taps.shape
    channels, rows = rows_all // 9, count // columns
    for tap_z in range(3):
        for tap_y in range(3):
            slot = tap_z * 3 + tap_y
            for row in range(rows):
                first = (tap_z * (rows + 2) + row + tap_y) * channels
                taps[
                    slot * channels : (slot + 1) * channels, row * columns : (row + 1) * columns
                ] = pack[first : first + channels]


def weight_terms(columns, share, taps, grad, keep_out, send_out, wide, terms):
    _, channels = grad.shape
    value = grad.astype(F32)
    wide[:, :channels] = moved_columns(value, -1, columns).astype(BF16)
    wide[:, channels : 2 * channels] = grad
    wide[:, 2 * channels :] = moved_columns(value, 1, columns).astype(BF16)
    pairs = channels // share // 2
    taps_each = keep_out.shape[1] // share
    terms[...] = jnp.dot(taps[...], wide[...], preferred_element_type=F32)
    mine = pl.multiple_of(lax.axis_index("c") * share, share)
    others = pl.multiple_of((1 - lax.axis_index("c")) * share, share)
    for tap in range(keep_out.shape[0] // pairs * taps_each):
        slot, tap_x = tap // 3, tap % 3
        cols = slice(tap_x * channels, (tap_x + 1) * channels)
        place = slice(tap % taps_each * share, (tap % taps_each + 1) * share)
        for pair in range(pairs):
            group = tap // taps_each * pairs + pair
            base = slot * channels + pair * 2 * share
            if tap < 27:
                keep_out[group, place, :] = terms[pl.ds(base + mine, share), cols]
                send_out[group, place, :] = terms[pl.ds(base + others, share), cols].astype(BF16)
            else:
                keep_out[group, place, :] = jnp.zeros((share, channels), F32)
                send_out[group, place, :] = jnp.zeros((share, channels), BF16)


def pair_kernel(kept, received, sum_out):
    sum_out[...] = (kept[...] + received[...].astype(F32)).astype(BF16)


def input_kernel(
    own, even, odd, even_rows, odd_rows, weight, grad_out, wide, ends, kernel_wide
):
    rows, columns, channels = own.shape
    gather_rows(even_rows, odd_rows, ends)
    place_all(wide, (own, (ends, 0)), (even, (ends, 1)), (odd, (ends, 2)), True)
    for slot in range(9):
        for tap_x in range(3):
            kernel_wide[
                tap_x * channels : (tap_x + 1) * channels,
                slot * channels : (slot + 1) * channels,
            ] = weight[slot * 3 + tap_x]
    flat = wide[...].reshape(rows * columns, 9 * channels)
    product = lax.dot_general(
        flat, kernel_wide[...], (((1,), (1,)), ((), ())), preferred_element_type=F32
    )
    total = product[:, channels : 2 * channels]
    total = total + moved_columns(product[:, :channels], -1, columns)
    total = total + moved_columns(product[:, 2 * channels :], 1, columns)
    grad_out[...] = total.astype(BF16)


def total_kernel(scale, parts, copies_out):
    total = parts[0].astype(F32)
    for i in range(1, parts.shape[0]):
        total = total + parts[i].astype(F32)
    total = (total * scale if scale != 1.0 else total).astype(copies_out.dtype)
    for i in range(copies_out.shape[0]):
        copies_out[i] = total


def exchange(parts, axes):
    return lax.all_to_all(parts, axes, 0, 0, tiled=True)


def total_copies(parts, count, dtype, scale=1.0):
    shape = jax.ShapeDtypeStruct((count,) + parts.shape[1:], dtype)
    return call(
        lambda *refs: total_kernel(scale, *refs), shape, [], parts.size, 2 * parts.size, parts
    )


def local(volume, conv_weight, target):
    _, rows, columns, channels = volume.shape
    count = rows * columns
    voxels = count * lax.axis_size(GZ) * lax.axis_size(GY)
    spread = lax.axis_size(SPREAD)
    levels = lax.axis_size("z")
    rows_y = lax.axis_size("y")
    share = channels // lax.axis_size(GY)
    taps_each = -(-27 // rows_y)
    flops = 2 * count * 27 * channels * channels
    weight = conv_weight.reshape(27, channels, channels)
    target_flat = target.reshape(count, channels)

    block = volume.reshape(rows, columns, channels)
    even, odd = plane_swaps(block)
    near, kernel_wide, target_near = call(
        ready_kernel,
        [
            jax.ShapeDtypeStruct(block.shape, BF16),
            jax.ShapeDtypeStruct((9 * channels, 3 * channels), BF16),
            jax.ShapeDtypeStruct((count, channels), BF16),
        ],
        [pltpu.SemaphoreType.DMA((29,))],
        0, 2**20, block, weight, target_flat, far=(0, 1, 2),
    )
    even_rows, odd_rows = row_swaps(near, even, odd)
    ends = pltpu.VMEM((2, 3, columns, channels), BF16)
    wide = pltpu.VMEM((rows, columns, 9 * channels), BF16)
    hidden, totals, moments_here, sums_here = call(
        conv_kernel,
        [
            jax.ShapeDtypeStruct((count, channels), BF16),
            jax.ShapeDtypeStruct((2 * columns, channels), F32),
            jax.ShapeDtypeStruct((2 * G, channels), F32),
            jax.ShapeDtypeStruct((8, channels), F32),
        ],
        [wide, pltpu.VMEM((2, 1, columns, channels), BF16)],
        flops, 3 * 2**20, near, even, odd, kernel_wide, target_near,
    )
    hidden_ends, sheet = call(
        finish_kernel,
        [
            jax.ShapeDtypeStruct((2 * columns, channels), BF16),
            jax.ShapeDtypeStruct((spread, 2 * G // spread + 1, channels), F32),
        ],
        [ends],
        flops // 12, 2**20,
        totals, even_rows, odd_rows, kernel_wide, target_near, moments_here, sums_here,
    )
    flat = jax.ShapeDtypeStruct((count, channels), BF16)
    pack = call(
        turn_kernel,
        jax.ShapeDtypeStruct((3 * (rows + 2) * channels + 2 * count, channels), BF16),
        [ends], 0, 3 * 2**20, near, even, odd, even_rows, odd_rows, hidden, hidden_ends, target_near,
    )

    mine = total_copies(exchange(sheet, SPREAD), levels, F32)
    mine = total_copies(exchange(mine, ("z",)), spread, F32)
    sheet = exchange(mine, SPREAD)
    groups = spread // 2
    shape = (groups, taps_each * share, channels)
    grad_hidden, keep, send, whitener, offset = call(
        lambda *refs: grad_kernel(voxels, columns, share, *refs),
        [
            flat,
            jax.ShapeDtypeStruct(shape, F32),
            jax.ShapeDtypeStruct(shape, BF16),
            jax.ShapeDtypeStruct((channels, channels), F32),
            jax.ShapeDtypeStruct((8, channels), F32),
        ],
        [
            pltpu.VMEM((2 * G, channels), F32),
            pltpu.VMEM((count, 3 * channels), BF16),
            pltpu.VMEM((9 * channels, 3 * channels), F32),
            pltpu.VMEM((9 * channels, count), BF16),
        ],
        flops, 2**20, sheet, pack,
    )
    received = lax.ppermute(send, ("c",), [(0, 1), (1, 0)])
    parts = call(
        pair_kernel, jax.ShapeDtypeStruct(shape, BF16), [], keep.size, 2**21, keep, received
    )
    block = grad_hidden.reshape(rows, columns, channels)
    whitener, parts = lax.optimization_barrier((whitener, parts))
    whitened = call(white_kernel, flat, [], flops, 2**20, pack, whitener, offset)
    even, odd = plane_swaps(block)
    part = total_copies(exchange(parts, ("y", "x")), levels, BF16)
    part, whitened = lax.optimization_barrier((part, whitened))
    row_ends = row_swaps(block, even, odd)
    part = total_copies(exchange(part, ("z",)), rows_y, BF16, 1.0 / math.sqrt(voxels))
    part, *row_ends = lax.optimization_barrier((part, *row_ends))
    whole = exchange(part, ("y",))
    weight_grad = whole.reshape(rows_y * taps_each, share, channels)[:27].astype(F32)
    weight_grad = weight_grad.reshape(3, 3, 3, share, channels)

    planes = [block, even, odd, *row_ends]
    input_grad = call(
        input_kernel,
        jax.ShapeDtypeStruct((count, channels), BF16),
        [wide, ends, pltpu.VMEM((3 * channels, 9 * channels), BF16)],
        flops, 3 * 2**20, *planes, weight,
    )
    return (whitened.reshape(volume.shape), input_grad.reshape(volume.shape), weight_grad)


def solution(mesh):
    cells = mesh.devices.reshape(4, 8, 4, 2)
    split = Mesh(cells, ("y", "z", "x", "c"))
    in_specs = (P(GZ, GY, None, None), P(), P(GZ, GY, None, None))
    out_specs = (
        P(GZ, GY, None, None),
        P(GZ, GY, None, None),
        P(None, None, None, GY, None),
    )
    return jax.shard_map(local, mesh=split, in_specs=in_specs, out_specs=out_specs, check_vma=False)
```

```python
import math

import jax
import jax.numpy as jnp
from jax import lax
from jax.experimental import pallas as pl
from jax.experimental.pallas import tpu as pltpu
from jax.sharding import Mesh, PartitionSpec as P

G = 64
NEWTON = 5
EPSILON = 1e-05
HIGHEST = lax.Precision.HIGHEST
F32 = jnp.float32
BF16 = jnp.bfloat16
GZ = ("y", "z")
GY = ("x", "c")
SPREAD = ("y", "x", "c")
VMEM_BYTES = 12 * 1024 * 1024


def swapped(block, axes, count, first):
    pairs = []
    for i in range(first, count - 1, 2):
        pairs += [(i, i + 1), (i + 1, i)]
    return lax.ppermute(block, axes, pairs)


def ends_kernel(own, even, odd, first_out, second_out):
    last = own.shape[0] - 1
    odd_row = lax.axis_index("c")
    for place, plane in enumerate((own, even, odd)):
        first_out[place : place + 1] = plane[pl.ds((1 - odd_row) * last, 1)]
        second_out[place : place + 1] = plane[pl.ds(odd_row * last, 1)]


def row_swaps(own, even, odd):
    ny = lax.axis_size(GY)
    ends = jax.ShapeDtypeStruct((3,) + own.shape[1:], BF16)
    first, second = call(ends_kernel, [ends, ends], [], 24 * 2**30, 2**18, own, even, odd)
    return swapped(first, GY, ny, 0), swapped(second, GY, ny, 1)


def plane_swaps(block):
    nz = lax.axis_size(GZ)
    return swapped(block, GZ, nz, 0), swapped(block, GZ, nz, 1)


def call(kernel, out_shape, scratch, flops, moved, *operands, far=()):
    vmem = pl.BlockSpec(memory_space=pltpu.VMEM)
    hbm = pl.BlockSpec(memory_space=pltpu.HBM)
    many = isinstance(out_shape, (list, tuple))
    return pl.pallas_call(
        kernel,
        out_shape=out_shape,
        in_specs=[hbm if i in far else vmem for i in range(len(operands))],
        out_specs=[vmem] * len(out_shape) if many else vmem,
        scratch_shapes=scratch,
        compiler_params=pltpu.CompilerParams(vmem_limit_bytes=VMEM_BYTES),
        cost_estimate=pl.CostEstimate(flops=flops, bytes_accessed=moved, transcendentals=0),
    )(*operands)


def place_rows(wide, slot, plane, edge, tap_y):
    rows, _, channels = plane.shape
    cols = slice(slot * channels, (slot + 1) * channels)
    odd_row = lax.axis_index("c")
    if tap_y == 0:
        wide[0:1, :, cols] = edge[0][pl.ds(1 - odd_row, 1), edge[1]]
        wide[1:rows, :, cols] = plane[0 : rows - 1]
    elif tap_y == 1:
        wide[:, :, cols] = plane[...]
    else:
        wide[0 : rows - 1, :, cols] = plane[1:rows]
        wide[rows - 1 : rows, :, cols] = edge[0][pl.ds(odd_row, 1), edge[1]]


def gather_rows(even_rows, odd_rows, ends):
    ends[0] = even_rows[...]
    ends[1] = odd_rows[...]


def place_all(wide, own, even, odd, flip):
    odd_plane = lax.rem(lax.axis_index("z"), 2)

    order = range(3)
    for tap_z in order:
        for tap_y in order:
            slot = tap_z * 3 + tap_y
            step_z, step_y = (2 - tap_z, 2 - tap_y) if flip else (tap_z, tap_y)
            if step_z == 1:
                place_rows(wide, slot, own[0], own[1], step_y)
    for parity in range(2):

        @pl.when(odd_plane == parity)
        def _():
            below, above = (odd, even) if parity == 0 else (even, odd)
            for tap_z in order:
                for tap_y in order:
                    slot = tap_z * 3 + tap_y
                    step_z, step_y = (2 - tap_z, 2 - tap_y) if flip else (tap_z, tap_y)
                    if step_z != 1:
                        piece = below if step_z == 0 else above
                        place_rows(wide, slot, piece[0], piece[1], step_y)


def moved_columns(flat, step, columns):
    count = flat.shape[0]
    column = lax.broadcasted_iota(jnp.int32, flat.shape, 0) % columns
    if step == 1:
        return jnp.where(column == 0, 0.0, pltpu.roll(flat, 1, 0))
    return jnp.where(column == columns - 1, 0.0, pltpu.roll(flat, count - 1, 0))


def over_rows(left, right):
    return lax.dot_general(left, right, (((0,), (0,)), ((), ())), preferred_element_type=F32)


def ready_kernel(block, weight, target, block_out, wide_out, target_out, sems):
    _, channels, _ = weight.shape
    moves = [
        pltpu.make_async_copy(block, block_out, sems.at[27]),
        pltpu.make_async_copy(target, target_out, sems.at[28]),
    ]
    for tap in range(27):
        slot, tap_x = tap // 3, tap % 3
        place = wide_out.at[
            slot * channels : (slot + 1) * channels, tap_x * channels : (tap_x + 1) * channels
        ]
        moves.append(pltpu.make_async_copy(weight.at[tap], place, sems.at[tap]))
    for move in moves:
        move.start()
    for move in moves:
        move.wait()


def with_shifts(product, columns):
    channels = product.shape[1] // 3
    total = product[:, channels : 2 * channels]
    total = total + moved_columns(product[:, :channels], 1, columns)
    return total + moved_columns(product[:, 2 * channels :], -1, columns)


def moments(hidden, features):
    second = over_rows(hidden, hidden)
    cross = over_rows(features, hidden)
    first = lax.broadcasted_iota(jnp.int32, (G, hidden.shape[1]), 1) < G
    second = jnp.where(first, second[:G], second[G:])
    return second, jnp.where(first, cross[:G], cross[G:])


def conv_kernel(
    own, odd, even, kernel_wide, target,
    hidden_out, ends_out, moments_out, sums_out, wide, none,
):
    rows, columns, channels = own.shape
    none[...] = jnp.zeros(none.shape, BF16)
    place_all(wide, (own, (none, 0)), (even, (none, 0)), (odd, (none, 0)), False)
    flat = wide[...].reshape(rows * columns, 9 * channels)
    product = jnp.dot(flat, kernel_wide[...], preferred_element_type=F32)
    total = with_shifts(product, columns)
    ends_out[:columns] = total[:columns]
    ends_out[columns:] = total[-columns:]
    hidden = total.astype(BF16)
    hidden_out[...] = hidden
    inner = hidden[columns:-columns]
    moments_out[:G], moments_out[G:] = moments(inner, target[columns:-columns])
    sums_out[0:1] = jnp.sum(inner.astype(F32), axis=0, keepdims=True)
    sums_out[1:2] = jnp.sum(target[...].astype(F32), axis=0, keepdims=True)
    sums_out[2:] = jnp.zeros((sums_out.shape[0] - 2, channels), F32)


def finish_kernel(
    totals, odd_rows, even_rows, kernel_wide, target, moments_in, sums,
    hidden_out, sheet_out, ends,
):
    _, columns, channels = even_rows.shape
    gather_rows(even_rows, odd_rows, ends)
    odd_row = lax.axis_index("c")
    odd_plane = lax.rem(lax.axis_index("z"), 2)
    order = (2 - odd_plane, 0, 1 + odd_plane)

    def part(side, tap_y):
        tiles = [ends[side, place] for place in order]
        taps = [(tap_z * 3 + tap_y) * channels for tap_z in range(3)]
        kernel = [kernel_wide[tap : tap + channels, :] for tap in taps]
        product = jnp.dot(
            jnp.concatenate(tiles, axis=1),
            jnp.concatenate(kernel, axis=0),
            preferred_element_type=F32,
        )
        return with_shifts(product, columns)

    total = totals[...] + jnp.concatenate([part(1 - odd_row, 0), part(odd_row, 2)], axis=0)
    hidden = total.astype(BF16)
    hidden_out[...] = hidden
    features = jnp.concatenate([target[:columns], target[target.shape[0] - columns :]], axis=0)
    second, cross = moments(hidden, features)
    second, cross = second + moments_in[:G], cross + moments_in[G:]
    spread, depth, _ = sheet_out.shape
    each = depth - 1
    half = spread // 2
    for j in range(half):
        sheet_out[j, 0:each, :] = second[each * j : each * (j + 1)]
        sheet_out[half + j, 0:each, :] = cross[each * j : each * (j + 1)]
    for j in range(2, spread):
        sheet_out[j, each:depth, :] = jnp.zeros((1, channels), F32)
    hidden_sum = jnp.sum(hidden.astype(F32), axis=0, keepdims=True)
    sheet_out[0, each:depth, :] = sums[0:1] + hidden_sum
    sheet_out[1, each:depth, :] = sums[1:2]


def thirds(value):
    high = value.astype(BF16)
    rest = value - high.astype(F32)
    middle = rest.astype(BF16)
    return high, middle, (rest - middle.astype(F32)).astype(BF16)


def left_terms(value):
    high, middle, low = thirds(value)
    return jnp.concatenate([low, high, middle, middle, high, high], axis=1)


def right_terms(value):
    high, middle, low = thirds(value)
    return jnp.concatenate([high, low, middle, high, middle, high], axis=0)


def exact(left, *rights):
    if len(rights) == 1:
        right = right_terms(rights[0])
    else:
        right = jnp.concatenate([right_terms(value) for value in rights], axis=1)
    return jnp.dot(left_terms(left), right, preferred_element_type=F32)


def through(values, matrix):
    high, middle, low = thirds(matrix)
    total = jnp.dot(values, low, preferred_element_type=F32)
    total = total + jnp.dot(values, middle, preferred_element_type=F32)
    return total + jnp.dot(values, high, preferred_element_type=F32)


def grad_kernel(
    voxels, columns, share, sheet, pack,
    grad_out, keep_out, send_out, whitener_out, offset_out,
    mats, wide, terms, taps,
):
    place_turned(columns, pack, taps)
    count = taps.shape[1]
    base = pack.shape[0] - 2 * count
    spread, depth, channels = sheet.shape
    each = depth - 1
    for j in range(spread):
        mats[each * j : each * (j + 1), :] = sheet[j, 0:each, :]
    row = lax.broadcasted_iota(jnp.int32, (channels, channels), 0)
    col = lax.broadcasted_iota(jnp.int32, (channels, channels), 1)
    same = (row < G) == (col < G)
    diagonal = row == col
    low_lane = lax.broadcasted_iota(jnp.int32, (1, channels), 1) < G

    def group_sums(value):
        line = jnp.sum(value, axis=0, keepdims=True)
        low = jnp.sum(jnp.where(low_lane, line, 0.0), axis=1, keepdims=True)
        high = jnp.sum(jnp.where(low_lane, 0.0, line), axis=1, keepdims=True)
        return jnp.where(low_lane, low, high)

    second = jnp.concatenate([mats[:G], mats[:G]], axis=0)
    cross = jnp.concatenate([mats[G:], mats[G:]], axis=0)
    mean = sheet[0, each:depth, :] / voxels
    target_sum = sheet[1, each:depth, :]
    mean_rows = jnp.broadcast_to(mean, (channels, channels))
    mean_cols = mean_rows.T
    target_cols = jnp.broadcast_to(target_sum, (channels, channels)).T
    second = jnp.where(same, second - voxels * (mean_cols * mean_rows), 0.0)
    cross = jnp.where(same, cross - target_cols * mean_rows, 0.0)
    covariance = second / voxels + jnp.where(diagonal, EPSILON, 0.0)
    trace = group_sums(jnp.where(diagonal, covariance, 0.0))
    scaled = covariance / trace
    root = jnp.sqrt(trace)

    direction = cross / root
    iterate = jnp.where(diagonal, 1.5, 0.0) - 0.5 * scaled
    change = -0.5 * direction
    slope = jnp.where(diagonal, -0.5, 0.0)

    def column(value, i):
        return value[:, i * channels : (i + 1) * channels]

    for sweep in range(1, NEWTON):
        first = exact(iterate, iterate, scaled, change, direction)
        squared, once = column(first, 0), column(first, 1)
        crossed = exact(change, iterate, scaled)
        steep = exact(slope, scaled)
        second_level = exact(squared, once, column(first, 3) + column(crossed, 1), steep, iterate)
        moved = column(second_level, 1) + exact(column(first, 2) + column(crossed, 0), once)
        change = 1.5 * change - 0.5 * moved
        slope = 1.5 * slope - 0.5 * (3.0 * column(second_level, 2) + column(second_level, 3))
        iterate = 1.5 * iterate - 0.5 * column(second_level, 0)
    whitener = iterate / root
    whitener_t = whitener.T
    aligned = exact(whitener, second)
    white_grad = aligned - cross
    change = exact(slope, aligned) / root - change
    trace_grad = -0.5 * group_sums(white_grad * whitener) / trace
    trace_grad = trace_grad - group_sums(change * scaled) / trace
    sigma_grad = change / trace + jnp.where(diagonal, trace_grad, 0.0)
    symmetric = (sigma_grad + sigma_grad.T) / voxels
    backward = (exact(whitener_t, whitener) + symmetric).T

    offset = exact(jnp.broadcast_to(mean, (8, channels)), whitener_t, backward)
    target_offset = exact(jnp.broadcast_to(target_sum / voxels, (8, channels)), whitener)
    whitener_out[...] = whitener_t
    offset_out[...] = offset[:, :channels]
    grad = through(pack[base : base + count], backward)
    grad = grad - through(pack[base + count :], whitener)
    wide_grad = grad - (offset[:1, channels:] - target_offset[:1])
    grad = wide_grad.astype(BF16)
    grad_out[...] = grad
    weight_terms(columns, share, taps, grad, keep_out, send_out, wide, terms)


def white_kernel(pack, whitener, offset, whitened_out):
    count = whitened_out.shape[0]
    hidden = pack[pack.shape[0] - 2 * count : pack.shape[0] - count]
    whitened_out[...] = (through(hidden, whitener[...]) - offset[0:1]).astype(BF16)


def turn_kernel(
    own, even, odd, even_rows, odd_rows, hidden, hidden_ends, target, pack_out, ends
):
    rows, columns, channels = own.shape
    count = rows * columns
    base = 3 * (rows + 2) * channels
    gather_rows(even_rows, odd_rows, ends)
    pack_out[base : base + columns] = hidden_ends[:columns]
    pack_out[base + columns : base + count - columns] = hidden[columns : count - columns]
    pack_out[base + count - columns : base + count] = hidden_ends[columns:]
    pack_out[base + count : base + 2 * count] = target[...]
    odd_row = lax.axis_index("c")
    odd_plane = lax.rem(lax.axis_index("z"), 2)

    def turn(tap_z, plane, edge):
        for source in range(-1, rows + 1):
            if source < 0:
                tile = ends[1 - odd_row, edge]
            elif source == rows:
                tile = ends[odd_row, edge]
            else:
                tile = plane[source]
            first = (tap_z * (rows + 2) + source + 1) * channels
            pack_out[first : first + channels] = tile.T

    turn(1, own, 0)
    for parity in range(2):

        @pl.when(odd_plane == parity)
        def _():
            below, above = ((odd, 2), (even, 1))[:: 1 - 2 * parity]
            turn(0, *below)
            turn(2, *above)


def place_turned(columns, pack, taps):
    rows_all, count = taps.shape
    channels, rows = rows_all // 9, count // columns
    for tap_z in range(3):
        for tap_y in range(3):
            slot = tap_z * 3 + tap_y
            for row in range(rows):
                first = (tap_z * (rows + 2) + row + tap_y) * channels
                taps[
                    slot * channels : (slot + 1) * channels, row * columns : (row + 1) * columns
                ] = pack[first : first + channels]


def weight_terms(columns, share, taps, grad, keep_out, send_out, wide, terms):
    _, channels = grad.shape
    value = grad.astype(F32)
    wide[:, :channels] = moved_columns(value, -1, columns).astype(BF16)
    wide[:, channels : 2 * channels] = grad
    wide[:, 2 * channels :] = moved_columns(value, 1, columns).astype(BF16)
    pairs = channels // share // 2
    taps_each = keep_out.shape[1] // share
    terms[...] = jnp.dot(taps[...], wide[...], preferred_element_type=F32)
    mine = pl.multiple_of(lax.axis_index("c") * share, share)
    others = pl.multiple_of((1 - lax.axis_index("c")) * share, share)
    for tap in range(keep_out.shape[0] // pairs * taps_each):
        slot, tap_x = tap // 3, tap % 3
        cols = slice(tap_x * channels, (tap_x + 1) * channels)
        place = slice(tap % taps_each * share, (tap % taps_each + 1) * share)
        for pair in range(pairs):
            group = tap // taps_each * pairs + pair
            base = slot * channels + pair * 2 * share
            if tap < 27:
                keep_out[group, place, :] = terms[pl.ds(base + mine, share), cols]
                send_out[group, place, :] = terms[pl.ds(base + others, share), cols].astype(BF16)
            else:
                keep_out[group, place, :] = jnp.zeros((share, channels), F32)
                send_out[group, place, :] = jnp.zeros((share, channels), BF16)


def pair_kernel(kept, received, sum_out):
    sum_out[...] = (kept[...] + received[...].astype(F32)).astype(BF16)


def input_kernel(
    own, even, odd, even_rows, odd_rows, weight, grad_out, wide, ends, kernel_wide
):
    rows, columns, channels = own.shape
    gather_rows(even_rows, odd_rows, ends)
    place_all(wide, (own, (ends, 0)), (even, (ends, 1)), (odd, (ends, 2)), True)
    for slot in range(9):
        for tap_x in range(3):
            kernel_wide[
                tap_x * channels : (tap_x + 1) * channels,
                slot * channels : (slot + 1) * channels,
            ] = weight[slot * 3 + tap_x]
    flat = wide[...].reshape(rows * columns, 9 * channels)
    product = lax.dot_general(
        flat, kernel_wide[...], (((1,), (1,)), ((), ())), preferred_element_type=F32
    )
    total = product[:, channels : 2 * channels]
    total = total + moved_columns(product[:, :channels], -1, columns)
    total = total + moved_columns(product[:, 2 * channels :], 1, columns)
    grad_out[...] = total.astype(BF16)


def total_kernel(scale, parts, copies_out):
    total = parts[0].astype(F32)
    for i in range(1, parts.shape[0]):
        total = total + parts[i].astype(F32)
    total = (total * scale if scale != 1.0 else total).astype(copies_out.dtype)
    for i in range(copies_out.shape[0]):
        copies_out[i] = total


def exchange(parts, axes):
    return lax.all_to_all(parts, axes, 0, 0, tiled=True)


def total_copies(parts, count, dtype, scale=1.0):
    shape = jax.ShapeDtypeStruct((count,) + parts.shape[1:], dtype)
    return call(
        lambda *refs: total_kernel(scale, *refs), shape, [], parts.size, 2 * parts.size, parts
    )


def local(volume, conv_weight, target):
    _, rows, columns, channels = volume.shape
    count = rows * columns
    voxels = count * lax.axis_size(GZ) * lax.axis_size(GY)
    spread = lax.axis_size(SPREAD)
    levels = lax.axis_size("z")
    rows_y = lax.axis_size("y")
    share = channels // lax.axis_size(GY)
    taps_each = -(-27 // rows_y)
    flops = 2 * count * 27 * channels * channels
    weight = conv_weight.reshape(27, channels, channels)
    target_flat = target.reshape(count, channels)

    block = volume.reshape(rows, columns, channels)
    even, odd = plane_swaps(block)
    near, kernel_wide, target_near = call(
        ready_kernel,
        [
            jax.ShapeDtypeStruct(block.shape, BF16),
            jax.ShapeDtypeStruct((9 * channels, 3 * channels), BF16),
            jax.ShapeDtypeStruct((count, channels), BF16),
        ],
        [pltpu.SemaphoreType.DMA((29,))],
        0, 2**20, block, weight, target_flat, far=(0, 1, 2),
    )
    even_rows, odd_rows = row_swaps(near, even, odd)
    ends = pltpu.VMEM((2, 3, columns, channels), BF16)
    wide = pltpu.VMEM((rows, columns, 9 * channels), BF16)
    hidden, totals, moments_here, sums_here = call(
        conv_kernel,
        [
            jax.ShapeDtypeStruct((count, channels), BF16),
            jax.ShapeDtypeStruct((2 * columns, channels), F32),
            jax.ShapeDtypeStruct((2 * G, channels), F32),
            jax.ShapeDtypeStruct((8, channels), F32),
        ],
        [wide, pltpu.VMEM((2, 1, columns, channels), BF16)],
        flops, 3 * 2**20, near, odd, even, kernel_wide, target_near,
    )
    hidden_ends, sheet = call(
        finish_kernel,
        [
            jax.ShapeDtypeStruct((2 * columns, channels), BF16),
            jax.ShapeDtypeStruct((spread, 2 * G // spread + 1, channels), F32),
        ],
        [ends],
        flops // 12, 2**20,
        totals, odd_rows, even_rows, kernel_wide, target_near, moments_here, sums_here,
    )
    flat = jax.ShapeDtypeStruct((count, channels), BF16)
    pack = call(
        turn_kernel,
        jax.ShapeDtypeStruct((3 * (rows + 2) * channels + 2 * count, channels), BF16),
        [ends], 0, 3 * 2**20, near, even, odd, even_rows, odd_rows, hidden, hidden_ends, target_near,
    )

    mine = total_copies(exchange(sheet, SPREAD), levels, F32)
    mine = total_copies(exchange(mine, ("z",)), spread, F32)
    sheet = exchange(mine, SPREAD)
    groups = spread // 2
    shape = (groups, taps_each * share, channels)
    grad_hidden, keep, send, whitener, offset = call(
        lambda *refs: grad_kernel(voxels, columns, share, *refs),
        [
            flat,
            jax.ShapeDtypeStruct(shape, F32),
            jax.ShapeDtypeStruct(shape, BF16),
            jax.ShapeDtypeStruct((channels, channels), F32),
            jax.ShapeDtypeStruct((8, channels), F32),
        ],
        [
            pltpu.VMEM((2 * G, channels), F32),
            pltpu.VMEM((count, 3 * channels), BF16),
            pltpu.VMEM((9 * channels, 3 * channels), F32),
            pltpu.VMEM((9 * channels, count), BF16),
        ],
        flops, 2**20, sheet, pack,
    )
    received = lax.ppermute(send, ("c",), [(0, 1), (1, 0)])
    parts = call(
        pair_kernel, jax.ShapeDtypeStruct(shape, BF16), [], keep.size, 2**21, keep, received
    )
    block = grad_hidden.reshape(rows, columns, channels)
    whitener, parts = lax.optimization_barrier((whitener, parts))
    whitened = call(white_kernel, flat, [], flops, 2**20, pack, whitener, offset)
    even, odd = plane_swaps(block)
    part = total_copies(exchange(parts, ("y", "x")), levels, BF16)
    part, whitened = lax.optimization_barrier((part, whitened))
    row_ends = row_swaps(block, even, odd)
    part = total_copies(exchange(part, ("z",)), rows_y, BF16, 1.0 / math.sqrt(voxels))
    part, *row_ends = lax.optimization_barrier((part, *row_ends))
    whole = exchange(part, ("y",))
    weight_grad = whole.reshape(rows_y * taps_each, share, channels)[:27].astype(F32)
    weight_grad = weight_grad.reshape(3, 3, 3, share, channels)

    planes = [block, even, odd, *row_ends]
    input_grad = call(
        input_kernel,
        jax.ShapeDtypeStruct((count, channels), BF16),
        [wide, ends, pltpu.VMEM((3 * channels, 9 * channels), BF16)],
        flops, 3 * 2**20, *planes, weight,
    )
    return (whitened.reshape(volume.shape), input_grad.reshape(volume.shape), weight_grad)


def solution(mesh):
    cells = mesh.devices.reshape(4, 8, 4, 2)
    split = Mesh(cells, ("y", "z", "x", "c"))
    in_specs = (P(GZ, GY, None, None), P(), P(GZ, GY, None, None))
    out_specs = (
        P(GZ, GY, None, None),
        P(GZ, GY, None, None),
        P(None, None, None, GY, None),
    )
    return jax.shard_map(local, mesh=split, in_specs=in_specs, out_specs=out_specs, check_vma=False)
```

```python
import math

import jax
import jax.numpy as jnp
from jax import lax
from jax.experimental import pallas as pl
from jax.experimental.pallas import tpu as pltpu
from jax.sharding import Mesh, PartitionSpec as P

G = 64
NEWTON = 5
EPSILON = 1e-05
HIGHEST = lax.Precision.HIGHEST
F32 = jnp.float32
BF16 = jnp.bfloat16
GZ = ("y", "z")
GY = ("x", "c")
SPREAD = ("y", "x", "c")
VMEM_BYTES = 12 * 1024 * 1024


def swapped(block, axes, count, first):
    pairs = []
    for i in range(first, count - 1, 2):
        pairs += [(i, i + 1), (i + 1, i)]
    return lax.ppermute(block, axes, pairs)


def ends_kernel(own, even, odd, first_out, second_out):
    last = own.shape[0] - 1
    odd_row = lax.axis_index("c")
    for place, plane in enumerate((own, even, odd)):
        first_out[place : place + 1] = plane[pl.ds((1 - odd_row) * last, 1)]
        second_out[place : place + 1] = plane[pl.ds(odd_row * last, 1)]


def row_swaps(own, even, odd):
    ny = lax.axis_size(GY)
    ends = jax.ShapeDtypeStruct((3,) + own.shape[1:], BF16)
    first, second = call(ends_kernel, [ends, ends], [], 24 * 2**30, 2**18, own, even, odd)
    return swapped(first, GY, ny, 0), swapped(second, GY, ny, 1)


def plane_swaps(block):
    nz = lax.axis_size(GZ)
    return swapped(block, GZ, nz, 0), swapped(block, GZ, nz, 1)


def call(kernel, out_shape, scratch, flops, moved, *operands, far=()):
    vmem = pl.BlockSpec(memory_space=pltpu.VMEM)
    hbm = pl.BlockSpec(memory_space=pltpu.HBM)
    many = isinstance(out_shape, (list, tuple))
    return pl.pallas_call(
        kernel,
        out_shape=out_shape,
        in_specs=[hbm if i in far else vmem for i in range(len(operands))],
        out_specs=[vmem] * len(out_shape) if many else vmem,
        scratch_shapes=scratch,
        compiler_params=pltpu.CompilerParams(vmem_limit_bytes=VMEM_BYTES),
        cost_estimate=pl.CostEstimate(flops=flops, bytes_accessed=moved, transcendentals=0),
    )(*operands)


def place_rows(wide, slot, plane, edge, tap_y):
    rows, _, channels = plane.shape
    cols = slice(slot * channels, (slot + 1) * channels)
    odd_row = lax.axis_index("c")
    if tap_y == 0:
        wide[0:1, :, cols] = edge[0][pl.ds(1 - odd_row, 1), edge[1]]
        wide[1:rows, :, cols] = plane[0 : rows - 1]
    elif tap_y == 1:
        wide[:, :, cols] = plane[...]
    else:
        wide[0 : rows - 1, :, cols] = plane[1:rows]
        wide[rows - 1 : rows, :, cols] = edge[0][pl.ds(odd_row, 1), edge[1]]


def gather_rows(even_rows, odd_rows, ends):
    ends[0] = even_rows[...]
    ends[1] = odd_rows[...]


def place_all(wide, own, even, odd, flip):
    odd_plane = lax.rem(lax.axis_index("z"), 2)

    order = range(3)
    for tap_z in order:
        for tap_y in order:
            slot = tap_z * 3 + tap_y
            step_z, step_y = (2 - tap_z, 2 - tap_y) if flip else (tap_z, tap_y)
            if step_z == 1:
                place_rows(wide, slot, own[0], own[1], step_y)
    for parity in range(2):

        @pl.when(odd_plane == parity)
        def _():
            below, above = (odd, even) if parity == 0 else (even, odd)
            for tap_z in order:
                for tap_y in order:
                    slot = tap_z * 3 + tap_y
                    step_z, step_y = (2 - tap_z, 2 - tap_y) if flip else (tap_z, tap_y)
                    if step_z != 1:
                        piece = below if step_z == 0 else above
                        place_rows(wide, slot, piece[0], piece[1], step_y)


def moved_columns(flat, step, columns):
    count = flat.shape[0]
    column = lax.broadcasted_iota(jnp.int32, flat.shape, 0) % columns
    if step == 1:
        return jnp.where(column == 0, 0.0, pltpu.roll(flat, 1, 0))
    return jnp.where(column == columns - 1, 0.0, pltpu.roll(flat, count - 1, 0))


def over_rows(left, right):
    return lax.dot_general(left, right, (((0,), (0,)), ((), ())), preferred_element_type=F32)


def ready_kernel(block, weight, target, block_out, wide_out, target_out, sems):
    _, channels, _ = weight.shape
    moves = [
        pltpu.make_async_copy(block, block_out, sems.at[27]),
        pltpu.make_async_copy(target, target_out, sems.at[28]),
    ]
    for tap in range(27):
        slot, tap_x = tap // 3, tap % 3
        place = wide_out.at[
            slot * channels : (slot + 1) * channels, tap_x * channels : (tap_x + 1) * channels
        ]
        moves.append(pltpu.make_async_copy(weight.at[tap], place, sems.at[tap]))
    for move in moves:
        move.start()
    for move in moves:
        move.wait()


def with_shifts(product, columns):
    channels = product.shape[1] // 3
    total = product[:, channels : 2 * channels]
    total = total + moved_columns(product[:, :channels], 1, columns)
    return total + moved_columns(product[:, 2 * channels :], -1, columns)


def moments(hidden, features):
    second = over_rows(hidden, hidden)
    cross = over_rows(features, hidden)
    first = lax.broadcasted_iota(jnp.int32, (G, hidden.shape[1]), 1) < G
    second = jnp.where(first, second[:G], second[G:])
    return second, jnp.where(first, cross[:G], cross[G:])


def conv_kernel(
    own, odd, even, kernel_wide, target,
    hidden_out, ends_out, moments_out, sums_out, wide, none,
):
    rows, columns, channels = own.shape
    none[...] = jnp.zeros(none.shape, BF16)
    place_all(wide, (own, (none, 0)), (even, (none, 0)), (odd, (none, 0)), False)
    flat = wide[...].reshape(rows * columns, 9 * channels)
    product = jnp.dot(flat, kernel_wide[...], preferred_element_type=F32)
    total = with_shifts(product, columns)
    ends_out[:columns] = total[:columns]
    ends_out[columns:] = total[-columns:]
    hidden = total.astype(BF16)
    hidden_out[...] = hidden
    inner = hidden[columns:-columns]
    moments_out[:G], moments_out[G:] = moments(inner, target[columns:-columns])
    sums_out[0:1] = jnp.sum(inner.astype(F32), axis=0, keepdims=True)
    sums_out[1:2] = jnp.sum(target[...].astype(F32), axis=0, keepdims=True)
    sums_out[2:] = jnp.zeros((sums_out.shape[0] - 2, channels), F32)


def finish_kernel(
    totals, odd_rows, even_rows, kernel_wide, target, moments_in, sums,
    hidden_out, sheet_out, ends,
):
    _, columns, channels = even_rows.shape
    gather_rows(even_rows, odd_rows, ends)
    odd_row = lax.axis_index("c")
    odd_plane = lax.rem(lax.axis_index("z"), 2)
    order = (2 - odd_plane, 0, 1 + odd_plane)

    def part(side, tap_y):
        tiles = [ends[side, place] for place in order]
        taps = [(tap_z * 3 + tap_y) * channels for tap_z in range(3)]
        kernel = [kernel_wide[tap : tap + channels, :] for tap in taps]
        product = jnp.dot(
            jnp.concatenate(tiles, axis=1),
            jnp.concatenate(kernel, axis=0),
            preferred_element_type=F32,
        )
        return with_shifts(product, columns)

    total = totals[...] + jnp.concatenate([part(1 - odd_row, 0), part(odd_row, 2)], axis=0)
    hidden = total.astype(BF16)
    hidden_out[...] = hidden
    features = jnp.concatenate([target[:columns], target[target.shape[0] - columns :]], axis=0)
    second, cross = moments(hidden, features)
    second, cross = second + moments_in[:G], cross + moments_in[G:]
    spread, depth, _ = sheet_out.shape
    each = depth - 1
    half = spread // 2
    for j in range(half):
        sheet_out[j, 0:each, :] = second[each * j : each * (j + 1)]
        sheet_out[half + j, 0:each, :] = cross[each * j : each * (j + 1)]
    for j in range(2, spread):
        sheet_out[j, each:depth, :] = jnp.zeros((1, channels), F32)
    hidden_sum = jnp.sum(hidden.astype(F32), axis=0, keepdims=True)
    sheet_out[0, each:depth, :] = sums[0:1] + hidden_sum
    sheet_out[1, each:depth, :] = sums[1:2]


def thirds(value):
    high = value.astype(BF16)
    rest = value - high.astype(F32)
    middle = rest.astype(BF16)
    return high, middle, (rest - middle.astype(F32)).astype(BF16)


def left_terms(value):
    high, middle, low = thirds(value)
    return jnp.concatenate([low, high, middle, middle, high, high], axis=1)


def right_terms(value):
    high, middle, low = thirds(value)
    return jnp.concatenate([high, low, middle, high, middle, high], axis=0)


def exact(left, *rights):
    if len(rights) == 1:
        right = right_terms(rights[0])
    else:
        right = jnp.concatenate([right_terms(value) for value in rights], axis=1)
    return jnp.dot(left_terms(left), right, preferred_element_type=F32)


def through(values, matrix):
    high, middle, low = thirds(matrix)
    total = jnp.dot(values, low, preferred_element_type=F32)
    total = total + jnp.dot(values, middle, preferred_element_type=F32)
    return total + jnp.dot(values, high, preferred_element_type=F32)


def grad_kernel(
    voxels, columns, share, sheet, pack,
    grad_out, keep_out, send_out, whitener_out, offset_out,
    mats, wide, terms, taps,
):
    place_turned(columns, pack, taps)
    count = taps.shape[1]
    base = pack.shape[0] - 2 * count
    spread, depth, channels = sheet.shape
    each = depth - 1
    for j in range(spread):
        mats[each * j : each * (j + 1), :] = sheet[j, 0:each, :]
    row = lax.broadcasted_iota(jnp.int32, (channels, channels), 0)
    col = lax.broadcasted_iota(jnp.int32, (channels, channels), 1)
    same = (row < G) == (col < G)
    diagonal = row == col
    low_lane = lax.broadcasted_iota(jnp.int32, (1, channels), 1) < G

    def group_sums(value):
        line = jnp.sum(value, axis=0, keepdims=True)
        low = jnp.sum(jnp.where(low_lane, line, 0.0), axis=1, keepdims=True)
        high = jnp.sum(jnp.where(low_lane, 0.0, line), axis=1, keepdims=True)
        return jnp.where(low_lane, low, high)

    second = jnp.concatenate([mats[:G], mats[:G]], axis=0)
    cross = jnp.concatenate([mats[G:], mats[G:]], axis=0)
    mean = sheet[0, each:depth, :] / voxels
    target_sum = sheet[1, each:depth, :]
    mean_rows = jnp.broadcast_to(mean, (channels, channels))
    mean_cols = mean_rows.T
    target_cols = jnp.broadcast_to(target_sum, (channels, channels)).T
    second = jnp.where(same, second - voxels * (mean_cols * mean_rows), 0.0)
    cross = jnp.where(same, cross - target_cols * mean_rows, 0.0)
    covariance = second / voxels + jnp.where(diagonal, EPSILON, 0.0)
    trace = group_sums(jnp.where(diagonal, covariance, 0.0))
    scaled = covariance / trace
    root = jnp.sqrt(trace)

    direction = cross / root
    iterate = jnp.where(diagonal, 1.5, 0.0) - 0.5 * scaled
    change = -0.5 * direction
    slope = jnp.where(diagonal, -0.5, 0.0)

    def column(value, i):
        return value[:, i * channels : (i + 1) * channels]

    for sweep in range(1, NEWTON):
        first = exact(iterate, iterate, scaled, change, direction)
        squared, once = column(first, 0), column(first, 1)
        crossed = exact(change, iterate, scaled)
        steep = exact(slope, scaled)
        second_level = exact(squared, once, column(first, 3) + column(crossed, 1), steep, iterate)
        moved = column(second_level, 1) + exact(column(first, 2) + column(crossed, 0), once)
        change = 1.5 * change - 0.5 * moved
        slope = 1.5 * slope - 0.5 * (3.0 * column(second_level, 2) + column(second_level, 3))
        iterate = 1.5 * iterate - 0.5 * column(second_level, 0)
    whitener = iterate / root
    whitener_t = whitener.T
    aligned = exact(whitener, second)
    white_grad = aligned - cross
    change = exact(slope, aligned) / root - change
    trace_grad = -0.5 * group_sums(white_grad * whitener) / trace
    trace_grad = trace_grad - group_sums(change * scaled) / trace
    sigma_grad = change / trace + jnp.where(diagonal, trace_grad, 0.0)
    symmetric = (sigma_grad + sigma_grad.T) / voxels
    backward = (exact(whitener_t, whitener) + symmetric).T

    offset = exact(jnp.broadcast_to(mean, (8, channels)), whitener_t, backward)
    target_offset = exact(jnp.broadcast_to(target_sum / voxels, (8, channels)), whitener)
    whitener_out[...] = whitener_t
    offset_out[...] = offset[:, :channels]
    grad = through(pack[base : base + count], backward)
    grad = grad - through(pack[base + count :], whitener)
    wide_grad = grad - (offset[:1, channels:] - target_offset[:1])
    grad = wide_grad.astype(BF16)
    grad_out[...] = grad
    weight_terms(columns, share, taps, grad, keep_out, send_out, wide, terms)


def white_kernel(pack, whitener, offset, whitened_out):
    count = whitened_out.shape[0]
    hidden = pack[pack.shape[0] - 2 * count : pack.shape[0] - count]
    whitened_out[...] = (through(hidden, whitener[...]) - offset[0:1]).astype(BF16)


def turn_kernel(
    own, even, odd, even_rows, odd_rows, hidden, hidden_ends, target, pack_out, ends
):
    rows, columns, channels = own.shape
    count = rows * columns
    base = 3 * (rows + 2) * channels
    gather_rows(even_rows, odd_rows, ends)
    pack_out[base : base + columns] = hidden_ends[:columns]
    pack_out[base + columns : base + count - columns] = hidden[columns : count - columns]
    pack_out[base + count - columns : base + count] = hidden_ends[columns:]
    pack_out[base + count : base + 2 * count] = target[...]
    odd_row = lax.axis_index("c")
    odd_plane = lax.rem(lax.axis_index("z"), 2)

    def turn(tap_z, plane, edge):
        for source in range(-1, rows + 1):
            if source < 0:
                tile = ends[1 - odd_row, edge]
            elif source == rows:
                tile = ends[odd_row, edge]
            else:
                tile = plane[source]
            first = (tap_z * (rows + 2) + source + 1) * channels
            pack_out[first : first + channels] = tile.T

    turn(1, own, 0)
    for parity in range(2):

        @pl.when(odd_plane == parity)
        def _():
            below, above = ((odd, 2), (even, 1))[:: 1 - 2 * parity]
            turn(0, *below)
            turn(2, *above)


def place_turned(columns, pack, taps):
    rows_all, count = taps.shape
    channels, rows = rows_all // 9, count // columns
    for tap_z in range(3):
        for tap_y in range(3):
            slot = tap_z * 3 + tap_y
            for row in range(rows):
                first = (tap_z * (rows + 2) + row + tap_y) * channels
                taps[
                    slot * channels : (slot + 1) * channels, row * columns : (row + 1) * columns
                ] = pack[first : first + channels]


def weight_terms(columns, share, taps, grad, keep_out, send_out, wide, terms):
    _, channels = grad.shape
    value = grad.astype(F32)
    wide[:, :channels] = moved_columns(value, -1, columns).astype(BF16)
    wide[:, channels : 2 * channels] = grad
    wide[:, 2 * channels :] = moved_columns(value, 1, columns).astype(BF16)
    pairs = channels // share // 2
    taps_each = keep_out.shape[1] // share
    terms[...] = jnp.dot(taps[...], wide[...], preferred_element_type=F32)
    mine = pl.multiple_of(lax.axis_index("c") * share, share)
    others = pl.multiple_of((1 - lax.axis_index("c")) * share, share)
    for tap in range(keep_out.shape[0] // pairs * taps_each):
        slot, tap_x = tap // 3, tap % 3
        cols = slice(tap_x * channels, (tap_x + 1) * channels)
        place = slice(tap % taps_each * share, (tap % taps_each + 1) * share)
        for pair in range(pairs):
            group = tap // taps_each * pairs + pair
            base = slot * channels + pair * 2 * share
            if tap < 27:
                keep_out[group, place, :] = terms[pl.ds(base + mine, share), cols]
                send_out[group, place, :] = terms[pl.ds(base + others, share), cols].astype(BF16)
            else:
                keep_out[group, place, :] = jnp.zeros((share, channels), F32)
                send_out[group, place, :] = jnp.zeros((share, channels), BF16)


def pair_kernel(kept, received, sum_out):
    sum_out[...] = (kept[...] + received[...].astype(F32)).astype(BF16)


def input_kernel(
    own, even, odd, odd_rows, even_rows, weight, grad_out, wide, ends, kernel_wide
):
    rows, columns, channels = own.shape
    gather_rows(even_rows, odd_rows, ends)
    place_all(wide, (own, (ends, 0)), (even, (ends, 1)), (odd, (ends, 2)), True)
    for slot in range(9):
        for tap_x in range(3):
            kernel_wide[
                tap_x * channels : (tap_x + 1) * channels,
                slot * channels : (slot + 1) * channels,
            ] = weight[slot * 3 + tap_x]
    flat = wide[...].reshape(rows * columns, 9 * channels)
    product = lax.dot_general(
        flat, kernel_wide[...], (((1,), (1,)), ((), ())), preferred_element_type=F32
    )
    total = product[:, channels : 2 * channels]
    total = total + moved_columns(product[:, :channels], -1, columns)
    total = total + moved_columns(product[:, 2 * channels :], 1, columns)
    grad_out[...] = total.astype(BF16)


def total_kernel(scale, parts, copies_out):
    total = parts[0].astype(F32)
    for i in range(1, parts.shape[0]):
        total = total + parts[i].astype(F32)
    total = (total * scale if scale != 1.0 else total).astype(copies_out.dtype)
    for i in range(copies_out.shape[0]):
        copies_out[i] = total


def exchange(parts, axes):
    return lax.all_to_all(parts, axes, 0, 0, tiled=True)


def total_copies(parts, count, dtype, scale=1.0):
    shape = jax.ShapeDtypeStruct((count,) + parts.shape[1:], dtype)
    return call(
        lambda *refs: total_kernel(scale, *refs), shape, [], parts.size, 2 * parts.size, parts
    )


def local(volume, conv_weight, target):
    _, rows, columns, channels = volume.shape
    count = rows * columns
    voxels = count * lax.axis_size(GZ) * lax.axis_size(GY)
    spread = lax.axis_size(SPREAD)
    levels = lax.axis_size("z")
    rows_y = lax.axis_size("y")
    share = channels // lax.axis_size(GY)
    taps_each = -(-27 // rows_y)
    flops = 2 * count * 27 * channels * channels
    weight = conv_weight.reshape(27, channels, channels)
    target_flat = target.reshape(count, channels)

    block = volume.reshape(rows, columns, channels)
    even, odd = plane_swaps(block)
    near, kernel_wide, target_near = call(
        ready_kernel,
        [
            jax.ShapeDtypeStruct(block.shape, BF16),
            jax.ShapeDtypeStruct((9 * channels, 3 * channels), BF16),
            jax.ShapeDtypeStruct((count, channels), BF16),
        ],
        [pltpu.SemaphoreType.DMA((29,))],
        0, 2**20, block, weight, target_flat, far=(0, 1, 2),
    )
    even_rows, odd_rows = row_swaps(near, even, odd)
    ends = pltpu.VMEM((2, 3, columns, channels), BF16)
    wide = pltpu.VMEM((rows, columns, 9 * channels), BF16)
    hidden, totals, moments_here, sums_here = call(
        conv_kernel,
        [
            jax.ShapeDtypeStruct((count, channels), BF16),
            jax.ShapeDtypeStruct((2 * columns, channels), F32),
            jax.ShapeDtypeStruct((2 * G, channels), F32),
            jax.ShapeDtypeStruct((8, channels), F32),
        ],
        [wide, pltpu.VMEM((2, 1, columns, channels), BF16)],
        flops, 3 * 2**20, near, odd, even, kernel_wide, target_near,
    )
    hidden_ends, sheet = call(
        finish_kernel,
        [
            jax.ShapeDtypeStruct((2 * columns, channels), BF16),
            jax.ShapeDtypeStruct((spread, 2 * G // spread + 1, channels), F32),
        ],
        [ends],
        flops // 12, 2**20,
        totals, odd_rows, even_rows, kernel_wide, target_near, moments_here, sums_here,
    )
    flat = jax.ShapeDtypeStruct((count, channels), BF16)
    pack = call(
        turn_kernel,
        jax.ShapeDtypeStruct((3 * (rows + 2) * channels + 2 * count, channels), BF16),
        [ends], 0, 3 * 2**20, near, even, odd, even_rows, odd_rows, hidden, hidden_ends, target_near,
    )

    mine = total_copies(exchange(sheet, SPREAD), levels, F32)
    mine = total_copies(exchange(mine, ("z",)), spread, F32)
    sheet = exchange(mine, SPREAD)
    groups = spread // 2
    shape = (groups, taps_each * share, channels)
    grad_hidden, keep, send, whitener, offset = call(
        lambda *refs: grad_kernel(voxels, columns, share, *refs),
        [
            flat,
            jax.ShapeDtypeStruct(shape, F32),
            jax.ShapeDtypeStruct(shape, BF16),
            jax.ShapeDtypeStruct((channels, channels), F32),
            jax.ShapeDtypeStruct((8, channels), F32),
        ],
        [
            pltpu.VMEM((2 * G, channels), F32),
            pltpu.VMEM((count, 3 * channels), BF16),
            pltpu.VMEM((9 * channels, 3 * channels), F32),
            pltpu.VMEM((9 * channels, count), BF16),
        ],
        flops, 2**20, sheet, pack,
    )
    received = lax.ppermute(send, ("c",), [(0, 1), (1, 0)])
    parts = call(
        pair_kernel, jax.ShapeDtypeStruct(shape, BF16), [], keep.size, 2**21, keep, received
    )
    block = grad_hidden.reshape(rows, columns, channels)
    whitener, parts = lax.optimization_barrier((whitener, parts))
    whitened = call(white_kernel, flat, [], flops, 2**20, pack, whitener, offset)
    even, odd = plane_swaps(block)
    part = total_copies(exchange(parts, ("y", "x")), levels, BF16)
    part, whitened = lax.optimization_barrier((part, whitened))
    row_ends = row_swaps(block, even, odd)
    part = total_copies(exchange(part, ("z",)), rows_y, BF16, 1.0 / math.sqrt(voxels))
    odd_rows, even_rows, part = lax.optimization_barrier((row_ends[1], row_ends[0], part))
    row_ends = (even_rows, odd_rows)
    whole = exchange(part, ("y",))
    weight_grad = whole.reshape(rows_y * taps_each, share, channels)[:27].astype(F32)
    weight_grad = weight_grad.reshape(3, 3, 3, share, channels)

    planes = [block, even, odd, *row_ends[::-1]]
    input_grad = call(
        input_kernel,
        jax.ShapeDtypeStruct((count, channels), BF16),
        [wide, ends, pltpu.VMEM((3 * channels, 9 * channels), BF16)],
        flops, 3 * 2**20, *planes, weight,
    )
    return (whitened.reshape(volume.shape), input_grad.reshape(volume.shape), weight_grad)


def solution(mesh):
    cells = mesh.devices.reshape(4, 8, 4, 2)
    split = Mesh(cells, ("y", "z", "x", "c"))
    in_specs = (P(GZ, GY, None, None), P(), P(GZ, GY, None, None))
    out_specs = (
        P(GZ, GY, None, None),
        P(GZ, GY, None, None),
        P(None, None, None, GY, None),
    )
    return jax.shard_map(local, mesh=split, in_specs=in_specs, out_specs=out_specs, check_vma=False)
```
